32 devices in a mesh: parts: 1, grid: 32 (over z, y, x, core).
Axes of the slice: x: 2, y: 2, z: 4, core: 2. Of those that a mesh axis runs over, the one named last changes fastest.
Arguments:
- tokens: bfloat16 [128, 32, 1024], P(('parts', 'grid')), may hold values from -6 to 6
- cotangent: bfloat16 [128, 32, 1024], P(('parts', 'grid')), may hold values from -6 to 6
- w_sqkv: bfloat16 [1024, 3072], P('grid'), may hold values from -0.1875 to 0.1875
- w_so: bfloat16 [1024, 1024], P('grid'), may hold values from -0.1875 to 0.1875
- w_gqkv: bfloat16 [1024, 3072], P('grid'), may hold values from -0.1875 to 0.1875
- w_go: bfloat16 [1024, 1024], P('grid'), may hold values from -0.1875 to 0.1875
- keep: int32 [32, 128], P(None, 'parts'), may hold values from 0 to 1, as said below
Outputs:
- mixed: bfloat16 [128, 32, 1024], P(('parts', 'grid'))
- token_grad: bfloat16 [128, 32, 1024], P(('parts', 'grid'))
The draws below stay inside these ranges and needn't reach their ends.
Inputs may be any that keep to these rules, and one draw needn't show every extreme that they name: `keep`: every band group keeps at least one patch; the kept share differs from group to group.
All inputs are finite; a program needn't handle non-finite values.
Results may differ from the reference program's by a relative error of at most 0.017.
Values may be sent and summed in bfloat16 or wider, within the bound.
No kernel may reach another device: no remote copies, remote signals or barrier semaphores. Data moves between devices by JAX's collectives and lax.ppermute only.
A program may use at most 192 MiB of HBM per device.

```python
from functools import partial
import jax
import jax.numpy as jnp
from jax import lax

D = 1024
H = 16
G = 32
P_SIZE = 128


def draw_keep(key, part):
    first = jax.random.fold_in(key, 11)
    second = jax.random.fold_in(key, 12)
    cutoff = jax.random.randint(first, (G, 1), 5, 85)
    noise = jax.random.randint(second, (G, P_SIZE), 0, 100)
    kept = (noise >= cutoff).astype(jnp.int32)
    forced = (jnp.arange(P_SIZE, dtype=jnp.int32)[None, :] % G == jnp.arange(G, dtype=jnp.int32)[:, None]).astype(jnp.int32)
    return jnp.maximum(kept, forced)


def levels(key, shape, shards, smallest, largest):
    factor_of, own = 1.0, jax.random.fold_in(key, 6)
    for axis_at, blocks in shards:
        draws = jnp.exp(jax.random.uniform(jax.random.fold_in(own, axis_at), (blocks,), jnp.float32, smallest / len(shards), largest / len(shards)))
        factor_of = factor_of * jnp.repeat(draws, shape[axis_at] // blocks).reshape([-1 if axis == axis_at else 1 for axis in range(len(shape))])
    return factor_of


def scatter_about(key, extent, deviation, bound, shards=(), held_as=jnp.bfloat16):
    drawn = deviation * jax.random.normal(key, extent, jnp.float32)
    if shards:
        drawn = drawn * levels(key, extent, shards, -0.22, 0.18)
    return jnp.clip(drawn, -bound, bound).astype(held_as)


def setup_inputs(seed: int = 0, part: int = 0) -> dict:
    seeds = jax.random.split(jax.random.key(seed), 8)
    part_splits = jax.random.split(jax.random.fold_in(seeds[7], part), 8)
    tokens = scatter_about(part_splits[0], (P_SIZE, G, D), 1.0, 6.0, ((0, 32),))
    cotangent = scatter_about(part_splits[1], (P_SIZE, G, D), 1.0, 6.0, ((0, 32),))
    w_sqkv = scatter_about(seeds[2], (D, 3 * D), D ** -0.5, 0.1875, ((0, 32),))
    w_so = scatter_about(seeds[3], (D, D), D ** -0.5, 0.1875, ((0, 32),))
    w_gqkv = scatter_about(seeds[4], (D, 3 * D), D ** -0.5, 0.1875, ((0, 32),))
    w_go = scatter_about(seeds[5], (D, D), D ** -0.5, 0.1875, ((0, 32),))
    keep = draw_keep(jax.random.fold_in(jax.random.fold_in(seeds[7], part), 71), part)
    return {"tokens": tokens, "cotangent": cotangent, "w_sqkv": w_sqkv, "w_so": w_so, "w_gqkv": w_gqkv, "w_go": w_go, "keep": keep}


def rms_normalize(values):
    wide = values.astype(jnp.float32)
    meansq = lax.optimization_barrier(jnp.mean(wide * wide, axis=-1, keepdims=True))
    return (wide * lax.rsqrt(meansq + 1e-06)).astype(jnp.bfloat16)

def project_spatial(tokens, weight):
    patches, groups, width = tokens.shape
    normed = rms_normalize(tokens).reshape(patches * groups, width)
    stacked = jnp.dot(normed, weight, preferred_element_type=jnp.float32).astype(jnp.bfloat16)
    stacked = stacked.reshape(patches, groups, 3, width).transpose(2, 0, 1, 3)
    return stacked.reshape(3, patches, groups * width)

def pair_attention(operands):
    stacked, keep_row = operands
    query, keyed, valued = (stacked[0], stacked[1], stacked[2])
    scale = query.shape[-1] ** (-0.5)
    scores = jnp.dot(query, keyed.T, preferred_element_type=jnp.float32) * scale
    weights = jnp.exp(scores) * keep_row[None, :]
    probs = (weights / lax.optimization_barrier(jnp.sum(weights, axis=-1, keepdims=True))).astype(jnp.bfloat16)
    return jnp.dot(probs, valued, preferred_element_type=jnp.float32).astype(jnp.bfloat16)

def spatial_attention(stacked, keep_rows):
    three, patches, columns = stacked.shape
    pairs = keep_rows.shape[0]
    split = stacked.reshape(3, patches, pairs, columns // pairs).transpose(2, 0, 1, 3)
    result = lax.map(jax.checkpoint(pair_attention), (split, keep_rows))
    return result.transpose(1, 0, 2).reshape(patches, columns)

def block_group(tokens, attended, w_so, w_gqkv, w_go):
    patches, groups, width = tokens.shape
    rows = patches * groups
    heads = H
    y_first = (tokens.reshape(rows, width).astype(jnp.float32) + jnp.dot(attended.reshape(rows, width), w_so, preferred_element_type=jnp.float32)).astype(jnp.bfloat16)
    normed = rms_normalize(y_first)
    stacked = jnp.dot(normed, w_gqkv, preferred_element_type=jnp.float32).astype(jnp.bfloat16)
    stacked = stacked.reshape(patches, groups, 3, heads, width // heads)
    query = stacked[:, :, 0].astype(jnp.float32)
    keyed = stacked[:, :, 1].astype(jnp.float32)
    valued = stacked[:, :, 2].astype(jnp.float32)
    scale = (width // heads) ** (-0.5)
    scores = jnp.einsum('pgne,pkne->pngk', query, keyed) * scale
    weights = jnp.exp(scores)
    probs = (weights / lax.optimization_barrier(jnp.sum(weights, axis=-1, keepdims=True))).astype(jnp.bfloat16)
    result = jnp.einsum('pngk,pkne->pgne', probs.astype(jnp.float32), valued).astype(jnp.bfloat16)
    result = result.reshape(rows, width)
    mixed = (y_first.astype(jnp.float32) + jnp.dot(result, w_go, preferred_element_type=jnp.float32)).astype(jnp.bfloat16)
    return mixed.reshape(patches, groups, width)

def reference(tokens, cotangent, w_sqkv, w_so, w_gqkv, w_go, keep):
    pair_group = jnp.arange(G * H, dtype=jnp.int32) // H
    keep_rows = keep.astype(jnp.float32)[pair_group]
    stacked, pull_first = jax.vjp(partial(project_spatial, weight=w_sqkv), tokens)
    attended, pull_spatial = jax.vjp(partial(spatial_attention, keep_rows=keep_rows), stacked)
    mixed, pull_group = jax.vjp(partial(block_group, w_so=w_so, w_gqkv=w_gqkv, w_go=w_go), tokens, attended)
    grad_direct, grad_attended = pull_group(cotangent)
    grad_stacked, = pull_spatial(grad_attended)
    grad_first, = pull_first(grad_stacked)
    return (mixed, grad_direct + grad_first)
```

```python
from functools import partial

import jax
import jax.numpy as jnp
from jax import lax
from jax.experimental import pallas as pl
from jax.experimental.pallas import tpu as pltpu
from jax.sharding import PartitionSpec as P

H = 16
G = 32


def rms_normalize(values):
    wide = values.astype(jnp.float32)
    meansq = jnp.mean(wide * wide, axis=-1, keepdims=True)
    return (wide * lax.rsqrt(meansq + 1e-06)).astype(jnp.bfloat16)


def project_spatial(tokens, weight):
    patches, groups, width = tokens.shape
    normed = rms_normalize(tokens).reshape(patches * groups, width)
    stacked = jnp.dot(normed, weight, preferred_element_type=jnp.float32).astype(jnp.bfloat16)
    stacked = stacked.reshape(patches, groups, 3, width).transpose(2, 0, 1, 3)
    return stacked.reshape(3, patches, groups * width)


def pair_attention(operands):
    stacked, keep_row = operands
    query, keyed, valued = (stacked[0], stacked[1], stacked[2])
    scale = query.shape[-1] ** (-0.5)
    scores = jnp.dot(query, keyed.T, preferred_element_type=jnp.float32) * scale
    weights = jnp.exp(scores) * keep_row[None, :]
    probs = (weights / jnp.sum(weights, axis=-1, keepdims=True)).astype(jnp.bfloat16)
    return jnp.dot(probs, valued, preferred_element_type=jnp.float32).astype(jnp.bfloat16)


def spatial_attention(stacked, keep_rows, attend):
    three, patches, columns = stacked.shape
    pairs = keep_rows.shape[0]
    split = stacked.reshape(3, patches, pairs, columns // pairs).transpose(2, 0, 1, 3)
    result = lax.map(attend, (split, keep_rows))
    return result.transpose(1, 0, 2).reshape(patches, columns)


def block_group(tokens, attended, w_so, w_gqkv, w_go):
    patches, groups, width = tokens.shape
    rows = patches * groups
    heads = H
    y_first = (
        tokens.reshape(rows, width).astype(jnp.float32)
        + jnp.dot(attended.reshape(rows, width), w_so, preferred_element_type=jnp.float32)
    ).astype(jnp.bfloat16)
    normed = rms_normalize(y_first)
    stacked = jnp.dot(normed, w_gqkv, preferred_element_type=jnp.float32).astype(jnp.bfloat16)
    stacked = stacked.reshape(patches, groups, 3, heads, width // heads)
    query = stacked[:, :, 0].astype(jnp.float32)
    keyed = stacked[:, :, 1].astype(jnp.float32)
    valued = stacked[:, :, 2].astype(jnp.float32)
    scale = (width // heads) ** (-0.5)
    scores = jnp.einsum("pgne,pkne->pngk", query, keyed) * scale
    weights = jnp.exp(scores)
    probs = (weights / jnp.sum(weights, axis=-1, keepdims=True)).astype(jnp.bfloat16)
    result = jnp.einsum("pngk,pkne->pgne", probs.astype(jnp.float32), valued).astype(jnp.bfloat16)
    result = result.reshape(rows, width)
    mixed = (
        y_first.astype(jnp.float32) + jnp.dot(result, w_go, preferred_element_type=jnp.float32)
    ).astype(jnp.bfloat16)
    return mixed.reshape(patches, groups, width)


def general_layer(tokens, cotangent, w_sqkv, w_so, w_gqkv, w_go, keep):
    grid_size = lax.axis_size("grid")
    position = lax.axis_index("grid")
    full_sqkv, full_so, full_gqkv, full_go = (
        lax.all_gather(w_sqkv, "grid", axis=0, tiled=True),
        lax.all_gather(w_so, "grid", axis=0, tiled=True),
        lax.all_gather(w_gqkv, "grid", axis=0, tiled=True),
        lax.all_gather(w_go, "grid", axis=0, tiled=True),
    )
    stacked, pull_first = jax.vjp(partial(project_spatial, weight=full_sqkv), tokens)
    banded = lax.all_to_all(stacked, "grid", split_axis=2, concat_axis=1, tiled=True)
    pairs = G * H // grid_size
    pair_ids = position * pairs + jnp.arange(pairs, dtype=jnp.int32)
    select = (pair_ids[:, None] // H == jnp.arange(G, dtype=jnp.int32)[None, :]).astype(jnp.float32)
    keep_rows = jnp.dot(select, keep.astype(jnp.float32), precision=lax.Precision.HIGHEST)
    attend = jax.checkpoint(pair_attention)
    attended_bands, pull_spatial = jax.vjp(
        partial(spatial_attention, keep_rows=keep_rows, attend=attend), banded
    )
    attended = lax.all_to_all(attended_bands, "grid", split_axis=0, concat_axis=1, tiled=True)
    mixed, pull_group = jax.vjp(
        partial(block_group, w_so=full_so, w_gqkv=full_gqkv, w_go=full_go), tokens, attended
    )
    grad_direct, grad_attended = pull_group(cotangent)
    grad_bands = lax.all_to_all(grad_attended, "grid", split_axis=1, concat_axis=0, tiled=True)
    (grad_banded,) = pull_spatial(grad_bands)
    grad_stacked = lax.all_to_all(grad_banded, "grid", split_axis=1, concat_axis=2, tiled=True)
    (grad_first,) = pull_first(grad_stacked)
    return (mixed, grad_direct + grad_first)


def nt(a, b):
    return lax.dot_general(a, b, (((1,), (1,)), ((), ())), preferred_element_type=jnp.float32)


def tn(a, b):
    return lax.dot_general(a, b, (((0,), (0,)), ((), ())), preferred_element_type=jnp.float32)


def nn(a, b):
    return jnp.dot(a, b, preferred_element_type=jnp.float32)


def inverse_rms(wide):
    return lax.rsqrt(jnp.mean(wide * wide, axis=-1, keepdims=True) + 1e-06)


def norm_grad(wide, inverse, grad):
    inner = jnp.mean(grad * wide, axis=-1, keepdims=True)
    return grad * inverse - wide * (inverse * inverse * inverse * inner)


def head_pair(values, low):
    zero = jnp.zeros_like(values)
    return jnp.concatenate([jnp.where(low, values, zero), jnp.where(low, zero, values)], axis=0)


def join_pair(stacked, low):
    rows = stacked.shape[0] // 2
    return jnp.where(low, stacked[:rows], stacked[rows:])


def halves(values):
    width = values.shape[1] // 2
    first = jnp.sum(values[:, :width], axis=-1, keepdims=True)
    second = jnp.sum(values[:, width:], axis=-1, keepdims=True)
    rows = values.shape[0]
    return jnp.concatenate(
        [jnp.broadcast_to(first, (rows, width)), jnp.broadcast_to(second, (rows, width))], axis=1
    )


def low_lanes(rows):
    return lax.broadcasted_iota(jnp.int32, (rows, 128), 1) < 64


def pair_forward(qkv, allowed, low, width, pair):
    query = qkv[:, pair * 128 : pair * 128 + 128]
    keyed = head_pair(qkv[:, width + pair * 128 : width + pair * 128 + 128], low)
    valued = head_pair(qkv[:, 2 * width + pair * 128 : 2 * width + pair * 128 + 128], low)
    weights = jnp.where(allowed, jnp.exp(nt(query, keyed) * 0.125), 0.0)
    probs = weights / halves(weights)
    result = nn(probs.astype(jnp.bfloat16), valued).astype(jnp.bfloat16)
    return probs, result


def pair_backward(qkv, probs, grad, low, width, pair):
    query = qkv[:, pair * 128 : pair * 128 + 128]
    keyed = head_pair(qkv[:, width + pair * 128 : width + pair * 128 + 128], low)
    valued = head_pair(qkv[:, 2 * width + pair * 128 : 2 * width + pair * 128 + 128], low)
    grad_probs = nt(grad, valued).astype(jnp.bfloat16).astype(jnp.float32)
    grad_scores = probs * (grad_probs - halves(grad_probs * probs))
    grad_scores = (grad_scores * 0.125).astype(jnp.bfloat16)
    grad_value = join_pair(tn(probs.astype(jnp.bfloat16), grad), low).astype(jnp.bfloat16)
    grad_query = nn(grad_scores, keyed).astype(jnp.bfloat16)
    grad_key = join_pair(tn(grad_scores, query), low).astype(jnp.bfloat16)
    return grad_query, grad_key, grad_value


def spatial_forward(tokens, keep, w_qkv, w_out, y_out, qkv_out, probs_out, qkv_buf, out_buf, sems):
    rows, width = tokens.shape
    span = 2 * rows
    load_qkv = pltpu.make_async_copy(w_qkv, qkv_buf, sems.at[0])
    load_out = pltpu.make_async_copy(w_out, out_buf, sems.at[1])
    load_qkv.start()
    load_out.start()
    wide = tokens[...].astype(jnp.float32)
    normed = (wide * inverse_rms(wide)).astype(jnp.bfloat16)
    allowed = keep[...] > 0
    low = low_lanes(rows)
    load_qkv.wait()
    qkv_out[...] = nn(normed, qkv_buf[...]).astype(jnp.bfloat16)
    results = []
    for pair in range(width // 128):
        probs, result = pair_forward(qkv_out, allowed, low, width, pair)
        probs_out[:, pair * span : pair * span + span] = probs
        results.append(result)
    load_out.wait()
    total = wide + nn(jnp.concatenate(results, axis=1), out_buf[...])
    y_out[...] = total.astype(jnp.bfloat16)


def spatial_backward(tokens, grad, qkv, probs, w_qkv, w_out, grad_out, qkv_buf, out_buf, grads, sems):
    rows, width = tokens.shape
    span = 2 * rows
    load_out = pltpu.make_async_copy(w_out, out_buf, sems.at[1])
    load_qkv = pltpu.make_async_copy(w_qkv, qkv_buf, sems.at[0])
    load_out.start()
    load_qkv.start()
    low = low_lanes(rows)
    load_out.wait()
    grad_attended = nt(grad[...], out_buf[...]).astype(jnp.bfloat16)
    for pair in range(width // 128):
        at = pair * 128
        parts = pair_backward(
            qkv, probs[:, pair * span : pair * span + span], grad_attended[:, at : at + 128], low, width, pair
        )
        for which, part in enumerate(parts):
            grads[:, which * width + at : which * width + at + 128] = part
    wide = tokens[...].astype(jnp.float32)
    inverse = inverse_rms(wide)
    load_qkv.wait()
    grad_normed = nt(grads[...], qkv_buf[...]).astype(jnp.bfloat16).astype(jnp.float32)
    grad_out[...] = norm_grad(wide, inverse, grad_normed).astype(jnp.bfloat16)


def reorder(patches, groups, backward):
    rows = patches * groups
    here = lax.broadcasted_iota(jnp.int32, (rows, rows), 1 if backward else 0)
    there = lax.broadcasted_iota(jnp.int32, (rows, rows), 0 if backward else 1)
    patch, group = here // groups, here % groups
    return (there == group * patches + patch).astype(jnp.bfloat16)


def group_layer(
    patches, y_in, cotangent, w_qkv, w_out, mixed, grad_y, grad_bands, qkv_buf, out_buf, qkv, grads, probs_buf, sems
):
    rows, width = y_in.shape
    groups = rows // patches
    span = 2 * rows
    load_qkv = pltpu.make_async_copy(w_qkv, qkv_buf, sems.at[0])
    load_out = pltpu.make_async_copy(w_out, out_buf, sems.at[1])
    load_qkv.start()
    load_out.start()
    y_first = nn(reorder(patches, groups, False), y_in[...]).astype(jnp.bfloat16)
    wide = y_first.astype(jnp.float32)
    inverse = inverse_rms(wide)
    normed = (wide * inverse).astype(jnp.bfloat16)
    low = low_lanes(rows)
    row_patch = lax.broadcasted_iota(jnp.int32, (rows, 2 * rows), 0) // groups
    column_patch = (lax.broadcasted_iota(jnp.int32, (rows, 2 * rows), 1) % rows) // groups
    allowed = row_patch == column_patch
    load_qkv.wait()
    qkv[...] = nn(normed, qkv_buf[...]).astype(jnp.bfloat16)
    results = []
    for pair in range(width // 128):
        probs, result = pair_forward(qkv, allowed, low, width, pair)
        probs_buf[:, pair * span : pair * span + span] = probs
        results.append(result)
    load_out.wait()
    mixed[...] = (wide + nn(jnp.concatenate(results, axis=1), out_buf[...])).astype(jnp.bfloat16)
    grad_attended = nt(cotangent[...], out_buf[...]).astype(jnp.bfloat16)
    for pair in range(width // 128):
        at = pair * 128
        parts = pair_backward(
            qkv, probs_buf[:, pair * span : pair * span + span], grad_attended[:, at : at + 128], low, width, pair
        )
        for which, part in enumerate(parts):
            grads[:, which * width + at : which * width + at + 128] = part
    grad_normed = nt(grads[...], qkv_buf[...]).astype(jnp.bfloat16).astype(jnp.float32)
    through = norm_grad(wide, inverse, grad_normed).astype(jnp.bfloat16)
    total = cotangent[...] + through
    grad_y[...] = total
    grad_bands[...] = nn(reorder(patches, groups, True), total).astype(jnp.bfloat16)


VMEM_SPEC = pl.BlockSpec(memory_space=pltpu.VMEM)
ANY_SPEC = pl.BlockSpec(memory_space=pl.ANY)
PARAMS = pltpu.CompilerParams(vmem_limit_bytes=44 * 1024 * 1024)


def shape(rows, columns, dtype=jnp.bfloat16):
    return jax.ShapeDtypeStruct((rows, columns), dtype)


def weight_scratch(width):
    return [pltpu.VMEM((width, 3 * width), jnp.bfloat16), pltpu.VMEM((width, width), jnp.bfloat16)]


def cost(rows, width, passes):
    return pl.CostEstimate(
        flops=passes * 8 * rows * width * width, bytes_accessed=8 * width * width, transcendentals=16 * rows * rows
    )


def exchange(values):
    return lax.all_to_all(values, "grid", split_axis=0, concat_axis=0, tiled=True)


def banded_layer(tokens, cotangent, w_sqkv, w_so, w_gqkv, w_go, keep):
    patches, groups, width = tokens.shape
    rows = patches * groups
    all_patches = patches * lax.axis_size("grid")
    position = lax.axis_index("grid")
    full_sqkv, full_so, full_gqkv, full_go = (
        lax.all_gather(w_sqkv, "grid", axis=0, tiled=True),
        lax.all_gather(w_so, "grid", axis=0, tiled=True),
        lax.all_gather(w_gqkv, "grid", axis=0, tiled=True),
        lax.all_gather(w_go, "grid", axis=0, tiled=True),
    )
    banded = exchange(tokens.transpose(1, 0, 2)).reshape(all_patches, width)
    keep_row = lax.dynamic_slice_in_dim(keep, position, 1, 0)
    keep_row = jnp.concatenate([keep_row, keep_row], axis=1)
    pairs = width // 128
    y_bands, qkv, probs = pl.pallas_call(
        spatial_forward,
        out_shape=(
            shape(all_patches, width),
            shape(all_patches, 3 * width),
            shape(all_patches, 2 * pairs * all_patches, jnp.float32),
        ),
        in_specs=[VMEM_SPEC, VMEM_SPEC, ANY_SPEC, ANY_SPEC],
        out_specs=(VMEM_SPEC,) * 3,
        scratch_shapes=weight_scratch(width) + [pltpu.SemaphoreType.DMA((2,))],
        compiler_params=PARAMS,
        cost_estimate=cost(all_patches, width, 1),
        name="spatial_forward",
    )(banded, keep_row, full_sqkv, full_so)
    y_rows = exchange(y_bands.reshape(groups, patches, width)).reshape(rows, width)
    mixed, grad_y, grad_bands = pl.pallas_call(
        partial(group_layer, patches),
        out_shape=(shape(rows, width),) * 3,
        in_specs=[VMEM_SPEC, VMEM_SPEC, ANY_SPEC, ANY_SPEC],
        out_specs=(VMEM_SPEC,) * 3,
        scratch_shapes=weight_scratch(width)
        + [
            pltpu.VMEM((rows, 3 * width), jnp.bfloat16),
            pltpu.VMEM((rows, 3 * width), jnp.bfloat16),
            pltpu.VMEM((rows, 2 * pairs * rows), jnp.float32),
            pltpu.SemaphoreType.DMA((2,)),
        ],
        compiler_params=PARAMS,
        cost_estimate=cost(rows, width, 2),
        name="group_layer",
    )(y_rows, cotangent.reshape(rows, width), full_gqkv, full_go)
    grad_banded = exchange(grad_bands.reshape(groups, patches, width)).reshape(all_patches, width)
    grad_first = pl.pallas_call(
        spatial_backward,
        out_shape=shape(all_patches, width),
        in_specs=[VMEM_SPEC] * 4 + [ANY_SPEC, ANY_SPEC],
        out_specs=VMEM_SPEC,
        scratch_shapes=weight_scratch(width)
        + [pltpu.VMEM((all_patches, 3 * width), jnp.bfloat16), pltpu.SemaphoreType.DMA((2,))],
        compiler_params=PARAMS,
        cost_estimate=cost(all_patches, width, 1),
        name="spatial_backward",
    )(banded, grad_banded, qkv, probs, full_sqkv, full_so)
    grad_first = exchange(grad_first.reshape(groups, patches, width)).transpose(1, 0, 2)
    whole = (patches, groups, width)
    return (mixed.reshape(whole), grad_y.reshape(whole) + grad_first)


def local(tokens, cotangent, w_sqkv, w_so, w_gqkv, w_go, keep):
    patches, groups, width = tokens.shape
    size = lax.axis_size("grid")
    fits = size == groups and width == 64 * H and patches * groups % 128 == 0 and patches * size % 128 == 0
    layer = banded_layer if fits else general_layer
    return layer(tokens, cotangent, w_sqkv, w_so, w_gqkv, w_go, keep)


def solution(mesh):
    placed = (
        P(("parts", "grid"), None, None),
        P(("parts", "grid"), None, None),
        P("grid", None),
        P("grid", None),
        P("grid", None),
        P("grid", None),
        P(None, "parts"),
    )
    return jax.shard_map(
        local,
        mesh=mesh,
        in_specs=placed,
        out_specs=(P(("parts", "grid"), None, None), P(("parts", "grid"), None, None)),
        check_vma=False,
    )
```

```python
from functools import partial

import jax
import jax.numpy as jnp
from jax import lax
from jax.experimental import pallas as pl
from jax.experimental.pallas import tpu as pltpu
from jax.sharding import PartitionSpec as P

H = 16
G = 32


def rms_normalize(values):
    wide = values.astype(jnp.float32)
    meansq = jnp.mean(wide * wide, axis=-1, keepdims=True)
    return (wide * lax.rsqrt(meansq + 1e-06)).astype(jnp.bfloat16)


def project_spatial(tokens, weight):
    patches, groups, width = tokens.shape
    normed = rms_normalize(tokens).reshape(patches * groups, width)
    stacked = jnp.dot(normed, weight, preferred_element_type=jnp.float32).astype(jnp.bfloat16)
    stacked = stacked.reshape(patches, groups, 3, width).transpose(2, 0, 1, 3)
    return stacked.reshape(3, patches, groups * width)


def pair_attention(operands):
    stacked, keep_row = operands
    query, keyed, valued = (stacked[0], stacked[1], stacked[2])
    scale = query.shape[-1] ** (-0.5)
    scores = jnp.dot(query, keyed.T, preferred_element_type=jnp.float32) * scale
    weights = jnp.exp(scores) * keep_row[None, :]
    probs = (weights / jnp.sum(weights, axis=-1, keepdims=True)).astype(jnp.bfloat16)
    return jnp.dot(probs, valued, preferred_element_type=jnp.float32).astype(jnp.bfloat16)


def spatial_attention(stacked, keep_rows, attend):
    three, patches, columns = stacked.shape
    pairs = keep_rows.shape[0]
    split = stacked.reshape(3, patches, pairs, columns // pairs).transpose(2, 0, 1, 3)
    result = lax.map(attend, (split, keep_rows))
    return result.transpose(1, 0, 2).reshape(patches, columns)


def block_group(tokens, attended, w_so, w_gqkv, w_go):
    patches, groups, width = tokens.shape
    rows = patches * groups
    heads = H
    y_first = (
        tokens.reshape(rows, width).astype(jnp.float32)
        + jnp.dot(attended.reshape(rows, width), w_so, preferred_element_type=jnp.float32)
    ).astype(jnp.bfloat16)
    normed = rms_normalize(y_first)
    stacked = jnp.dot(normed, w_gqkv, preferred_element_type=jnp.float32).astype(jnp.bfloat16)
    stacked = stacked.reshape(patches, groups, 3, heads, width // heads)
    query = stacked[:, :, 0].astype(jnp.float32)
    keyed = stacked[:, :, 1].astype(jnp.float32)
    valued = stacked[:, :, 2].astype(jnp.float32)
    scale = (width // heads) ** (-0.5)
    scores = jnp.einsum("pgne,pkne->pngk", query, keyed) * scale
    weights = jnp.exp(scores)
    probs = (weights / jnp.sum(weights, axis=-1, keepdims=True)).astype(jnp.bfloat16)
    result = jnp.einsum("pngk,pkne->pgne", probs.astype(jnp.float32), valued).astype(jnp.bfloat16)
    result = result.reshape(rows, width)
    mixed = (
        y_first.astype(jnp.float32) + jnp.dot(result, w_go, preferred_element_type=jnp.float32)
    ).astype(jnp.bfloat16)
    return mixed.reshape(patches, groups, width)


def general_layer(tokens, cotangent, w_sqkv, w_so, w_gqkv, w_go, keep):
    grid_size = lax.axis_size("grid")
    position = lax.axis_index("grid")
    full_sqkv, full_so, full_gqkv, full_go = (
        lax.all_gather(w_sqkv, "grid", axis=0, tiled=True),
        lax.all_gather(w_so, "grid", axis=0, tiled=True),
        lax.all_gather(w_gqkv, "grid", axis=0, tiled=True),
        lax.all_gather(w_go, "grid", axis=0, tiled=True),
    )
    stacked, pull_first = jax.vjp(partial(project_spatial, weight=full_sqkv), tokens)
    banded = lax.all_to_all(stacked, "grid", split_axis=2, concat_axis=1, tiled=True)
    pairs = G * H // grid_size
    pair_ids = position * pairs + jnp.arange(pairs, dtype=jnp.int32)
    select = (pair_ids[:, None] // H == jnp.arange(G, dtype=jnp.int32)[None, :]).astype(jnp.float32)
    keep_rows = jnp.dot(select, keep.astype(jnp.float32), precision=lax.Precision.HIGHEST)
    attend = jax.checkpoint(pair_attention)
    attended_bands, pull_spatial = jax.vjp(
        partial(spatial_attention, keep_rows=keep_rows, attend=attend), banded
    )
    attended = lax.all_to_all(attended_bands, "grid", split_axis=0, concat_axis=1, tiled=True)
    mixed, pull_group = jax.vjp(
        partial(block_group, w_so=full_so, w_gqkv=full_gqkv, w_go=full_go), tokens, attended
    )
    grad_direct, grad_attended = pull_group(cotangent)
    grad_bands = lax.all_to_all(grad_attended, "grid", split_axis=1, concat_axis=0, tiled=True)
    (grad_banded,) = pull_spatial(grad_bands)
    grad_stacked = lax.all_to_all(grad_banded, "grid", split_axis=1, concat_axis=2, tiled=True)
    (grad_first,) = pull_first(grad_stacked)
    return (mixed, grad_direct + grad_first)


def nt(a, b):
    return lax.dot_general(a, b, (((1,), (1,)), ((), ())), preferred_element_type=jnp.float32)


def tn(a, b):
    return lax.dot_general(a, b, (((0,), (0,)), ((), ())), preferred_element_type=jnp.float32)


def nn(a, b):
    return jnp.dot(a, b, preferred_element_type=jnp.float32)


def inverse_rms(wide):
    return lax.rsqrt(jnp.mean(wide * wide, axis=-1, keepdims=True) + 1e-06)


def norm_grad(wide, inverse, grad):
    inner = jnp.mean(grad * wide, axis=-1, keepdims=True)
    return grad * inverse - wide * (inverse * inverse * inverse * inner)


def head_pair(values, low):
    zero = jnp.zeros_like(values)
    return jnp.concatenate([jnp.where(low, values, zero), jnp.where(low, zero, values)], axis=0)


def join_pair(stacked, low):
    rows = stacked.shape[0] // 2
    return jnp.where(low, stacked[:rows], stacked[rows:])


def halves(values):
    width = values.shape[1] // 2
    first = jnp.sum(values[:, :width], axis=-1, keepdims=True)
    second = jnp.sum(values[:, width:], axis=-1, keepdims=True)
    rows = values.shape[0]
    return jnp.concatenate(
        [jnp.broadcast_to(first, (rows, width)), jnp.broadcast_to(second, (rows, width))], axis=1
    )


def low_lanes(rows):
    return lax.broadcasted_iota(jnp.int32, (rows, 128), 1) < 64


def pair_forward(qkv, allowed, low, width, pair):
    query = qkv[:, pair * 128 : pair * 128 + 128]
    keyed = head_pair(qkv[:, width + pair * 128 : width + pair * 128 + 128], low)
    valued = head_pair(qkv[:, 2 * width + pair * 128 : 2 * width + pair * 128 + 128], low)
    weights = jnp.where(allowed, jnp.exp(nt(query, keyed) * 0.125), 0.0)
    probs = weights / halves(weights)
    result = nn(probs.astype(jnp.bfloat16), valued).astype(jnp.bfloat16)
    return probs, result


def pair_backward(qkv, probs, grad, low, width, pair):
    query = qkv[:, pair * 128 : pair * 128 + 128]
    keyed = head_pair(qkv[:, width + pair * 128 : width + pair * 128 + 128], low)
    valued = head_pair(qkv[:, 2 * width + pair * 128 : 2 * width + pair * 128 + 128], low)
    grad_probs = nt(grad, valued).astype(jnp.bfloat16).astype(jnp.float32)
    grad_scores = probs * (grad_probs - halves(grad_probs * probs))
    grad_scores = (grad_scores * 0.125).astype(jnp.bfloat16)
    grad_value = join_pair(tn(probs.astype(jnp.bfloat16), grad), low).astype(jnp.bfloat16)
    grad_query = nn(grad_scores, keyed).astype(jnp.bfloat16)
    grad_key = join_pair(tn(grad_scores, query), low).astype(jnp.bfloat16)
    return grad_query, grad_key, grad_value


def place_rows(pieces, first, buffer, sem, rows_each):
    position = lax.axis_index("grid")
    size = buffer.shape[0] // rows_each
    core = position % 2
    one, other = 2 * (core + 1), 4 // (core + 1)
    own = (0, one, other, 6)
    sibling = (0, other, one, 6)
    depth = len(pieces) // 2
    for at, piece in enumerate(pieces):
        flip = own[at] if at < depth else sibling[at - depth]
        base = (position if at < depth else position + 1 - 2 * core) ^ flip
        for step in range(piece.shape[0] // rows_each):
            shard = lax.rem(base + size - 8 * step, size)
            pltpu.make_async_copy(
                piece.at[pl.ds(step * rows_each, rows_each), pl.ds(first, buffer.shape[1])],
                buffer.at[pl.ds(pl.multiple_of(shard * rows_each, rows_each), rows_each)],
                sem,
            ).start()


def wait_rows(buffer, sem):
    pltpu.make_async_copy(buffer, buffer, sem).wait()


def spatial_forward(tokens, keep, *refs):
    pieces, (result_out, qkv_out, probs_out, qkv_buf, sems) = refs[:-5], refs[-5:]
    rows, width = tokens.shape
    span = 2 * rows
    place_rows(pieces, 0, qkv_buf, sems.at[0], width // lax.axis_size("grid"))
    wide = tokens[...].astype(jnp.float32)
    normed = (wide * inverse_rms(wide)).astype(jnp.bfloat16)
    allowed = keep[...] > 0
    low = low_lanes(rows)
    wait_rows(qkv_buf, sems.at[0])
    qkv_out[...] = nn(normed, qkv_buf[...]).astype(jnp.bfloat16)
    for pair in range(width // 128):
        probs, result = pair_forward(qkv_out, allowed, low, width, pair)
        probs_out[:, pair * span : pair * span + span] = probs
        result_out[:, pair * 128 : pair * 128 + 128] = result


def spatial_backward(tokens, grad, qkv, probs, *refs):
    pieces, (grad_out, qkv_buf, grads, sems) = refs[:-4], refs[-4:]
    rows, width = tokens.shape
    span = 2 * rows
    place_rows(pieces, 0, qkv_buf, sems.at[0], width // lax.axis_size("grid"))
    low = low_lanes(rows)
    for pair in range(width // 128):
        at = pair * 128
        parts = pair_backward(
            qkv, probs[:, pair * span : pair * span + span], grad[:, at : at + 128], low, width, pair
        )
        for which, part in enumerate(parts):
            grads[:, which * width + at : which * width + at + 128] = part
    wide = tokens[...].astype(jnp.float32)
    inverse = inverse_rms(wide)
    wait_rows(qkv_buf, sems.at[0])
    grad_normed = nt(grads[...], qkv_buf[...]).astype(jnp.bfloat16).astype(jnp.float32)
    grad_out[...] = norm_grad(wide, inverse, grad_normed).astype(jnp.bfloat16)


def reorder(patches, groups, backward):
    rows = patches * groups
    here = lax.broadcasted_iota(jnp.int32, (rows, rows), 1 if backward else 0)
    there = lax.broadcasted_iota(jnp.int32, (rows, rows), 0 if backward else 1)
    patch, group = here // groups, here % groups
    return (there == group * patches + patch).astype(jnp.bfloat16)


def group_layer(patches, tokens, attended, cotangent, w_go, *refs):
    pieces, rest = refs[:-12], refs[-12:]
    mixed, grad_y, grad_bands, so_buf, qkv_buf, go_buf, qkv, grads, probs_buf, y_buf, go_sem, sems = rest
    rows, width = tokens.shape
    groups = rows // patches
    span = 2 * rows
    each = width // lax.axis_size("grid")
    place_rows(pieces, 0, so_buf, sems.at[0], each)
    place_rows(pieces, width, qkv_buf, sems.at[1], each)
    load_go = pltpu.make_async_copy(w_go, go_buf, go_sem)
    load_go.start()
    ordered = nn(reorder(patches, groups, False), attended[...]).astype(jnp.bfloat16)
    low = low_lanes(rows)
    row_patch = lax.broadcasted_iota(jnp.int32, (rows, span), 0) // groups
    column_patch = (lax.broadcasted_iota(jnp.int32, (rows, span), 1) % rows) // groups
    allowed = row_patch == column_patch
    wait_rows(so_buf, sems.at[0])
    y_first = (tokens[...].astype(jnp.float32) + nn(ordered, so_buf[...])).astype(jnp.bfloat16)
    wide = y_first.astype(jnp.float32)
    y_buf[...] = wide
    inverse = inverse_rms(wide)
    normed = (wide * inverse).astype(jnp.bfloat16)
    wait_rows(qkv_buf, sems.at[1])
    qkv[...] = nn(normed, qkv_buf[...]).astype(jnp.bfloat16)
    results = []
    for pair in range(width // 128):
        probs, result = pair_forward(qkv, allowed, low, width, pair)
        probs_buf[:, pair * span : pair * span + span] = probs
        results.append(result)
    load_go.wait()
    mixed[...] = (y_buf[...] + nn(jnp.concatenate(results, axis=1), go_buf[...])).astype(jnp.bfloat16)
    grad_attended = nt(cotangent[...], go_buf[...]).astype(jnp.bfloat16)
    for pair in range(width // 128):
        at = pair * 128
        parts = pair_backward(
            qkv, probs_buf[:, pair * span : pair * span + span], grad_attended[:, at : at + 128], low, width, pair
        )
        for which, part in enumerate(parts):
            grads[:, which * width + at : which * width + at + 128] = part
    grad_normed = nt(grads[...], qkv_buf[...]).astype(jnp.bfloat16).astype(jnp.float32)
    through = norm_grad(y_buf[...], inverse, grad_normed).astype(jnp.bfloat16)
    total = cotangent[...] + through
    grad_y[...] = total
    spread = nt(total, so_buf[...]).astype(jnp.bfloat16)
    grad_bands[...] = nn(reorder(patches, groups, True), spread).astype(jnp.bfloat16)


VMEM_SPEC = pl.BlockSpec(memory_space=pltpu.VMEM)
ANY_SPEC = pl.BlockSpec(memory_space=pl.ANY)
PARAMS = pltpu.CompilerParams(vmem_limit_bytes=56 * 1024 * 1024)


def shape(rows, columns, dtype=jnp.bfloat16):
    return jax.ShapeDtypeStruct((rows, columns), dtype)


def cost(rows, width, passes):
    return pl.CostEstimate(
        flops=passes * 8 * rows * width * width, bytes_accessed=8 * width * width, transcendentals=16 * rows * rows
    )


def exchange(values):
    return lax.all_to_all(values, "grid", split_axis=0, concat_axis=0, tiled=True)


def mesh_moves(size):
    everyone = range(size)
    first = [(i, i ^ (2 if i % 2 == 0 else 4)) for i in everyone]
    second = [(i, i ^ (4 if i % 2 == 0 else 2)) for i in everyone]
    sibling = [(i, i ^ 1) for i in everyone]
    along = [[(i, (i + 8 * step) % size) for i in everyone] for step in range(1, size // 8)]
    return first, second, sibling, along


def move(values, table):
    return lax.ppermute(values, "grid", table)


def gather_rows(shard):
    first, second, sibling, along = mesh_moves(lax.axis_size("grid"))
    line = jnp.concatenate([shard] + [move(shard, table) for table in along], axis=0)
    one = move(line, first)
    other = move(line, second)
    both = move(one, second)
    held = [line, one, other, both]
    return held + [move(block, sibling) for block in held]


def banded_layer(tokens, cotangent, w_sqkv, w_so, w_gqkv, w_go, keep):
    patches, groups, width = tokens.shape
    rows = patches * groups
    all_patches = patches * lax.axis_size("grid")
    position = lax.axis_index("grid")
    spatial_rows = gather_rows(w_sqkv)
    group_rows = gather_rows(jnp.concatenate([w_so, w_gqkv], axis=1))
    full_go = lax.all_gather(w_go, "grid", axis=0, tiled=True)
    banded = exchange(tokens.transpose(1, 0, 2)).reshape(all_patches, width)
    keep_row = lax.dynamic_slice_in_dim(keep, position, 1, 0)
    keep_row = jnp.concatenate([keep_row, keep_row], axis=1)
    pairs = width // 128
    attended, qkv, probs = pl.pallas_call(
        spatial_forward,
        out_shape=(
            shape(all_patches, width),
            shape(all_patches, 3 * width),
            shape(all_patches, 2 * pairs * all_patches, jnp.float32),
        ),
        in_specs=[VMEM_SPEC] * 2 + [ANY_SPEC] * len(spatial_rows),
        out_specs=(VMEM_SPEC,) * 3,
        scratch_shapes=[pltpu.VMEM((width, 3 * width), jnp.bfloat16), pltpu.SemaphoreType.DMA((1,))],
        compiler_params=PARAMS,
        cost_estimate=cost(all_patches, width, 1),
        name="spatial_forward",
    )(banded, keep_row, *spatial_rows)
    attended = exchange(attended.reshape(groups, patches, width)).reshape(rows, width)
    mixed, grad_y, grad_bands = pl.pallas_call(
        partial(group_layer, patches),
        out_shape=(shape(rows, width),) * 3,
        in_specs=[VMEM_SPEC] * 3 + [ANY_SPEC] * (1 + len(group_rows)),
        out_specs=(VMEM_SPEC,) * 3,
        scratch_shapes=[
            pltpu.VMEM((width, width), jnp.bfloat16),
            pltpu.VMEM((width, 3 * width), jnp.bfloat16),
            pltpu.VMEM((width, width), jnp.bfloat16),
            pltpu.VMEM((rows, 3 * width), jnp.bfloat16),
            pltpu.VMEM((rows, 3 * width), jnp.bfloat16),
            pltpu.VMEM((rows, 2 * pairs * rows), jnp.float32),
            pltpu.VMEM((rows, width), jnp.float32),
            pltpu.SemaphoreType.DMA,
            pltpu.SemaphoreType.DMA((2,)),
        ],
        compiler_params=PARAMS,
        cost_estimate=cost(rows, width, 2),
        name="group_layer",
    )(tokens.reshape(rows, width), attended, cotangent.reshape(rows, width), full_go, *group_rows)
    grad_banded = exchange(grad_bands.reshape(groups, patches, width)).reshape(all_patches, width)
    grad_first = pl.pallas_call(
        spatial_backward,
        out_shape=shape(all_patches, width),
        in_specs=[VMEM_SPEC] * 4 + [ANY_SPEC] * len(spatial_rows),
        out_specs=VMEM_SPEC,
        scratch_shapes=[
            pltpu.VMEM((width, 3 * width), jnp.bfloat16),
            pltpu.VMEM((all_patches, 3 * width), jnp.bfloat16),
            pltpu.SemaphoreType.DMA((1,)),
        ],
        compiler_params=PARAMS,
        cost_estimate=cost(all_patches, width, 1),
        name="spatial_backward",
    )(banded, grad_banded, qkv, probs, *spatial_rows)
    grad_first = exchange(grad_first.reshape(groups, patches, width)).transpose(1, 0, 2)
    whole = (patches, groups, width)
    return (mixed.reshape(whole), grad_y.reshape(whole) + grad_first)


def local(tokens, cotangent, w_sqkv, w_so, w_gqkv, w_go, keep):
    patches, groups, width = tokens.shape
    size = lax.axis_size("grid")
    fits = size == groups and size % 8 == 0 and width % (16 * size) == 0 and width == 64 * H and patches * groups % 128 == 0 and patches * size % 128 == 0
    layer = banded_layer if fits else general_layer
    return layer(tokens, cotangent, w_sqkv, w_so, w_gqkv, w_go, keep)


def solution(mesh):
    placed = (
        P(("parts", "grid"), None, None),
        P(("parts", "grid"), None, None),
        P("grid", None),
        P("grid", None),
        P("grid", None),
        P("grid", None),
        P(None, "parts"),
    )
    return jax.shard_map(
        local,
        mesh=mesh,
        in_specs=placed,
        out_specs=(P(("parts", "grid"), None, None), P(("parts", "grid"), None, None)),
        check_vma=False,
    )
```

```python
from functools import partial

import jax
import jax.numpy as jnp
from jax import lax
from jax.experimental import pallas as pl
from jax.experimental.pallas import tpu as pltpu
from jax.sharding import PartitionSpec as P

H = 16
G = 32


def rms_normalize(values):
    wide = values.astype(jnp.float32)
    meansq = jnp.mean(wide * wide, axis=-1, keepdims=True)
    return (wide * lax.rsqrt(meansq + 1e-06)).astype(jnp.bfloat16)


def project_spatial(tokens, weight):
    patches, groups, width = tokens.shape
    normed = rms_normalize(tokens).reshape(patches * groups, width)
    stacked = jnp.dot(normed, weight, preferred_element_type=jnp.float32).astype(jnp.bfloat16)
    stacked = stacked.reshape(patches, groups, 3, width).transpose(2, 0, 1, 3)
    return stacked.reshape(3, patches, groups * width)


def pair_attention(operands):
    stacked, keep_row = operands
    query, keyed, valued = (stacked[0], stacked[1], stacked[2])
    scale = query.shape[-1] ** (-0.5)
    scores = jnp.dot(query, keyed.T, preferred_element_type=jnp.float32) * scale
    weights = jnp.exp(scores) * keep_row[None, :]
    probs = (weights / jnp.sum(weights, axis=-1, keepdims=True)).astype(jnp.bfloat16)
    return jnp.dot(probs, valued, preferred_element_type=jnp.float32).astype(jnp.bfloat16)


def spatial_attention(stacked, keep_rows, attend):
    three, patches, columns = stacked.shape
    pairs = keep_rows.shape[0]
    split = stacked.reshape(3, patches, pairs, columns // pairs).transpose(2, 0, 1, 3)
    result = lax.map(attend, (split, keep_rows))
    return result.transpose(1, 0, 2).reshape(patches, columns)


def block_group(tokens, attended, w_so, w_gqkv, w_go):
    patches, groups, width = tokens.shape
    rows = patches * groups
    heads = H
    y_first = (
        tokens.reshape(rows, width).astype(jnp.float32)
        + jnp.dot(attended.reshape(rows, width), w_so, preferred_element_type=jnp.float32)
    ).astype(jnp.bfloat16)
    normed = rms_normalize(y_first)
    stacked = jnp.dot(normed, w_gqkv, preferred_element_type=jnp.float32).astype(jnp.bfloat16)
    stacked = stacked.reshape(patches, groups, 3, heads, width // heads)
    query = stacked[:, :, 0].astype(jnp.float32)
    keyed = stacked[:, :, 1].astype(jnp.float32)
    valued = stacked[:, :, 2].astype(jnp.float32)
    scale = (width // heads) ** (-0.5)
    scores = jnp.einsum("pgne,pkne->pngk", query, keyed) * scale
    weights = jnp.exp(scores)
    probs = (weights / jnp.sum(weights, axis=-1, keepdims=True)).astype(jnp.bfloat16)
    result = jnp.einsum("pngk,pkne->pgne", probs.astype(jnp.float32), valued).astype(jnp.bfloat16)
    result = result.reshape(rows, width)
    mixed = (
        y_first.astype(jnp.float32) + jnp.dot(result, w_go, preferred_element_type=jnp.float32)
    ).astype(jnp.bfloat16)
    return mixed.reshape(patches, groups, width)


def general_layer(tokens, cotangent, w_sqkv, w_so, w_gqkv, w_go, keep):
    grid_size = lax.axis_size("grid")
    position = lax.axis_index("grid")
    full_sqkv, full_so, full_gqkv, full_go = (
        lax.all_gather(w_sqkv, "grid", axis=0, tiled=True),
        lax.all_gather(w_so, "grid", axis=0, tiled=True),
        lax.all_gather(w_gqkv, "grid", axis=0, tiled=True),
        lax.all_gather(w_go, "grid", axis=0, tiled=True),
    )
    stacked, pull_first = jax.vjp(partial(project_spatial, weight=full_sqkv), tokens)
    banded = lax.all_to_all(stacked, "grid", split_axis=2, concat_axis=1, tiled=True)
    pairs = G * H // grid_size
    pair_ids = position * pairs + jnp.arange(pairs, dtype=jnp.int32)
    select = (pair_ids[:, None] // H == jnp.arange(G, dtype=jnp.int32)[None, :]).astype(jnp.float32)
    keep_rows = jnp.dot(select, keep.astype(jnp.float32), precision=lax.Precision.HIGHEST)
    attend = jax.checkpoint(pair_attention)
    attended_bands, pull_spatial = jax.vjp(
        partial(spatial_attention, keep_rows=keep_rows, attend=attend), banded
    )
    attended = lax.all_to_all(attended_bands, "grid", split_axis=0, concat_axis=1, tiled=True)
    mixed, pull_group = jax.vjp(
        partial(block_group, w_so=full_so, w_gqkv=full_gqkv, w_go=full_go), tokens, attended
    )
    grad_direct, grad_attended = pull_group(cotangent)
    grad_bands = lax.all_to_all(grad_attended, "grid", split_axis=1, concat_axis=0, tiled=True)
    (grad_banded,) = pull_spatial(grad_bands)
    grad_stacked = lax.all_to_all(grad_banded, "grid", split_axis=1, concat_axis=2, tiled=True)
    (grad_first,) = pull_first(grad_stacked)
    return (mixed, grad_direct + grad_first)


def nt(a, b):
    return lax.dot_general(a, b, (((1,), (1,)), ((), ())), preferred_element_type=jnp.float32)


def tn(a, b):
    return lax.dot_general(a, b, (((0,), (0,)), ((), ())), preferred_element_type=jnp.float32)


def nn(a, b):
    return jnp.dot(a, b, preferred_element_type=jnp.float32)


def inverse_rms(wide):
    return lax.rsqrt(jnp.mean(wide * wide, axis=-1, keepdims=True) + 1e-06)


def norm_grad(wide, inverse, grad):
    inner = jnp.mean(grad * wide, axis=-1, keepdims=True)
    return grad * inverse - wide * (inverse * inverse * inverse * inner)


def head_pair(values, low):
    zero = jnp.zeros_like(values)
    return jnp.concatenate([jnp.where(low, values, zero), jnp.where(low, zero, values)], axis=0)


def join_pair(stacked, low):
    rows = stacked.shape[0] // 2
    return jnp.where(low, stacked[:rows], stacked[rows:])


def halves(values):
    width = values.shape[1] // 2
    first = jnp.sum(values[:, :width], axis=-1, keepdims=True)
    second = jnp.sum(values[:, width:], axis=-1, keepdims=True)
    rows = values.shape[0]
    return jnp.concatenate(
        [jnp.broadcast_to(first, (rows, width)), jnp.broadcast_to(second, (rows, width))], axis=1
    )


def low_lanes(rows):
    return lax.broadcasted_iota(jnp.int32, (rows, 128), 1) < 64


def pair_forward(qkv, allowed, low, width, pair):
    query = qkv[:, pair * 128 : pair * 128 + 128]
    keyed = head_pair(qkv[:, width + pair * 128 : width + pair * 128 + 128], low)
    valued = head_pair(qkv[:, 2 * width + pair * 128 : 2 * width + pair * 128 + 128], low)
    weights = jnp.where(allowed, jnp.exp(nt(query, keyed) * 0.125), 0.0)
    probs = weights / halves(weights)
    result = nn(probs.astype(jnp.bfloat16), valued).astype(jnp.bfloat16)
    return probs, result


def pair_backward(qkv, probs, grad, low, width, pair):
    query = qkv[:, pair * 128 : pair * 128 + 128]
    keyed = head_pair(qkv[:, width + pair * 128 : width + pair * 128 + 128], low)
    valued = head_pair(qkv[:, 2 * width + pair * 128 : 2 * width + pair * 128 + 128], low)
    grad_probs = nt(grad, valued).astype(jnp.bfloat16).astype(jnp.float32)
    grad_scores = probs * (grad_probs - halves(grad_probs * probs))
    grad_scores = (grad_scores * 0.125).astype(jnp.bfloat16)
    grad_value = join_pair(tn(probs.astype(jnp.bfloat16), grad), low).astype(jnp.bfloat16)
    grad_query = nn(grad_scores, keyed).astype(jnp.bfloat16)
    grad_key = join_pair(tn(grad_scores, query), low).astype(jnp.bfloat16)
    return grad_query, grad_key, grad_value


def place_rows(refs, plan, first, buffer, sem):
    position = lax.axis_index("grid")
    size = lax.axis_size("grid")
    each = buffer.shape[0] // size
    core = lax.rem(position, 2)
    for ref, (from_sibling, blocks) in zip(refs, plan):
        side = 1 - core if from_sibling else core
        holder = position + 1 - 2 * core if from_sibling else position
        flips = (0, 2 * (side + 1), 4 - 2 * side, 6)
        for at, (step, flip) in enumerate(blocks):
            shard = lax.rem((holder ^ flips[flip]) + (size - 8 * step), size)
            pltpu.make_async_copy(
                ref.at[pl.ds(at * each, each), pl.ds(first, buffer.shape[1])],
                buffer.at[pl.ds(pl.multiple_of(shard * each, each), each)],
                sem,
            ).start()


def wait_rows(buffer, sem):
    pltpu.make_async_copy(buffer, buffer, sem).wait()


def packed_row(row, half, patches, groups, by_band):
    band, patch = (row // patches, row % patches) if by_band else (row % groups, row // groups)
    return (band * 2 + half) * patches + patch


def unpack(packed, patches, groups, by_band):
    rows = packed.shape[0] // 2
    row = lax.broadcasted_iota(jnp.int32, (rows, 2 * rows), 0)
    there = lax.broadcasted_iota(jnp.int32, (rows, 2 * rows), 1)
    parts = []
    for half in range(2):
        chosen = (there == packed_row(row, half, patches, groups, by_band)).astype(jnp.bfloat16)
        parts.append(nn(chosen, packed))
    return jnp.concatenate(parts, axis=1).astype(jnp.bfloat16)


def pack(values, patches, groups, by_band):
    rows, width = values.shape
    row = lax.broadcasted_iota(jnp.int32, (2 * rows, rows), 1)
    there = lax.broadcasted_iota(jnp.int32, (2 * rows, rows), 0)
    total = 0.0
    for half in range(2):
        chosen = (there == packed_row(row, half, patches, groups, by_band)).astype(jnp.bfloat16)
        total += nn(chosen, values[:, half * (width // 2) : (half + 1) * (width // 2)])
    return total.astype(jnp.bfloat16)


def prepare(patches, groups, tokens, w_so, w_gqkv, w_go, packed, joined, first_two):
    packed[...] = pack(tokens[...], patches, groups, False)
    width = w_so.shape[1]
    joined[:, :width] = w_so[...]
    joined[:, width : 4 * width] = w_gqkv[...]
    joined[:, 4 * width :] = w_go[...]
    first_two[:, :width] = w_so[...]
    first_two[:, width:] = w_gqkv[...]


def add_packed(patches, groups, values, packed, total):
    total[...] = values[...] + unpack(packed[...], patches, groups, False)


def spatial_forward(plan, patches, groups, packed, keep, *refs):
    pieces, (result_out, qkv_out, probs_out, qkv_buf, sems) = refs[:-5], refs[-5:]
    rows, width = packed.shape[0] // 2, packed.shape[1] * 2
    span = 2 * rows
    place_rows(pieces, plan, 0, qkv_buf, sems.at[0])
    wide = unpack(packed[...], patches, groups, True).astype(jnp.float32)
    normed = (wide * inverse_rms(wide)).astype(jnp.bfloat16)
    kept = keep[pl.ds(lax.axis_index("grid"), 1), :]
    allowed = jnp.concatenate([kept, kept], axis=1) > 0
    low = low_lanes(rows)
    wait_rows(qkv_buf, sems.at[0])
    qkv_out[...] = nn(normed, qkv_buf[...]).astype(jnp.bfloat16)
    results = []
    for pair in range(width // 128):
        probs, result = pair_forward(qkv_out, allowed, low, width, pair)
        probs_out[:, pair * span : pair * span + span] = probs
        results.append(result)
    result_out[...] = pack(jnp.concatenate(results, axis=1), patches, groups, True)


def spatial_backward(plan, patches, groups, packed, grad_packed, qkv, probs, *refs):
    pieces, (grad_out, qkv_buf, grads, sems) = refs[:-4], refs[-4:]
    rows, width = packed.shape[0] // 2, packed.shape[1] * 2
    span = 2 * rows
    place_rows(pieces, plan, 0, qkv_buf, sems.at[0])
    low = low_lanes(rows)
    grad = unpack(grad_packed[...], patches, groups, True)
    for pair in range(width // 128):
        at = pair * 128
        parts = pair_backward(
            qkv, probs[:, pair * span : pair * span + span], grad[:, at : at + 128], low, width, pair
        )
        for which, part in enumerate(parts):
            grads[:, which * width + at : which * width + at + 128] = part
    wide = unpack(packed[...], patches, groups, True).astype(jnp.float32)
    inverse = inverse_rms(wide)
    wait_rows(qkv_buf, sems.at[0])
    grad_normed = nt(grads[...], qkv_buf[...]).astype(jnp.bfloat16).astype(jnp.float32)
    grad_out[...] = pack(norm_grad(wide, inverse, grad_normed).astype(jnp.bfloat16), patches, groups, True)


def group_layer(patches, own_plan, plan, go_plan, tokens, attended, cotangent, *refs):
    pieces, rest = refs[:-11], refs[-11:]
    mixed, grad_y, grad_bands, so_buf, qkv_buf, go_buf, qkv, grads, probs_buf, y_buf, sems = rest
    rows, width = tokens.shape
    groups = rows // patches
    span = 2 * rows
    own, pieces, out = pieces[:2], pieces[2:-4], pieces[-4:]
    place_rows(own, own_plan, 0, so_buf, sems.at[0])
    place_rows(pieces, plan, 0, so_buf, sems.at[0])
    place_rows(own, own_plan, width, qkv_buf, sems.at[1])
    place_rows(pieces, plan, width, qkv_buf, sems.at[1])
    place_rows(own, own_plan, 4 * width, go_buf, sems.at[2])
    place_rows(out, go_plan, 0, go_buf, sems.at[2])
    ordered = unpack(attended[...], patches, groups, False)
    low = low_lanes(rows)
    row_patch = lax.broadcasted_iota(jnp.int32, (rows, span), 0) // groups
    column_patch = (lax.broadcasted_iota(jnp.int32, (rows, span), 1) % rows) // groups
    allowed = row_patch == column_patch
    wait_rows(so_buf, sems.at[0])
    y_first = (tokens[...].astype(jnp.float32) + nn(ordered, so_buf[...])).astype(jnp.bfloat16)
    wide = y_first.astype(jnp.float32)
    y_buf[...] = wide
    inverse = inverse_rms(wide)
    normed = (wide * inverse).astype(jnp.bfloat16)
    wait_rows(qkv_buf, sems.at[1])
    qkv[...] = nn(normed, qkv_buf[...]).astype(jnp.bfloat16)
    results = []
    for pair in range(width // 128):
        probs, result = pair_forward(qkv, allowed, low, width, pair)
        probs_buf[:, pair * span : pair * span + span] = probs
        results.append(result)
    wait_rows(go_buf, sems.at[2])
    mixed[...] = (y_buf[...] + nn(jnp.concatenate(results, axis=1), go_buf[...])).astype(jnp.bfloat16)
    grad_attended = nt(cotangent[...], go_buf[...]).astype(jnp.bfloat16)
    for pair in range(width // 128):
        at = pair * 128
        parts = pair_backward(
            qkv, probs_buf[:, pair * span : pair * span + span], grad_attended[:, at : at + 128], low, width, pair
        )
        for which, part in enumerate(parts):
            grads[:, which * width + at : which * width + at + 128] = part
    grad_normed = nt(grads[...], qkv_buf[...]).astype(jnp.bfloat16).astype(jnp.float32)
    through = norm_grad(y_buf[...], inverse, grad_normed).astype(jnp.bfloat16)
    total = cotangent[...] + through
    grad_y[...] = total
    spread = nt(total, so_buf[...]).astype(jnp.bfloat16)
    grad_bands[...] = pack(spread, patches, groups, False)


VMEM_SPEC = pl.BlockSpec(memory_space=pltpu.VMEM)
ANY_SPEC = pl.BlockSpec(memory_space=pltpu.HBM)
PARAMS = pltpu.CompilerParams(vmem_limit_bytes=56 * 1024 * 1024)


def shape(rows, columns, dtype=jnp.bfloat16):
    return jax.ShapeDtypeStruct((rows, columns), dtype)


def cost(rows, width, passes):
    return pl.CostEstimate(
        flops=passes * 8 * rows * width * width, bytes_accessed=8 * width * width, transcendentals=16 * rows * rows
    )


def exchange(packed):
    size = lax.axis_size("grid")
    rows, columns = packed.shape
    blocks = packed.reshape(size, rows // size, columns)
    return lax.all_to_all(blocks, "grid", split_axis=0, concat_axis=0, tiled=True).reshape(rows, columns)


def mesh_moves(size):
    everyone = range(size)
    first = [(i, i ^ (2 if i % 2 == 0 else 4)) for i in everyone]
    second = [(i, i ^ (4 if i % 2 == 0 else 2)) for i in everyone]
    sibling = [(i, i ^ 1) for i in everyone]
    along = [[(i, (i + 8 * step) % size) for i in everyone] for step in range(1, size // 8)]
    return first, second, sibling, along


def move(values, table):
    return lax.ppermute(values, "grid", table)


def together(*values):
    return lax.optimization_barrier(values)


def stack(*values):
    return jnp.concatenate(values, axis=0)


def plans(size):
    steps = range(size // 8)
    line = [[(step, flip) for step in steps] for flip in range(4)]
    own, rest = [(0, flip) for flip in range(4)], [[(step, flip) for step in steps[1:]] for flip in range(4)]
    out = [(step, flip) for step in steps[1:] for flip in range(4)]

    def plan(held, across):
        return [(False, blocks) for blocks in held] + [(True, blocks) for blocks in across]

    return (
        plan(line, [line[0], line[1] + line[2], line[3]]),
        plan([own], [own]),
        plan([rest[0] + rest[1] + rest[2], rest[3]], [rest[0] + rest[1] + rest[2], rest[3]]),
        plan([out[:-4], out[-4:]], [out[:-4], out[-4:]]),
    )


def banded_layer(tokens, cotangent, w_sqkv, w_so, w_gqkv, w_go, keep):
    patches, groups, width = tokens.shape
    rows = patches * groups
    all_patches = patches * lax.axis_size("grid")
    first, second, sibling, along = mesh_moves(lax.axis_size("grid"))
    spatial_plan, *group_plans = plans(lax.axis_size("grid"))
    pairs = width // 128
    packed_shape = shape(2 * rows, width // 2)

    tokens = tokens.reshape(rows, width)
    packed, own, group = pl.pallas_call(
        partial(prepare, patches, groups),
        out_shape=(packed_shape, shape(w_so.shape[0], 5 * width), shape(w_so.shape[0], 4 * width)),
        in_specs=[VMEM_SPEC] * 4,
        out_specs=(VMEM_SPEC,) * 3,
        name="prepare",
    )(tokens, w_so, w_gqkv, w_go)
    spatial_line = [w_sqkv] + [move(w_sqkv, table) for table in along]
    own_one, own_other = move(own, first), move(own, second)
    spatial_line, own_one, own_other, banded, group = together(
        stack(*spatial_line), own_one, own_other, exchange(packed), group
    )
    spatial_one, spatial_other = move(spatial_line, first), move(spatial_line, second)
    group_parts = [move(group, table) for table in along[:-1]]
    own_both = move(own_one, second)
    spatial_one, spatial_other, own_plane, group, spatial_line, *group_parts = together(
        spatial_one, spatial_other, stack(own, own_one, own_other, own_both), group, spatial_line, *group_parts
    )
    out_plane = own_plane[:, 4 * width :]
    spatial_both = move(spatial_one, second)
    spatial_line_x = move(spatial_line, sibling)
    spatial_pair_x = move(stack(spatial_one, spatial_other), sibling)
    group_parts.append(move(group, along[-1]))
    spatial_both, spatial_line_x, spatial_pair_x, group_line, out_plane = together(
        spatial_both, spatial_line_x, spatial_pair_x, stack(*group_parts), out_plane
    )
    group_one, group_other = move(group_line, first), move(group_line, second)
    out_parts = [move(out_plane, table) for table in along[:-1]]
    spatial_rows = [spatial_line, spatial_one, spatial_other, spatial_both]
    spatial_rows += [spatial_line_x, spatial_pair_x, move(spatial_both, sibling)]
    attended, qkv, probs = pl.pallas_call(
        partial(spatial_forward, spatial_plan, patches, groups),
        out_shape=(
            packed_shape,
            shape(all_patches, 3 * width),
            shape(all_patches, 2 * pairs * all_patches, jnp.float32),
        ),
        in_specs=[VMEM_SPEC] * 2 + [ANY_SPEC] * len(spatial_rows),
        out_specs=(VMEM_SPEC,) * 3,
        scratch_shapes=[pltpu.VMEM((width, 3 * width), jnp.bfloat16), pltpu.SemaphoreType.DMA((1,))],
        compiler_params=PARAMS,
        cost_estimate=cost(all_patches, width, 1),
        name="spatial_forward",
    )(banded, keep, *spatial_rows)
    group_one, group_other, attended, own_plane, group_line, out_plane, *out_parts = together(
        group_one, group_other, attended, own_plane, group_line, out_plane, *out_parts
    )
    group_both = move(group_one, second)
    out_last = move(out_plane, along[-1])
    group_most, out_most = stack(group_line, group_one, group_other), stack(*out_parts)
    group_both, attended, own_plane_x, group_most_x, out_last, out_most_x = together(
        group_both,
        exchange(attended),
        move(own_plane, sibling),
        move(group_most, sibling),
        out_last,
        move(out_most, sibling),
    )
    group_rows = [own_plane, own_plane_x, group_most, group_both, group_most_x, move(group_both, sibling)]
    group_rows += [out_most, out_last, out_most_x, move(out_last, sibling)]
    mixed, grad_y, grad_bands = pl.pallas_call(
        partial(group_layer, patches, *group_plans),
        out_shape=(shape(rows, width), shape(rows, width), packed_shape),
        in_specs=[VMEM_SPEC] * 3 + [ANY_SPEC] * len(group_rows),
        out_specs=(VMEM_SPEC,) * 3,
        scratch_shapes=[
            pltpu.VMEM((width, width), jnp.bfloat16),
            pltpu.VMEM((width, 3 * width), jnp.bfloat16),
            pltpu.VMEM((width, width), jnp.bfloat16),
            pltpu.VMEM((rows, 3 * width), jnp.bfloat16),
            pltpu.VMEM((rows, 3 * width), jnp.bfloat16),
            pltpu.VMEM((rows, 2 * pairs * rows), jnp.float32),
            pltpu.VMEM((rows, width), jnp.float32),
            pltpu.SemaphoreType.DMA((3,)),
        ],
        compiler_params=PARAMS,
        cost_estimate=cost(rows, width, 2),
        name="group_layer",
    )(tokens, attended, cotangent.reshape(rows, width), *group_rows)
    grad_first = pl.pallas_call(
        partial(spatial_backward, spatial_plan, patches, groups),
        out_shape=packed_shape,
        in_specs=[VMEM_SPEC] * 4 + [ANY_SPEC] * len(spatial_rows),
        out_specs=VMEM_SPEC,
        scratch_shapes=[
            pltpu.VMEM((width, 3 * width), jnp.bfloat16),
            pltpu.VMEM((all_patches, 3 * width), jnp.bfloat16),
            pltpu.SemaphoreType.DMA((1,)),
        ],
        compiler_params=PARAMS,
        cost_estimate=cost(all_patches, width, 1),
        name="spatial_backward",
    )(banded, exchange(grad_bands), qkv, probs, *spatial_rows)
    token_grad = pl.pallas_call(
        partial(add_packed, patches, groups),
        out_shape=shape(rows, width),
        in_specs=[VMEM_SPEC] * 2,
        out_specs=VMEM_SPEC,
        name="add_packed",
    )(grad_y, exchange(grad_first))
    whole = (patches, groups, width)
    return (mixed.reshape(whole), token_grad.reshape(whole))


def local(tokens, cotangent, w_sqkv, w_so, w_gqkv, w_go, keep):
    patches, groups, width = tokens.shape
    size = lax.axis_size("grid")
    fits = size == groups and size % 8 == 0 and width % (16 * size) == 0 and width == 64 * H and patches * groups % 128 == 0 and 2 * patches % 8 == 0
    layer = banded_layer if fits else general_layer
    return layer(tokens, cotangent, w_sqkv, w_so, w_gqkv, w_go, keep)


def solution(mesh):
    placed = (
        P(("parts", "grid"), None, None),
        P(("parts", "grid"), None, None),
        P("grid", None),
        P("grid", None),
        P("grid", None),
        P("grid", None),
        P(None, "parts"),
    )
    return jax.shard_map(
        local,
        mesh=mesh,
        in_specs=placed,
        out_specs=(P(("parts", "grid"), None, None), P(("parts", "grid"), None, None)),
        check_vma=False,
    )
```

```python
from functools import partial

import jax
import jax.numpy as jnp
from jax import lax
from jax.experimental import pallas as pl
from jax.experimental.pallas import tpu as pltpu
from jax.sharding import PartitionSpec as P

H = 16
G = 32


def rms_normalize(values):
    wide = values.astype(jnp.float32)
    meansq = jnp.mean(wide * wide, axis=-1, keepdims=True)
    return (wide * lax.rsqrt(meansq + 1e-06)).astype(jnp.bfloat16)


def project_spatial(tokens, weight):
    patches, groups, width = tokens.shape
    normed = rms_normalize(tokens).reshape(patches * groups, width)
    stacked = jnp.dot(normed, weight, preferred_element_type=jnp.float32).astype(jnp.bfloat16)
    stacked = stacked.reshape(patches, groups, 3, width).transpose(2, 0, 1, 3)
    return stacked.reshape(3, patches, groups * width)


def pair_attention(operands):
    stacked, keep_row = operands
    query, keyed, valued = (stacked[0], stacked[1], stacked[2])
    scale = query.shape[-1] ** (-0.5)
    scores = jnp.dot(query, keyed.T, preferred_element_type=jnp.float32) * scale
    weights = jnp.exp(scores) * keep_row[None, :]
    probs = (weights / jnp.sum(weights, axis=-1, keepdims=True)).astype(jnp.bfloat16)
    return jnp.dot(probs, valued, preferred_element_type=jnp.float32).astype(jnp.bfloat16)


def spatial_attention(stacked, keep_rows, attend):
    three, patches, columns = stacked.shape
    pairs = keep_rows.shape[0]
    split = stacked.reshape(3, patches, pairs, columns // pairs).transpose(2, 0, 1, 3)
    result = lax.map(attend, (split, keep_rows))
    return result.transpose(1, 0, 2).reshape(patches, columns)


def block_group(tokens, attended, w_so, w_gqkv, w_go):
    patches, groups, width = tokens.shape
    rows = patches * groups
    heads = H
    y_first = (
        tokens.reshape(rows, width).astype(jnp.float32)
        + jnp.dot(attended.reshape(rows, width), w_so, preferred_element_type=jnp.float32)
    ).astype(jnp.bfloat16)
    normed = rms_normalize(y_first)
    stacked = jnp.dot(normed, w_gqkv, preferred_element_type=jnp.float32).astype(jnp.bfloat16)
    stacked = stacked.reshape(patches, groups, 3, heads, width // heads)
    query = stacked[:, :, 0].astype(jnp.float32)
    keyed = stacked[:, :, 1].astype(jnp.float32)
    valued = stacked[:, :, 2].astype(jnp.float32)
    scale = (width // heads) ** (-0.5)
    scores = jnp.einsum("pgne,pkne->pngk", query, keyed) * scale
    weights = jnp.exp(scores)
    probs = (weights / jnp.sum(weights, axis=-1, keepdims=True)).astype(jnp.bfloat16)
    result = jnp.einsum("pngk,pkne->pgne", probs.astype(jnp.float32), valued).astype(jnp.bfloat16)
    result = result.reshape(rows, width)
    mixed = (
        y_first.astype(jnp.float32) + jnp.dot(result, w_go, preferred_element_type=jnp.float32)
    ).astype(jnp.bfloat16)
    return mixed.reshape(patches, groups, width)


def general_layer(tokens, cotangent, w_sqkv, w_so, w_gqkv, w_go, keep):
    grid_size = lax.axis_size("grid")
    position = lax.axis_index("grid")
    full_sqkv, full_so, full_gqkv, full_go = (
        lax.all_gather(w_sqkv, "grid", axis=0, tiled=True),
        lax.all_gather(w_so, "grid", axis=0, tiled=True),
        lax.all_gather(w_gqkv, "grid", axis=0, tiled=True),
        lax.all_gather(w_go, "grid", axis=0, tiled=True),
    )
    stacked, pull_first = jax.vjp(partial(project_spatial, weight=full_sqkv), tokens)
    banded = lax.all_to_all(stacked, "grid", split_axis=2, concat_axis=1, tiled=True)
    pairs = G * H // grid_size
    pair_ids = position * pairs + jnp.arange(pairs, dtype=jnp.int32)
    select = (pair_ids[:, None] // H == jnp.arange(G, dtype=jnp.int32)[None, :]).astype(jnp.float32)
    keep_rows = jnp.dot(select, keep.astype(jnp.float32), precision=lax.Precision.HIGHEST)
    attend = jax.checkpoint(pair_attention)
    attended_bands, pull_spatial = jax.vjp(
        partial(spatial_attention, keep_rows=keep_rows, attend=attend), banded
    )
    attended = lax.all_to_all(attended_bands, "grid", split_axis=0, concat_axis=1, tiled=True)
    mixed, pull_group = jax.vjp(
        partial(block_group, w_so=full_so, w_gqkv=full_gqkv, w_go=full_go), tokens, attended
    )
    grad_direct, grad_attended = pull_group(cotangent)
    grad_bands = lax.all_to_all(grad_attended, "grid", split_axis=1, concat_axis=0, tiled=True)
    (grad_banded,) = pull_spatial(grad_bands)
    grad_stacked = lax.all_to_all(grad_banded, "grid", split_axis=1, concat_axis=2, tiled=True)
    (grad_first,) = pull_first(grad_stacked)
    return (mixed, grad_direct + grad_first)


def nt(a, b):
    return lax.dot_general(a, b, (((1,), (1,)), ((), ())), preferred_element_type=jnp.float32)


def tn(a, b):
    return lax.dot_general(a, b, (((0,), (0,)), ((), ())), preferred_element_type=jnp.float32)


def nn(a, b):
    return jnp.dot(a, b, preferred_element_type=jnp.float32)


def inverse_rms(wide):
    return lax.rsqrt(jnp.mean(wide * wide, axis=-1, keepdims=True) + 1e-06)


def norm_grad(wide, inverse, grad):
    inner = jnp.mean(grad * wide, axis=-1, keepdims=True)
    return grad * inverse - wide * (inverse * inverse * inverse * inner)


def head_pair(values, low):
    zero = jnp.zeros_like(values)
    return jnp.concatenate([jnp.where(low, values, zero), jnp.where(low, zero, values)], axis=0)


def join_pair(stacked, low):
    rows = stacked.shape[0] // 2
    return jnp.where(low, stacked[:rows], stacked[rows:])


def halves(values):
    width = values.shape[1] // 2
    first = jnp.sum(values[:, :width], axis=-1, keepdims=True)
    second = jnp.sum(values[:, width:], axis=-1, keepdims=True)
    rows = values.shape[0]
    return jnp.concatenate(
        [jnp.broadcast_to(first, (rows, width)), jnp.broadcast_to(second, (rows, width))], axis=1
    )


def low_lanes(rows):
    return lax.broadcasted_iota(jnp.int32, (rows, 128), 1) < 64


def pair_forward(qkv, allowed, low, width, pair):
    query = qkv[:, pair * 128 : pair * 128 + 128]
    keyed = head_pair(qkv[:, width + pair * 128 : width + pair * 128 + 128], low)
    valued = head_pair(qkv[:, 2 * width + pair * 128 : 2 * width + pair * 128 + 128], low)
    weights = jnp.where(allowed, jnp.exp(nt(query, keyed) * 0.125), 0.0)
    probs = weights / halves(weights)
    result = nn(probs.astype(jnp.bfloat16), valued).astype(jnp.bfloat16)
    return probs, result


def pair_backward(qkv, probs, grad, low, width, pair):
    query = qkv[:, pair * 128 : pair * 128 + 128]
    keyed = head_pair(qkv[:, width + pair * 128 : width + pair * 128 + 128], low)
    valued = head_pair(qkv[:, 2 * width + pair * 128 : 2 * width + pair * 128 + 128], low)
    grad_probs = nt(grad, valued).astype(jnp.bfloat16).astype(jnp.float32)
    grad_scores = probs * (grad_probs - halves(grad_probs * probs))
    grad_scores = (grad_scores * 0.125).astype(jnp.bfloat16)
    grad_value = join_pair(tn(probs.astype(jnp.bfloat16), grad), low).astype(jnp.bfloat16)
    grad_query = nn(grad_scores, keyed).astype(jnp.bfloat16)
    grad_key = join_pair(tn(grad_scores, query), low).astype(jnp.bfloat16)
    return grad_query, grad_key, grad_value


def place_rows(refs, plan, first, buffer):
    position = lax.axis_index("grid")
    size = lax.axis_size("grid")
    each = buffer.shape[0] // size
    core = lax.rem(position, 2)
    for ref, (from_sibling, blocks) in zip(refs, plan):
        side = 1 - core if from_sibling else core
        holder = position + 1 - 2 * core if from_sibling else position
        flips = (0, 2 * (side + 1), 4 - 2 * side, 6)
        for at, (step, flip) in enumerate(blocks):
            shard = lax.rem((holder ^ flips[flip]) + (size - 8 * step), size)
            rows = pl.ds(pl.multiple_of(shard * each, each), each)
            buffer[rows, :] = ref[at * each : at * each + each, first : first + buffer.shape[1]]


def packed_row(row, half, patches, groups, by_band):
    band, patch = (row // patches, row % patches) if by_band else (row % groups, row // groups)
    return (band * 2 + half) * patches + patch


def unpack(packed, patches, groups, by_band):
    rows = packed.shape[0] // 2
    row = lax.broadcasted_iota(jnp.int32, (rows, 2 * rows), 0)
    there = lax.broadcasted_iota(jnp.int32, (rows, 2 * rows), 1)
    parts = []
    for half in range(2):
        chosen = (there == packed_row(row, half, patches, groups, by_band)).astype(jnp.bfloat16)
        parts.append(nn(chosen, packed))
    return jnp.concatenate(parts, axis=1).astype(jnp.bfloat16)


def pack(values, patches, groups, by_band):
    rows, width = values.shape
    row = lax.broadcasted_iota(jnp.int32, (2 * rows, rows), 1)
    there = lax.broadcasted_iota(jnp.int32, (2 * rows, rows), 0)
    total = 0.0
    for half in range(2):
        chosen = (there == packed_row(row, half, patches, groups, by_band)).astype(jnp.bfloat16)
        total += nn(chosen, values[:, half * (width // 2) : (half + 1) * (width // 2)])
    return total.astype(jnp.bfloat16)


def prepare(patches, groups, tokens, w_so, w_gqkv, w_go, packed, joined):
    packed[...] = pack(tokens[...], patches, groups, False)
    width = w_so.shape[1]
    joined[:, :width] = w_so[...]
    joined[:, width : 4 * width] = w_gqkv[...]
    joined[:, 4 * width :] = w_go[...]


def add_packed(patches, groups, values, packed, total):
    total[...] = values[...] + unpack(packed[...], patches, groups, False)


def spatial_forward(plan, patches, groups, packed, keep, *refs):
    pieces, (result_out, qkv_out, probs_out, qkv_buf) = refs[:-4], refs[-4:]
    rows, width = packed.shape[0] // 2, packed.shape[1] * 2
    span = 2 * rows
    place_rows(pieces, plan, 0, qkv_buf)
    wide = unpack(packed[...], patches, groups, True).astype(jnp.float32)
    normed = (wide * inverse_rms(wide)).astype(jnp.bfloat16)
    kept = keep[pl.ds(lax.axis_index("grid"), 1), :]
    allowed = jnp.concatenate([kept, kept], axis=1) > 0
    low = low_lanes(rows)
    qkv_out[...] = nn(normed, qkv_buf[...]).astype(jnp.bfloat16)
    results = []
    for pair in range(width // 128):
        probs, result = pair_forward(qkv_out, allowed, low, width, pair)
        probs_out[:, pair * span : pair * span + span] = probs
        results.append(result)
    result_out[...] = pack(jnp.concatenate(results, axis=1), patches, groups, True)


def spatial_backward(plan, patches, groups, packed, grad_packed, qkv, probs, *refs):
    pieces, (grad_out, qkv_buf, grads) = refs[:-3], refs[-3:]
    rows, width = packed.shape[0] // 2, packed.shape[1] * 2
    span = 2 * rows
    place_rows(pieces, plan, 0, qkv_buf)
    low = low_lanes(rows)
    grad = unpack(grad_packed[...], patches, groups, True)
    for pair in range(width // 128):
        at = pair * 128
        parts = pair_backward(
            qkv, probs[:, pair * span : pair * span + span], grad[:, at : at + 128], low, width, pair
        )
        for which, part in enumerate(parts):
            grads[:, which * width + at : which * width + at + 128] = part
    wide = unpack(packed[...], patches, groups, True).astype(jnp.float32)
    inverse = inverse_rms(wide)
    grad_normed = nt(grads[...], qkv_buf[...]).astype(jnp.bfloat16).astype(jnp.float32)
    grad_out[...] = pack(norm_grad(wide, inverse, grad_normed).astype(jnp.bfloat16), patches, groups, True)


def group_layer(patches, plan, tokens, attended, cotangent, *refs):
    pieces, rest = refs[:-10], refs[-10:]
    mixed, grad_y, grad_bands, so_buf, qkv_buf, go_buf, qkv, grads, probs_buf, y_buf = rest
    rows, width = tokens.shape
    groups = rows // patches
    span = 2 * rows
    place_rows(pieces, plan, 0, so_buf)
    place_rows(pieces, plan, width, qkv_buf)
    place_rows(pieces, plan, 4 * width, go_buf)
    ordered = unpack(attended[...], patches, groups, False)
    low = low_lanes(rows)
    row_patch = lax.broadcasted_iota(jnp.int32, (rows, span), 0) // groups
    column_patch = (lax.broadcasted_iota(jnp.int32, (rows, span), 1) % rows) // groups
    allowed = row_patch == column_patch
    y_first = (tokens[...].astype(jnp.float32) + nn(ordered, so_buf[...])).astype(jnp.bfloat16)
    wide = y_first.astype(jnp.float32)
    y_buf[...] = wide
    inverse = inverse_rms(wide)
    normed = (wide * inverse).astype(jnp.bfloat16)
    qkv[...] = nn(normed, qkv_buf[...]).astype(jnp.bfloat16)
    results = []
    for pair in range(width // 128):
        probs, result = pair_forward(qkv, allowed, low, width, pair)
        probs_buf[:, pair * span : pair * span + span] = probs
        results.append(result)
    mixed[...] = (y_buf[...] + nn(jnp.concatenate(results, axis=1), go_buf[...])).astype(jnp.bfloat16)
    grad_attended = nt(cotangent[...], go_buf[...]).astype(jnp.bfloat16)
    for pair in range(width // 128):
        at = pair * 128
        parts = pair_backward(
            qkv, probs_buf[:, pair * span : pair * span + span], grad_attended[:, at : at + 128], low, width, pair
        )
        for which, part in enumerate(parts):
            grads[:, which * width + at : which * width + at + 128] = part
    grad_normed = nt(grads[...], qkv_buf[...]).astype(jnp.bfloat16).astype(jnp.float32)
    through = norm_grad(y_buf[...], inverse, grad_normed).astype(jnp.bfloat16)
    total = cotangent[...] + through
    grad_y[...] = total
    spread = nt(total, so_buf[...]).astype(jnp.bfloat16)
    grad_bands[...] = pack(spread, patches, groups, False)


VMEM_SPEC = pl.BlockSpec(memory_space=pltpu.VMEM)


def room(mebibytes):
    return pltpu.CompilerParams(vmem_limit_bytes=mebibytes * 1024 * 1024)


def shape(rows, columns, dtype=jnp.bfloat16):
    return jax.ShapeDtypeStruct((rows, columns), dtype)


def cost(rows, width, weights, passes):
    return pl.CostEstimate(
        flops=2 * passes * weights * rows * width * width,
        bytes_accessed=2 * passes * weights * width * width + 16 * rows * width,
        transcendentals=16 * rows * rows,
    )


def exchange(packed):
    size = lax.axis_size("grid")
    rows, columns = packed.shape
    blocks = packed.reshape(size, rows // size, columns)
    return lax.all_to_all(blocks, "grid", split_axis=0, concat_axis=0, tiled=True).reshape(rows, columns)


def mesh_moves(size):
    everyone = range(size)
    first = [(i, i ^ (2 if i % 2 == 0 else 4)) for i in everyone]
    second = [(i, i ^ (4 if i % 2 == 0 else 2)) for i in everyone]
    sibling = [(i, i ^ 1) for i in everyone]
    along = [[(i, (i + 8 * step) % size) for i in everyone] for step in range(1, size // 8)]
    return first, second, sibling, along


def move(values, table):
    return lax.ppermute(values, "grid", table)


def together(*values):
    return lax.optimization_barrier(values)


def stack(*values):
    return jnp.concatenate(values, axis=0)


def plans(size):
    steps = range(size // 8)
    line = [[(step, flip) for step in steps] for flip in range(4)]
    own, rest = [(0, flip) for flip in range(4)], [blocks[1:] for blocks in line]

    def both_cores(held):
        return [(False, blocks) for blocks in held] + [(True, blocks) for blocks in held]

    return both_cores(line), both_cores([own] + rest)


def banded_layer(tokens, cotangent, w_sqkv, w_so, w_gqkv, w_go, keep):
    patches, groups, width = tokens.shape
    rows = patches * groups
    all_patches = patches * lax.axis_size("grid")
    first, second, sibling, along = mesh_moves(lax.axis_size("grid"))
    spatial_plan, group_plan = plans(lax.axis_size("grid"))
    pairs = width // 128
    packed_shape = shape(2 * rows, width // 2)

    tokens = tokens.reshape(rows, width)
    packed, group = pl.pallas_call(
        partial(prepare, patches, groups),
        out_shape=(packed_shape, shape(w_so.shape[0], 5 * width)),
        in_specs=[VMEM_SPEC] * 4,
        out_specs=(VMEM_SPEC,) * 2,
        name="prepare",
    )(tokens, w_so, w_gqkv, w_go)
    spatial_line = [w_sqkv] + [move(w_sqkv, table) for table in along]
    group_one, group_other = move(group, first), move(group, second)
    spatial_line, group_one, group_other, banded, group = together(
        stack(*spatial_line), group_one, group_other, exchange(packed), group
    )
    spatial_one, spatial_other = move(spatial_line, first), move(spatial_line, second)
    group_both = move(group_one, second)
    group_parts = [move(group, table) for table in along[:-1]]
    spatial_one, spatial_other, group_plane, group, spatial_line, *group_parts = together(
        spatial_one, spatial_other, stack(group, group_one, group_other, group_both), group, spatial_line, *group_parts
    )
    spatial_both = move(spatial_one, second)
    spatial_across = [move(part, sibling) for part in (spatial_line, spatial_one, spatial_other)]
    group_parts.append(move(group, along[-1]))
    spatial_both, group_line, group_plane, *spatial_across = together(
        spatial_both, stack(*group_parts), group_plane, *spatial_across
    )
    group_one, group_other = move(group_line, first), move(group_line, second)
    group_across = [move(group_plane, sibling), move(group_line, sibling)]
    spatial_rows = [spatial_line, spatial_one, spatial_other, spatial_both]
    spatial_rows += [*spatial_across, move(spatial_both, sibling)]
    attended, qkv, probs = pl.pallas_call(
        partial(spatial_forward, spatial_plan, patches, groups),
        out_shape=(
            packed_shape,
            shape(all_patches, 3 * width),
            shape(all_patches, 2 * pairs * all_patches, jnp.float32),
        ),
        in_specs=[VMEM_SPEC] * (2 + len(spatial_rows)),
        out_specs=(VMEM_SPEC,) * 3,
        scratch_shapes=[pltpu.VMEM((width, 3 * width), jnp.bfloat16)],
        compiler_params=room(18),
        cost_estimate=cost(all_patches, width, 3, 1),
        name="spatial_forward",
    )(banded, keep, *spatial_rows)
    group_one, group_other, attended, *group_across = together(group_one, group_other, attended, *group_across)
    group_both = move(group_one, second)
    group_across += [move(group_one, sibling), move(group_other, sibling)]
    group_both, attended, *group_across = together(group_both, exchange(attended), *group_across)
    group_rows = [group_plane, group_line, group_one, group_other, group_both]
    group_rows += [*group_across, move(group_both, sibling)]
    mixed, grad_y, grad_bands = pl.pallas_call(
        partial(group_layer, patches, group_plan),
        out_shape=(shape(rows, width), shape(rows, width), packed_shape),
        in_specs=[VMEM_SPEC] * (3 + len(group_rows)),
        out_specs=(VMEM_SPEC,) * 3,
        scratch_shapes=[
            pltpu.VMEM((width, width), jnp.bfloat16),
            pltpu.VMEM((width, 3 * width), jnp.bfloat16),
            pltpu.VMEM((width, width), jnp.bfloat16),
            pltpu.VMEM((rows, 3 * width), jnp.bfloat16),
            pltpu.VMEM((rows, 3 * width), jnp.bfloat16),
            pltpu.VMEM((rows, 2 * pairs * rows), jnp.float32),
            pltpu.VMEM((rows, width), jnp.float32),
        ],
        compiler_params=room(32),
        cost_estimate=cost(rows, width, 5, 2),
        name="group_layer",
    )(tokens, attended, cotangent.reshape(rows, width), *group_rows)
    grad_first = pl.pallas_call(
        partial(spatial_backward, spatial_plan, patches, groups),
        out_shape=packed_shape,
        in_specs=[VMEM_SPEC] * (4 + len(spatial_rows)),
        out_specs=VMEM_SPEC,
        scratch_shapes=[
            pltpu.VMEM((width, 3 * width), jnp.bfloat16),
            pltpu.VMEM((all_patches, 3 * width), jnp.bfloat16),
        ],
        compiler_params=room(18),
        cost_estimate=cost(all_patches, width, 3, 1),
        name="spatial_backward",
    )(banded, exchange(grad_bands), qkv, probs, *spatial_rows)
    token_grad = pl.pallas_call(
        partial(add_packed, patches, groups),
        out_shape=shape(rows, width),
        in_specs=[VMEM_SPEC] * 2,
        out_specs=VMEM_SPEC,
        compiler_params=room(8),
        name="add_packed",
    )(grad_y, exchange(grad_first))
    whole = (patches, groups, width)
    return (mixed.reshape(whole), token_grad.reshape(whole))


def local(tokens, cotangent, w_sqkv, w_so, w_gqkv, w_go, keep):
    patches, groups, width = tokens.shape
    size = lax.axis_size("grid")
    fits = size == groups and size % 8 == 0 and width % (16 * size) == 0 and width == 64 * H and patches * groups % 128 == 0 and 2 * patches % 8 == 0
    layer = banded_layer if fits else general_layer
    return layer(tokens, cotangent, w_sqkv, w_so, w_gqkv, w_go, keep)


def solution(mesh):
    placed = (
        P(("parts", "grid"), None, None),
        P(("parts", "grid"), None, None),
        P("grid", None),
        P("grid", None),
        P("grid", None),
        P("grid", None),
        P(None, "parts"),
    )
    return jax.shard_map(
        local,
        mesh=mesh,
        in_specs=placed,
        out_specs=(P(("parts", "grid"), None, None), P(("parts", "grid"), None, None)),
        check_vma=False,
    )
```

```python
from functools import partial

import jax
import jax.numpy as jnp
from jax import lax
from jax.experimental import pallas as pl
from jax.experimental.pallas import tpu as pltpu
from jax.sharding import PartitionSpec as P

H = 16
G = 32


def rms_normalize(values):
    wide = values.astype(jnp.float32)
    meansq = jnp.mean(wide * wide, axis=-1, keepdims=True)
    return (wide * lax.rsqrt(meansq + 1e-06)).astype(jnp.bfloat16)


def project_spatial(tokens, weight):
    patches, groups, width = tokens.shape
    normed = rms_normalize(tokens).reshape(patches * groups, width)
    stacked = jnp.dot(normed, weight, preferred_element_type=jnp.float32).astype(jnp.bfloat16)
    stacked = stacked.reshape(patches, groups, 3, width).transpose(2, 0, 1, 3)
    return stacked.reshape(3, patches, groups * width)


def pair_attention(operands):
    stacked, keep_row = operands
    query, keyed, valued = (stacked[0], stacked[1], stacked[2])
    scale = query.shape[-1] ** (-0.5)
    scores = jnp.dot(query, keyed.T, preferred_element_type=jnp.float32) * scale
    weights = jnp.exp(scores) * keep_row[None, :]
    probs = (weights / jnp.sum(weights, axis=-1, keepdims=True)).astype(jnp.bfloat16)
    return jnp.dot(probs, valued, preferred_element_type=jnp.float32).astype(jnp.bfloat16)


def spatial_attention(stacked, keep_rows, attend):
    three, patches, columns = stacked.shape
    pairs = keep_rows.shape[0]
    split = stacked.reshape(3, patches, pairs, columns // pairs).transpose(2, 0, 1, 3)
    result = lax.map(attend, (split, keep_rows))
    return result.transpose(1, 0, 2).reshape(patches, columns)


def block_group(tokens, attended, w_so, w_gqkv, w_go):
    patches, groups, width = tokens.shape
    rows = patches * groups
    heads = H
    y_first = (
        tokens.reshape(rows, width).astype(jnp.float32)
        + jnp.dot(attended.reshape(rows, width), w_so, preferred_element_type=jnp.float32)
    ).astype(jnp.bfloat16)
    normed = rms_normalize(y_first)
    stacked = jnp.dot(normed, w_gqkv, preferred_element_type=jnp.float32).astype(jnp.bfloat16)
    stacked = stacked.reshape(patches, groups, 3, heads, width // heads)
    query = stacked[:, :, 0].astype(jnp.float32)
    keyed = stacked[:, :, 1].astype(jnp.float32)
    valued = stacked[:, :, 2].astype(jnp.float32)
    scale = (width // heads) ** (-0.5)
    scores = jnp.einsum("pgne,pkne->pngk", query, keyed) * scale
    weights = jnp.exp(scores)
    probs = (weights / jnp.sum(weights, axis=-1, keepdims=True)).astype(jnp.bfloat16)
    result = jnp.einsum("pngk,pkne->pgne", probs.astype(jnp.float32), valued).astype(jnp.bfloat16)
    result = result.reshape(rows, width)
    mixed = (
        y_first.astype(jnp.float32) + jnp.dot(result, w_go, preferred_element_type=jnp.float32)
    ).astype(jnp.bfloat16)
    return mixed.reshape(patches, groups, width)


def general_layer(tokens, cotangent, w_sqkv, w_so, w_gqkv, w_go, keep):
    grid_size = lax.axis_size("grid")
    position = lax.axis_index("grid")
    full_sqkv, full_so, full_gqkv, full_go = (
        lax.all_gather(w_sqkv, "grid", axis=0, tiled=True),
        lax.all_gather(w_so, "grid", axis=0, tiled=True),
        lax.all_gather(w_gqkv, "grid", axis=0, tiled=True),
        lax.all_gather(w_go, "grid", axis=0, tiled=True),
    )
    stacked, pull_first = jax.vjp(partial(project_spatial, weight=full_sqkv), tokens)
    banded = lax.all_to_all(stacked, "grid", split_axis=2, concat_axis=1, tiled=True)
    pairs = G * H // grid_size
    pair_ids = position * pairs + jnp.arange(pairs, dtype=jnp.int32)
    select = (pair_ids[:, None] // H == jnp.arange(G, dtype=jnp.int32)[None, :]).astype(jnp.float32)
    keep_rows = jnp.dot(select, keep.astype(jnp.float32), precision=lax.Precision.HIGHEST)
    attend = jax.checkpoint(pair_attention)
    attended_bands, pull_spatial = jax.vjp(
        partial(spatial_attention, keep_rows=keep_rows, attend=attend), banded
    )
    attended = lax.all_to_all(attended_bands, "grid", split_axis=0, concat_axis=1, tiled=True)
    mixed, pull_group = jax.vjp(
        partial(block_group, w_so=full_so, w_gqkv=full_gqkv, w_go=full_go), tokens, attended
    )
    grad_direct, grad_attended = pull_group(cotangent)
    grad_bands = lax.all_to_all(grad_attended, "grid", split_axis=1, concat_axis=0, tiled=True)
    (grad_banded,) = pull_spatial(grad_bands)
    grad_stacked = lax.all_to_all(grad_banded, "grid", split_axis=1, concat_axis=2, tiled=True)
    (grad_first,) = pull_first(grad_stacked)
    return (mixed, grad_direct + grad_first)


def nt(a, b):
    return lax.dot_general(a, b, (((1,), (1,)), ((), ())), preferred_element_type=jnp.float32)


def tn(a, b):
    return lax.dot_general(a, b, (((0,), (0,)), ((), ())), preferred_element_type=jnp.float32)


def nn(a, b):
    return jnp.dot(a, b, preferred_element_type=jnp.float32)


def inverse_rms(wide):
    return lax.rsqrt(jnp.mean(wide * wide, axis=-1, keepdims=True) + 1e-06)


def norm_grad(wide, inverse, grad):
    inner = jnp.mean(grad * wide, axis=-1, keepdims=True)
    return grad * inverse - wide * (inverse * inverse * inverse * inner)


def head_pair(values, low):
    zero = jnp.zeros_like(values)
    return jnp.concatenate([jnp.where(low, values, zero), jnp.where(low, zero, values)], axis=0)


def join_pair(stacked, low):
    rows = stacked.shape[0] // 2
    return jnp.where(low, stacked[:rows], stacked[rows:])


def low_lanes(rows):
    return lax.broadcasted_iota(jnp.int32, (rows, 128), 1) < 64


def columns(which, pair, width):
    return slice(which * width + pair * 128, which * width + pair * 128 + 128)


def attention_forward(qkv, allowed, probs):
    rows, width = qkv.shape[0], qkv.shape[1] // 3
    span, pairs, low = 2 * rows, width // 128, low_lanes(rows)
    for pair in range(pairs):
        keyed = head_pair(qkv[:, columns(1, pair, width)], low)
        probs[:, pair * span : pair * span + span] = nt(qkv[:, columns(0, pair, width)], keyed)
    for head in range(2 * pairs):
        at = slice(head * rows, head * rows + rows)
        weights = jnp.where(allowed, jnp.exp(probs[:, at] * 0.125), 0.0)
        probs[:, at] = weights * (1.0 / jnp.sum(weights, axis=-1, keepdims=True))
    results = []
    for pair in range(pairs):
        valued = head_pair(qkv[:, columns(2, pair, width)], low)
        results.append(nn(probs[:, pair * span : pair * span + span].astype(jnp.bfloat16), valued).astype(jnp.bfloat16))
    return jnp.concatenate(results, axis=1)


def attention_backward(qkv, probs, grad, grad_probs, grad_scores, grads):
    rows, width = qkv.shape[0], qkv.shape[1] // 3
    span, pairs, low = 2 * rows, width // 128, low_lanes(rows)
    for pair in range(pairs):
        valued = head_pair(qkv[:, columns(2, pair, width)], low)
        part = nt(grad[:, columns(0, pair, width)], valued)
        grad_probs[:, pair * span : pair * span + span] = part.astype(jnp.bfloat16)
    for head in range(2 * pairs):
        at = slice(head * rows, head * rows + rows)
        share, part = probs[:, at], grad_probs[:, at].astype(jnp.float32)
        inner = jnp.sum(part * share, axis=-1, keepdims=True)
        grad_scores[:, at] = (share * (part - inner) * 0.125).astype(jnp.bfloat16)
    for pair in range(pairs):
        at = slice(pair * span, pair * span + span)
        keyed = head_pair(qkv[:, columns(1, pair, width)], low)
        query, part = qkv[:, columns(0, pair, width)], grad[:, columns(0, pair, width)]
        scored = grad_scores[:, at]
        grads[:, columns(0, pair, width)] = nn(scored, keyed).astype(jnp.bfloat16)
        grads[:, columns(1, pair, width)] = join_pair(tn(scored, query), low).astype(jnp.bfloat16)
        shares = probs[:, at].astype(jnp.bfloat16)
        grads[:, columns(2, pair, width)] = join_pair(tn(shares, part), low).astype(jnp.bfloat16)


def place_rows(refs, plan, first, buffer):
    position = lax.axis_index("grid")
    size = lax.axis_size("grid")
    each = buffer.shape[0] // size
    core = lax.rem(position, 2)
    for ref, (from_sibling, blocks) in zip(refs, plan):
        side = 1 - core if from_sibling else core
        holder = position + 1 - 2 * core if from_sibling else position
        flips = (0, 2 * (side + 1), 4 - 2 * side, 6)
        for at, (step, flip) in enumerate(blocks):
            shard = lax.rem((holder ^ flips[flip]) + (size - 8 * step), size)
            rows = pl.ds(pl.multiple_of(shard * each, each), each)
            buffer[rows, :] = ref[at * each : at * each + each, first : first + buffer.shape[1]]


def packed_row(row, half, patches, groups, by_band):
    band, patch = (row // patches, row % patches) if by_band else (row % groups, row // groups)
    return (band * 2 + half) * patches + patch


def unpack(packed, patches, groups, by_band):
    rows = packed.shape[0] // 2
    row = lax.broadcasted_iota(jnp.int32, (rows, 2 * rows), 0)
    there = lax.broadcasted_iota(jnp.int32, (rows, 2 * rows), 1)
    parts = []
    for half in range(2):
        chosen = (there == packed_row(row, half, patches, groups, by_band)).astype(jnp.bfloat16)
        parts.append(nn(chosen, packed))
    return jnp.concatenate(parts, axis=1).astype(jnp.bfloat16)


def pack(values, patches, groups, by_band):
    rows, width = values.shape
    row = lax.broadcasted_iota(jnp.int32, (2 * rows, rows), 1)
    there = lax.broadcasted_iota(jnp.int32, (2 * rows, rows), 0)
    total = 0.0
    for half in range(2):
        chosen = (there == packed_row(row, half, patches, groups, by_band)).astype(jnp.bfloat16)
        total += nn(chosen, values[:, half * (width // 2) : (half + 1) * (width // 2)])
    return total.astype(jnp.bfloat16)


def prepare(patches, groups, tokens, w_so, w_gqkv, w_go, packed, joined):
    packed[...] = pack(tokens[...], patches, groups, False)
    width = w_so.shape[1]
    joined[:, :width] = w_so[...]
    joined[:, width : 4 * width] = w_gqkv[...]
    joined[:, 4 * width :] = w_go[...]


def add_packed(patches, groups, values, packed, total):
    total[...] = values[...] + unpack(packed[...], patches, groups, False)


def spatial_forward(plan, patches, groups, packed, keep, *refs):
    pieces, (result_out, qkv_out, probs_out, banded_out, weight_out) = refs[:-5], refs[-5:]
    place_rows(pieces, plan, 0, weight_out)
    banded = unpack(packed[...], patches, groups, True)
    banded_out[...] = banded
    wide = banded.astype(jnp.float32)
    normed = (wide * inverse_rms(wide)).astype(jnp.bfloat16)
    allowed = keep[pl.ds(lax.axis_index("grid"), 1), :] > 0
    qkv_out[...] = nn(normed, weight_out[...]).astype(jnp.bfloat16)
    result_out[...] = pack(attention_forward(qkv_out, allowed, probs_out), patches, groups, True)


def spatial_backward(
    patches, groups, grad_packed, banded, qkv, probs, weight, grad_out, grads, grad_probs, grad_scores
):
    grad = unpack(grad_packed[...], patches, groups, True)
    attention_backward(qkv, probs, grad, grad_probs, grad_scores, grads)
    wide = banded[...].astype(jnp.float32)
    inverse = inverse_rms(wide)
    grad_normed = nt(grads[...], weight[...]).astype(jnp.bfloat16).astype(jnp.float32)
    grad_out[...] = pack(norm_grad(wide, inverse, grad_normed).astype(jnp.bfloat16), patches, groups, True)


def group_layer(patches, plan, tokens, attended, cotangent, *refs):
    pieces, rest = refs[:-12], refs[-12:]
    mixed, grad_y, grad_bands, so_buf, qkv_buf, go_buf, qkv, probs, y_buf, grads, grad_probs, grad_scores = rest
    rows, width = tokens.shape
    groups = rows // patches
    place_rows(pieces, plan, 0, so_buf)
    ordered = unpack(attended[...], patches, groups, False)
    y_first = (tokens[...].astype(jnp.float32) + nn(ordered, so_buf[...])).astype(jnp.bfloat16)
    wide = y_first.astype(jnp.float32)
    y_buf[...] = wide
    inverse = inverse_rms(wide)
    normed = (wide * inverse).astype(jnp.bfloat16)
    place_rows(pieces, plan, width, qkv_buf)
    qkv[...] = nn(normed, qkv_buf[...]).astype(jnp.bfloat16)
    place_rows(pieces, plan, 4 * width, go_buf)
    grad_attended = nt(cotangent[...], go_buf[...]).astype(jnp.bfloat16)
    row_patch = lax.broadcasted_iota(jnp.int32, (rows, rows), 0) // groups
    allowed = row_patch == lax.broadcasted_iota(jnp.int32, (rows, rows), 1) // groups
    results = attention_forward(qkv, allowed, probs)
    mixed[...] = (y_buf[...] + nn(results, go_buf[...])).astype(jnp.bfloat16)
    attention_backward(qkv, probs, grad_attended, grad_probs, grad_scores, grads)
    grad_normed = nt(grads[...], qkv_buf[...]).astype(jnp.bfloat16).astype(jnp.float32)
    through = norm_grad(y_buf[...], inverse, grad_normed).astype(jnp.bfloat16)
    total = cotangent[...] + through
    grad_y[...] = total
    spread = nt(total, so_buf[...]).astype(jnp.bfloat16)
    grad_bands[...] = pack(spread, patches, groups, False)


VMEM_SPEC = pl.BlockSpec(memory_space=pltpu.VMEM)


def room(mebibytes):
    return pltpu.CompilerParams(vmem_limit_bytes=mebibytes * 1024 * 1024)


def shape(rows, columns, dtype=jnp.bfloat16):
    return jax.ShapeDtypeStruct((rows, columns), dtype)


def cost(rows, width, weights, passes):
    return pl.CostEstimate(
        flops=2 * passes * weights * rows * width * width,
        bytes_accessed=2 * passes * weights * width * width + 16 * rows * width,
        transcendentals=16 * rows * rows,
    )


def exchange(packed):
    size = lax.axis_size("grid")
    rows, columns = packed.shape
    blocks = packed.reshape(size, rows // size, columns)
    return lax.all_to_all(blocks, "grid", split_axis=0, concat_axis=0, tiled=True).reshape(rows, columns)


def mesh_moves(size):
    everyone = range(size)
    first = [(i, i ^ (2 if i % 2 == 0 else 4)) for i in everyone]
    second = [(i, i ^ (4 if i % 2 == 0 else 2)) for i in everyone]
    sibling = [(i, i ^ 1) for i in everyone]
    along = [[(i, (i + 8 * step) % size) for i in everyone] for step in range(1, size // 8)]
    return first, second, sibling, along


def move(values, table):
    return lax.ppermute(values, "grid", table)


def together(*values):
    return lax.optimization_barrier(values)


def stack(*values):
    return jnp.concatenate(values, axis=0)


def plans(size):
    steps = range(size // 8)
    line = [[(step, flip) for step in steps] for flip in range(4)]
    own, rest = [(0, flip) for flip in range(4)], [blocks[1:] for blocks in line]

    def both_cores(held):
        return [(False, blocks) for blocks in held] + [(True, blocks) for blocks in held]

    return both_cores(line), both_cores([own] + rest)


def banded_layer(tokens, cotangent, w_sqkv, w_so, w_gqkv, w_go, keep):
    patches, groups, width = tokens.shape
    rows = patches * groups
    all_patches = patches * lax.axis_size("grid")
    first, second, sibling, along = mesh_moves(lax.axis_size("grid"))
    spatial_plan, group_plan = plans(lax.axis_size("grid"))
    pairs = width // 128
    packed_shape = shape(2 * rows, width // 2)

    tokens = tokens.reshape(rows, width)
    packed, group = pl.pallas_call(
        partial(prepare, patches, groups),
        out_shape=(packed_shape, shape(w_so.shape[0], 5 * width)),
        in_specs=[VMEM_SPEC] * 4,
        out_specs=(VMEM_SPEC,) * 2,
        name="prepare",
    )(tokens, w_so, w_gqkv, w_go)
    spatial_line = [w_sqkv] + [move(w_sqkv, table) for table in along]
    group_one, group_other = move(group, first), move(group, second)
    spatial_line, group_one, group_other, banded, group = together(
        stack(*spatial_line), group_one, group_other, exchange(packed), group
    )
    spatial_one, spatial_other = move(spatial_line, first), move(spatial_line, second)
    group_both = move(group_one, second)
    group_parts = [move(group, table) for table in along[:-1]]
    spatial_one, spatial_other, group_plane, group, spatial_line, *group_parts = together(
        spatial_one, spatial_other, stack(group, group_one, group_other, group_both), group, spatial_line, *group_parts
    )
    spatial_both = move(spatial_one, second)
    spatial_across = [move(part, sibling) for part in (spatial_line, spatial_one, spatial_other)]
    group_parts.append(move(group, along[-1]))
    spatial_both, group_line, group_plane, *spatial_across = together(
        spatial_both, stack(*group_parts), group_plane, *spatial_across
    )
    group_one, group_other = move(group_line, first), move(group_line, second)
    group_across = [move(group_plane, sibling), move(group_line, sibling)]
    spatial_rows = [spatial_line, spatial_one, spatial_other, spatial_both]
    spatial_rows += [*spatial_across, move(spatial_both, sibling)]
    probs_shape = shape(all_patches, 2 * pairs * all_patches, jnp.float32)
    attended, qkv, probs, banded, full_sqkv = pl.pallas_call(
        partial(spatial_forward, spatial_plan, patches, groups),
        out_shape=(
            packed_shape,
            shape(all_patches, 3 * width),
            probs_shape,
            shape(all_patches, width),
            shape(width, 3 * width),
        ),
        in_specs=[VMEM_SPEC] * (2 + len(spatial_rows)),
        out_specs=(VMEM_SPEC,) * 5,
        compiler_params=room(18),
        cost_estimate=cost(all_patches, width, 3, 1),
        name="spatial_forward",
    )(banded, keep, *spatial_rows)
    group_one, group_other, attended, *group_across = together(group_one, group_other, attended, *group_across)
    group_both = move(group_one, second)
    group_across += [move(group_one, sibling), move(group_other, sibling)]
    group_both, attended, *group_across = together(group_both, exchange(attended), *group_across)
    group_rows = [group_plane, group_line, group_one, group_other, group_both]
    group_rows += [*group_across, move(group_both, sibling)]
    heads_wide = 2 * pairs * rows
    mixed, grad_y, grad_bands = pl.pallas_call(
        partial(group_layer, patches, group_plan),
        out_shape=(shape(rows, width), shape(rows, width), packed_shape),
        in_specs=[VMEM_SPEC] * (3 + len(group_rows)),
        out_specs=(VMEM_SPEC,) * 3,
        scratch_shapes=[
            pltpu.VMEM((width, width), jnp.bfloat16),
            pltpu.VMEM((width, 3 * width), jnp.bfloat16),
            pltpu.VMEM((width, width), jnp.bfloat16),
            pltpu.VMEM((rows, 3 * width), jnp.bfloat16),
            pltpu.VMEM((rows, heads_wide), jnp.float32),
            pltpu.VMEM((rows, width), jnp.float32),
            pltpu.VMEM((rows, 3 * width), jnp.bfloat16),
            pltpu.VMEM((rows, heads_wide), jnp.bfloat16),
            pltpu.VMEM((rows, heads_wide), jnp.bfloat16),
        ],
        compiler_params=room(32),
        cost_estimate=cost(rows, width, 5, 2),
        name="group_layer",
    )(tokens, attended, cotangent.reshape(rows, width), *group_rows)
    heads_wide = 2 * pairs * all_patches
    grad_first = pl.pallas_call(
        partial(spatial_backward, patches, groups),
        out_shape=packed_shape,
        in_specs=[VMEM_SPEC] * 5,
        out_specs=VMEM_SPEC,
        scratch_shapes=[
            pltpu.VMEM((all_patches, 3 * width), jnp.bfloat16),
            pltpu.VMEM((all_patches, heads_wide), jnp.bfloat16),
            pltpu.VMEM((all_patches, heads_wide), jnp.bfloat16),
        ],
        compiler_params=room(18),
        cost_estimate=cost(all_patches, width, 3, 1),
        name="spatial_backward",
    )(exchange(grad_bands), banded, qkv, probs, full_sqkv)
    token_grad = pl.pallas_call(
        partial(add_packed, patches, groups),
        out_shape=shape(rows, width),
        in_specs=[VMEM_SPEC] * 2,
        out_specs=VMEM_SPEC,
        compiler_params=room(8),
        name="add_packed",
    )(grad_y, exchange(grad_first))
    whole = (patches, groups, width)
    return (mixed.reshape(whole), token_grad.reshape(whole))


def local(tokens, cotangent, w_sqkv, w_so, w_gqkv, w_go, keep):
    patches, groups, width = tokens.shape
    size = lax.axis_size("grid")
    fits = size == groups and size % 8 == 0 and width % (16 * size) == 0 and width == 64 * H and patches * groups % 128 == 0 and 2 * patches % 8 == 0
    layer = banded_layer if fits else general_layer
    return layer(tokens, cotangent, w_sqkv, w_so, w_gqkv, w_go, keep)


def solution(mesh):
    placed = (
        P(("parts", "grid"), None, None),
        P(("parts", "grid"), None, None),
        P("grid", None),
        P("grid", None),
        P("grid", None),
        P("grid", None),
        P(None, "parts"),
    )
    return jax.shard_map(
        local,
        mesh=mesh,
        in_specs=placed,
        out_specs=(P(("parts", "grid"), None, None), P(("parts", "grid"), None, None)),
        check_vma=False,
    )
```

```python
from functools import partial

import jax
import jax.numpy as jnp
from jax import lax
from jax.experimental import pallas as pl
from jax.experimental.pallas import tpu as pltpu
from jax.sharding import PartitionSpec as P

H = 16
G = 32


def rms_normalize(values):
    wide = values.astype(jnp.float32)
    meansq = jnp.mean(wide * wide, axis=-1, keepdims=True)
    return (wide * lax.rsqrt(meansq + 1e-06)).astype(jnp.bfloat16)


def project_spatial(tokens, weight):
    patches, groups, width = tokens.shape
    normed = rms_normalize(tokens).reshape(patches * groups, width)
    stacked = jnp.dot(normed, weight, preferred_element_type=jnp.float32).astype(jnp.bfloat16)
    stacked = stacked.reshape(patches, groups, 3, width).transpose(2, 0, 1, 3)
    return stacked.reshape(3, patches, groups * width)


def pair_attention(operands):
    stacked, keep_row = operands
    query, keyed, valued = (stacked[0], stacked[1], stacked[2])
    scale = query.shape[-1] ** (-0.5)
    scores = jnp.dot(query, keyed.T, preferred_element_type=jnp.float32) * scale
    weights = jnp.exp(scores) * keep_row[None, :]
    probs = (weights / jnp.sum(weights, axis=-1, keepdims=True)).astype(jnp.bfloat16)
    return jnp.dot(probs, valued, preferred_element_type=jnp.float32).astype(jnp.bfloat16)


def spatial_attention(stacked, keep_rows, attend):
    three, patches, columns = stacked.shape
    pairs = keep_rows.shape[0]
    split = stacked.reshape(3, patches, pairs, columns // pairs).transpose(2, 0, 1, 3)
    result = lax.map(attend, (split, keep_rows))
    return result.transpose(1, 0, 2).reshape(patches, columns)


def block_group(tokens, attended, w_so, w_gqkv, w_go):
    patches, groups, width = tokens.shape
    rows = patches * groups
    heads = H
    y_first = (
        tokens.reshape(rows, width).astype(jnp.float32)
        + jnp.dot(attended.reshape(rows, width), w_so, preferred_element_type=jnp.float32)
    ).astype(jnp.bfloat16)
    normed = rms_normalize(y_first)
    stacked = jnp.dot(normed, w_gqkv, preferred_element_type=jnp.float32).astype(jnp.bfloat16)
    stacked = stacked.reshape(patches, groups, 3, heads, width // heads)
    query = stacked[:, :, 0].astype(jnp.float32)
    keyed = stacked[:, :, 1].astype(jnp.float32)
    valued = stacked[:, :, 2].astype(jnp.float32)
    scale = (width // heads) ** (-0.5)
    scores = jnp.einsum("pgne,pkne->pngk", query, keyed) * scale
    weights = jnp.exp(scores)
    probs = (weights / jnp.sum(weights, axis=-1, keepdims=True)).astype(jnp.bfloat16)
    result = jnp.einsum("pngk,pkne->pgne", probs.astype(jnp.float32), valued).astype(jnp.bfloat16)
    result = result.reshape(rows, width)
    mixed = (
        y_first.astype(jnp.float32) + jnp.dot(result, w_go, preferred_element_type=jnp.float32)
    ).astype(jnp.bfloat16)
    return mixed.reshape(patches, groups, width)


def general_layer(tokens, cotangent, w_sqkv, w_so, w_gqkv, w_go, keep):
    grid_size = lax.axis_size("grid")
    position = lax.axis_index("grid")
    full_sqkv, full_so, full_gqkv, full_go = (
        lax.all_gather(w_sqkv, "grid", axis=0, tiled=True),
        lax.all_gather(w_so, "grid", axis=0, tiled=True),
        lax.all_gather(w_gqkv, "grid", axis=0, tiled=True),
        lax.all_gather(w_go, "grid", axis=0, tiled=True),
    )
    stacked, pull_first = jax.vjp(partial(project_spatial, weight=full_sqkv), tokens)
    banded = lax.all_to_all(stacked, "grid", split_axis=2, concat_axis=1, tiled=True)
    pairs = G * H // grid_size
    pair_ids = position * pairs + jnp.arange(pairs, dtype=jnp.int32)
    select = (pair_ids[:, None] // H == jnp.arange(G, dtype=jnp.int32)[None, :]).astype(jnp.float32)
    keep_rows = jnp.dot(select, keep.astype(jnp.float32), precision=lax.Precision.HIGHEST)
    attend = jax.checkpoint(pair_attention)
    attended_bands, pull_spatial = jax.vjp(
        partial(spatial_attention, keep_rows=keep_rows, attend=attend), banded
    )
    attended = lax.all_to_all(attended_bands, "grid", split_axis=0, concat_axis=1, tiled=True)
    mixed, pull_group = jax.vjp(
        partial(block_group, w_so=full_so, w_gqkv=full_gqkv, w_go=full_go), tokens, attended
    )
    grad_direct, grad_attended = pull_group(cotangent)
    grad_bands = lax.all_to_all(grad_attended, "grid", split_axis=1, concat_axis=0, tiled=True)
    (grad_banded,) = pull_spatial(grad_bands)
    grad_stacked = lax.all_to_all(grad_banded, "grid", split_axis=1, concat_axis=2, tiled=True)
    (grad_first,) = pull_first(grad_stacked)
    return (mixed, grad_direct + grad_first)


def nt(a, b):
    return lax.dot_general(a, b, (((1,), (1,)), ((), ())), preferred_element_type=jnp.float32)


def tn(a, b):
    return lax.dot_general(a, b, (((0,), (0,)), ((), ())), preferred_element_type=jnp.float32)


def nn(a, b):
    return jnp.dot(a, b, preferred_element_type=jnp.float32)


def inverse_rms(wide):
    return lax.rsqrt(jnp.mean(wide * wide, axis=-1, keepdims=True) + 1e-06)


def norm_grad(wide, inverse, grad):
    inner = jnp.mean(grad * wide, axis=-1, keepdims=True)
    return grad * inverse - wide * (inverse * inverse * inverse * inner)


def head_pair(values, low):
    zero = jnp.zeros_like(values)
    return jnp.concatenate([jnp.where(low, values, zero), jnp.where(low, zero, values)], axis=0)


def join_pair(stacked, low):
    rows = stacked.shape[0] // 2
    return jnp.where(low, stacked[:rows], stacked[rows:])


def low_lanes(rows):
    return lax.broadcasted_iota(jnp.int32, (rows, 128), 1) < 64


def columns(which, pair, width):
    return slice(which * width + pair * 128, which * width + pair * 128 + 128)


def attention_forward(qkv, allowed, probs):
    rows, width = qkv.shape[0], qkv.shape[1] // 3
    span, pairs, low = 2 * rows, width // 128, low_lanes(rows)
    for pair in range(pairs):
        keyed = head_pair(qkv[:, columns(1, pair, width)], low)
        probs[:, pair * span : pair * span + span] = nt(qkv[:, columns(0, pair, width)], keyed)
    for head in range(2 * pairs):
        at = slice(head * rows, head * rows + rows)
        weights = jnp.where(allowed, jnp.exp(probs[:, at] * 0.125), 0.0)
        probs[:, at] = weights * (1.0 / jnp.sum(weights, axis=-1, keepdims=True))
    results = []
    for pair in range(pairs):
        valued = head_pair(qkv[:, columns(2, pair, width)], low)
        results.append(nn(probs[:, pair * span : pair * span + span].astype(jnp.bfloat16), valued).astype(jnp.bfloat16))
    return jnp.concatenate(results, axis=1)


def attention_backward(qkv, probs, grad, grad_probs, grad_scores, grads):
    rows, width = qkv.shape[0], qkv.shape[1] // 3
    span, pairs, low = 2 * rows, width // 128, low_lanes(rows)
    for pair in range(pairs):
        valued = head_pair(qkv[:, columns(2, pair, width)], low)
        part = nt(grad[:, columns(0, pair, width)], valued)
        grad_probs[:, pair * span : pair * span + span] = part.astype(jnp.bfloat16)
    for head in range(2 * pairs):
        at = slice(head * rows, head * rows + rows)
        share, part = probs[:, at], grad_probs[:, at].astype(jnp.float32)
        inner = jnp.sum(part * share, axis=-1, keepdims=True)
        grad_scores[:, at] = (share * (part - inner) * 0.125).astype(jnp.bfloat16)
    for pair in range(pairs):
        at = slice(pair * span, pair * span + span)
        keyed = head_pair(qkv[:, columns(1, pair, width)], low)
        query, part = qkv[:, columns(0, pair, width)], grad[:, columns(0, pair, width)]
        scored = grad_scores[:, at]
        grads[:, columns(0, pair, width)] = nn(scored, keyed).astype(jnp.bfloat16)
        grads[:, columns(1, pair, width)] = join_pair(tn(scored, query), low).astype(jnp.bfloat16)
        shares = probs[:, at].astype(jnp.bfloat16)
        grads[:, columns(2, pair, width)] = join_pair(tn(shares, part), low).astype(jnp.bfloat16)


def place_rows(refs, plan, first, buffer):
    position = lax.axis_index("grid")
    size = lax.axis_size("grid")
    each = buffer.shape[0] // size
    core = lax.rem(position, 2)
    for ref, (from_sibling, blocks) in zip(refs, plan):
        side = 1 - core if from_sibling else core
        holder = position + 1 - 2 * core if from_sibling else position
        flips = (0, 2 * (side + 1), 4 - 2 * side, 6)
        for at, (step, flip) in enumerate(blocks):
            shard = lax.rem((holder ^ flips[flip]) + (size - 8 * step), size)
            rows = pl.ds(pl.multiple_of(shard * each, each), each)
            buffer[rows, :] = ref[at * each : at * each + each, first : first + buffer.shape[1]]


def packed_row(row, half, patches, groups, by_band):
    band, patch = (row // patches, row % patches) if by_band else (row % groups, row // groups)
    return (band * 2 + half) * patches + patch


def unpack(packed, patches, groups, by_band):
    rows = packed.shape[0] // 2
    row = lax.broadcasted_iota(jnp.int32, (rows, 2 * rows), 0)
    there = lax.broadcasted_iota(jnp.int32, (rows, 2 * rows), 1)
    parts = []
    for half in range(2):
        chosen = (there == packed_row(row, half, patches, groups, by_band)).astype(jnp.bfloat16)
        parts.append(nn(chosen, packed))
    return jnp.concatenate(parts, axis=1).astype(jnp.bfloat16)


def pack(values, patches, groups, by_band):
    rows, width = values.shape
    row = lax.broadcasted_iota(jnp.int32, (2 * rows, rows), 1)
    there = lax.broadcasted_iota(jnp.int32, (2 * rows, rows), 0)
    total = 0.0
    for half in range(2):
        chosen = (there == packed_row(row, half, patches, groups, by_band)).astype(jnp.bfloat16)
        total += nn(chosen, values[:, half * (width // 2) : (half + 1) * (width // 2)])
    return total.astype(jnp.bfloat16)


def prepare(patches, groups, tokens, w_so, w_gqkv, w_go, packed, joined):
    packed[...] = pack(tokens[...], patches, groups, False)
    width = w_so.shape[1]
    joined[:, :width] = w_so[...]
    joined[:, width : 4 * width] = w_gqkv[...]
    joined[:, 4 * width :] = w_go[...]


def add_packed(patches, groups, values, packed, total):
    total[...] = values[...] + unpack(packed[...], patches, groups, False)


def spatial_forward(plan, patches, groups, packed, keep, *refs):
    pieces, (result_out, qkv_out, probs_out, banded_out, turned_out, weight) = refs[:-6], refs[-6:]
    place_rows(pieces, plan, 0, weight)
    banded = unpack(packed[...], patches, groups, True)
    banded_out[...] = banded
    wide = banded.astype(jnp.float32)
    normed = (wide * inverse_rms(wide)).astype(jnp.bfloat16)
    allowed = keep[pl.ds(lax.axis_index("grid"), 1), :] > 0
    qkv_out[...] = nn(normed, weight[...]).astype(jnp.bfloat16)
    result_out[...] = pack(attention_forward(qkv_out, allowed, probs_out), patches, groups, True)
    turned_out[...] = weight[...].T


def spatial_backward(
    patches, groups, grad_packed, banded, qkv, probs, turned, grad_out, grads, grad_probs, grad_scores
):
    grad = unpack(grad_packed[...], patches, groups, True)
    attention_backward(qkv, probs, grad, grad_probs, grad_scores, grads)
    wide = banded[...].astype(jnp.float32)
    inverse = inverse_rms(wide)
    grad_normed = nn(grads[...], turned[...]).astype(jnp.bfloat16).astype(jnp.float32)
    grad_out[...] = pack(norm_grad(wide, inverse, grad_normed).astype(jnp.bfloat16), patches, groups, True)


def group_layer(patches, plan, tokens, attended, cotangent, *refs):
    pieces, rest = refs[:-12], refs[-12:]
    mixed, grad_y, grad_bands, so_buf, qkv_buf, go_buf, qkv, probs, y_buf, grads, grad_probs, grad_scores = rest
    rows, width = tokens.shape
    groups = rows // patches
    place_rows(pieces, plan, 0, so_buf)
    ordered = unpack(attended[...], patches, groups, False)
    y_first = (tokens[...].astype(jnp.float32) + nn(ordered, so_buf[...])).astype(jnp.bfloat16)
    wide = y_first.astype(jnp.float32)
    y_buf[...] = wide
    inverse = inverse_rms(wide)
    normed = (wide * inverse).astype(jnp.bfloat16)
    place_rows(pieces, plan, width, qkv_buf)
    qkv[...] = nn(normed, qkv_buf[...]).astype(jnp.bfloat16)
    place_rows(pieces, plan, 4 * width, go_buf)
    grad_attended = nt(cotangent[...], go_buf[...]).astype(jnp.bfloat16)
    row_patch = lax.broadcasted_iota(jnp.int32, (rows, rows), 0) // groups
    allowed = row_patch == lax.broadcasted_iota(jnp.int32, (rows, rows), 1) // groups
    results = attention_forward(qkv, allowed, probs)
    mixed[...] = (y_buf[...] + nn(results, go_buf[...])).astype(jnp.bfloat16)
    attention_backward(qkv, probs, grad_attended, grad_probs, grad_scores, grads)
    grad_normed = nt(grads[...], qkv_buf[...]).astype(jnp.bfloat16).astype(jnp.float32)
    through = norm_grad(y_buf[...], inverse, grad_normed).astype(jnp.bfloat16)
    total = cotangent[...] + through
    grad_y[...] = total
    spread = nt(total, so_buf[...]).astype(jnp.bfloat16)
    grad_bands[...] = pack(spread, patches, groups, False)


VMEM_SPEC = pl.BlockSpec(memory_space=pltpu.VMEM)


def room(mebibytes):
    return pltpu.CompilerParams(vmem_limit_bytes=mebibytes * 1024 * 1024)


def shape(rows, columns, dtype=jnp.bfloat16):
    return jax.ShapeDtypeStruct((rows, columns), dtype)


def cost(rows, width, weights, passes):
    return pl.CostEstimate(
        flops=2 * passes * weights * rows * width * width,
        bytes_accessed=2 * passes * weights * width * width + 16 * rows * width,
        transcendentals=16 * rows * rows,
    )


def exchange(packed):
    size = lax.axis_size("grid")
    rows, columns = packed.shape
    blocks = packed.reshape(size, rows // size, columns)
    return lax.all_to_all(blocks, "grid", split_axis=0, concat_axis=0, tiled=True).reshape(rows, columns)


def mesh_moves(size):
    everyone = range(size)
    first = [(i, i ^ (2 if i % 2 == 0 else 4)) for i in everyone]
    second = [(i, i ^ (4 if i % 2 == 0 else 2)) for i in everyone]
    sibling = [(i, i ^ 1) for i in everyone]
    along = [[(i, (i + 8 * step) % size) for i in everyone] for step in range(1, size // 8)]
    return first, second, sibling, along


def move(values, table):
    return lax.ppermute(values, "grid", table)


def together(*values):
    return lax.optimization_barrier(values)


def stack(*values):
    return jnp.concatenate(values, axis=0)


def plans(size):
    steps = range(size // 8)
    line = [[(step, flip) for step in steps] for flip in range(4)]
    own, rest = [(0, flip) for flip in range(4)], [blocks[1:] for blocks in line]

    def both_cores(held):
        return [(False, blocks) for blocks in held] + [(True, blocks) for blocks in held]

    return both_cores(line), both_cores([own] + rest)


def banded_layer(tokens, cotangent, w_sqkv, w_so, w_gqkv, w_go, keep):
    patches, groups, width = tokens.shape
    rows = patches * groups
    all_patches = patches * lax.axis_size("grid")
    first, second, sibling, along = mesh_moves(lax.axis_size("grid"))
    spatial_plan, group_plan = plans(lax.axis_size("grid"))
    pairs = width // 128
    packed_shape = shape(2 * rows, width // 2)

    tokens = tokens.reshape(rows, width)
    packed, group = pl.pallas_call(
        partial(prepare, patches, groups),
        out_shape=(packed_shape, shape(w_so.shape[0], 5 * width)),
        in_specs=[VMEM_SPEC] * 4,
        out_specs=(VMEM_SPEC,) * 2,
        name="prepare",
    )(tokens, w_so, w_gqkv, w_go)
    spatial_line = [w_sqkv] + [move(w_sqkv, table) for table in along]
    group_one, group_other = move(group, first), move(group, second)
    spatial_line, group_one, group_other, packed, group = together(
        stack(*spatial_line), group_one, group_other, packed, group
    )
    spatial_one, spatial_other = move(spatial_line, first), move(spatial_line, second)
    group_both = move(group_one, second)
    group_parts = [move(group, table) for table in along[:-1]]
    spatial_one, spatial_other, group_plane, group, spatial_line, packed, group_part = together(
        spatial_one,
        spatial_other,
        stack(group, group_one, group_other, group_both),
        group,
        spatial_line,
        packed,
        stack(*group_parts),
    )
    spatial_both = move(spatial_one, second)
    spatial_across = [move(part, sibling) for part in (spatial_line, spatial_one, spatial_other)]
    group_line = stack(group_part, move(group, along[-1]))
    spatial_both, group_line, group_plane, banded, *spatial_across = together(
        spatial_both, group_line, group_plane, exchange(packed), *spatial_across
    )
    group_one, group_other = move(group_line, first), move(group_line, second)
    group_across = [move(group_plane, sibling), move(group_line, sibling)]
    spatial_rows = [spatial_line, spatial_one, spatial_other, spatial_both]
    spatial_rows += [*spatial_across, move(spatial_both, sibling)]
    probs_shape = shape(all_patches, 2 * pairs * all_patches, jnp.float32)
    attended, qkv, probs, banded, turned = pl.pallas_call(
        partial(spatial_forward, spatial_plan, patches, groups),
        out_shape=(
            packed_shape,
            shape(all_patches, 3 * width),
            probs_shape,
            shape(all_patches, width),
            shape(3 * width, width),
        ),
        in_specs=[VMEM_SPEC] * (2 + len(spatial_rows)),
        out_specs=(VMEM_SPEC,) * 5,
        scratch_shapes=[pltpu.VMEM((width, 3 * width), jnp.bfloat16)],
        compiler_params=room(28),
        cost_estimate=cost(all_patches, width, 3, 1),
        name="spatial_forward",
    )(banded, keep, *spatial_rows)
    group_one, group_other, attended, *group_across = together(group_one, group_other, attended, *group_across)
    group_both = move(group_one, second)
    group_across += [move(group_one, sibling), move(group_other, sibling)]
    group_both, attended, *group_across = together(group_both, exchange(attended), *group_across)
    group_rows = [group_plane, group_line, group_one, group_other, group_both]
    group_rows += [*group_across, move(group_both, sibling)]
    heads_wide = 2 * pairs * rows
    mixed, grad_y, grad_bands = pl.pallas_call(
        partial(group_layer, patches, group_plan),
        out_shape=(shape(rows, width), shape(rows, width), packed_shape),
        in_specs=[VMEM_SPEC] * (3 + len(group_rows)),
        out_specs=(VMEM_SPEC,) * 3,
        scratch_shapes=[
            pltpu.VMEM((width, width), jnp.bfloat16),
            pltpu.VMEM((width, 3 * width), jnp.bfloat16),
            pltpu.VMEM((width, width), jnp.bfloat16),
            pltpu.VMEM((rows, 3 * width), jnp.bfloat16),
            pltpu.VMEM((rows, heads_wide), jnp.float32),
            pltpu.VMEM((rows, width), jnp.float32),
            pltpu.VMEM((rows, 3 * width), jnp.bfloat16),
            pltpu.VMEM((rows, heads_wide), jnp.bfloat16),
            pltpu.VMEM((rows, heads_wide), jnp.bfloat16),
        ],
        compiler_params=room(32),
        cost_estimate=cost(rows, width, 5, 2),
        name="group_layer",
    )(tokens, attended, cotangent.reshape(rows, width), *group_rows)
    heads_wide = 2 * pairs * all_patches
    grad_first = pl.pallas_call(
        partial(spatial_backward, patches, groups),
        out_shape=packed_shape,
        in_specs=[VMEM_SPEC] * 5,
        out_specs=VMEM_SPEC,
        scratch_shapes=[
            pltpu.VMEM((all_patches, 3 * width), jnp.bfloat16),
            pltpu.VMEM((all_patches, heads_wide), jnp.bfloat16),
            pltpu.VMEM((all_patches, heads_wide), jnp.bfloat16),
        ],
        compiler_params=room(18),
        cost_estimate=cost(all_patches, width, 3, 1),
        name="spatial_backward",
    )(exchange(grad_bands), banded, qkv, probs, turned)
    token_grad = pl.pallas_call(
        partial(add_packed, patches, groups),
        out_shape=shape(rows, width),
        in_specs=[VMEM_SPEC] * 2,
        out_specs=VMEM_SPEC,
        compiler_params=room(8),
        name="add_packed",
    )(grad_y, exchange(grad_first))
    whole = (patches, groups, width)
    return (mixed.reshape(whole), token_grad.reshape(whole))


def local(tokens, cotangent, w_sqkv, w_so, w_gqkv, w_go, keep):
    patches, groups, width = tokens.shape
    size = lax.axis_size("grid")
    fits = size == groups and size % 8 == 0 and width % (16 * size) == 0 and width == 64 * H and patches * groups % 128 == 0 and 2 * patches % 8 == 0
    layer = banded_layer if fits else general_layer
    return layer(tokens, cotangent, w_sqkv, w_so, w_gqkv, w_go, keep)


def solution(mesh):
    placed = (
        P(("parts", "grid"), None, None),
        P(("parts", "grid"), None, None),
        P("grid", None),
        P("grid", None),
        P("grid", None),
        P("grid", None),
        P(None, "parts"),
    )
    return jax.shard_map(
        local,
        mesh=mesh,
        in_specs=placed,
        out_specs=(P(("parts", "grid"), None, None), P(("parts", "grid"), None, None)),
        check_vma=False,
    )
```

```python
from functools import partial

import jax
import jax.numpy as jnp
from jax import lax
from jax.experimental import pallas as pl
from jax.experimental.pallas import tpu as pltpu
from jax.sharding import PartitionSpec as P

H = 16
G = 32


def rms_normalize(values):
    wide = values.astype(jnp.float32)
    meansq = jnp.mean(wide * wide, axis=-1, keepdims=True)
    return (wide * lax.rsqrt(meansq + 1e-06)).astype(jnp.bfloat16)


def project_spatial(tokens, weight):
    patches, groups, width = tokens.shape
    normed = rms_normalize(tokens).reshape(patches * groups, width)
    stacked = jnp.dot(normed, weight, preferred_element_type=jnp.float32).astype(jnp.bfloat16)
    stacked = stacked.reshape(patches, groups, 3, width).transpose(2, 0, 1, 3)
    return stacked.reshape(3, patches, groups * width)


def pair_attention(operands):
    stacked, keep_row = operands
    query, keyed, valued = (stacked[0], stacked[1], stacked[2])
    scale = query.shape[-1] ** (-0.5)
    scores = jnp.dot(query, keyed.T, preferred_element_type=jnp.float32) * scale
    weights = jnp.exp(scores) * keep_row[None, :]
    probs = (weights / jnp.sum(weights, axis=-1, keepdims=True)).astype(jnp.bfloat16)
    return jnp.dot(probs, valued, preferred_element_type=jnp.float32).astype(jnp.bfloat16)


def spatial_attention(stacked, keep_rows, attend):
    three, patches, columns = stacked.shape
    pairs = keep_rows.shape[0]
    split = stacked.reshape(3, patches, pairs, columns // pairs).transpose(2, 0, 1, 3)
    result = lax.map(attend, (split, keep_rows))
    return result.transpose(1, 0, 2).reshape(patches, columns)


def block_group(tokens, attended, w_so, w_gqkv, w_go):
    patches, groups, width = tokens.shape
    rows = patches * groups
    heads = H
    y_first = (
        tokens.reshape(rows, width).astype(jnp.float32)
        + jnp.dot(attended.reshape(rows, width), w_so, preferred_element_type=jnp.float32)
    ).astype(jnp.bfloat16)
    normed = rms_normalize(y_first)
    stacked = jnp.dot(normed, w_gqkv, preferred_element_type=jnp.float32).astype(jnp.bfloat16)
    stacked = stacked.reshape(patches, groups, 3, heads, width // heads)
    query = stacked[:, :, 0].astype(jnp.float32)
    keyed = stacked[:, :, 1].astype(jnp.float32)
    valued = stacked[:, :, 2].astype(jnp.float32)
    scale = (width // heads) ** (-0.5)
    scores = jnp.einsum("pgne,pkne->pngk", query, keyed) * scale
    weights = jnp.exp(scores)
    probs = (weights / jnp.sum(weights, axis=-1, keepdims=True)).astype(jnp.bfloat16)
    result = jnp.einsum("pngk,pkne->pgne", probs.astype(jnp.float32), valued).astype(jnp.bfloat16)
    result = result.reshape(rows, width)
    mixed = (
        y_first.astype(jnp.float32) + jnp.dot(result, w_go, preferred_element_type=jnp.float32)
    ).astype(jnp.bfloat16)
    return mixed.reshape(patches, groups, width)


def general_layer(tokens, cotangent, w_sqkv, w_so, w_gqkv, w_go, keep):
    grid_size = lax.axis_size("grid")
    position = lax.axis_index("grid")
    full_sqkv, full_so, full_gqkv, full_go = (
        lax.all_gather(w_sqkv, "grid", axis=0, tiled=True),
        lax.all_gather(w_so, "grid", axis=0, tiled=True),
        lax.all_gather(w_gqkv, "grid", axis=0, tiled=True),
        lax.all_gather(w_go, "grid", axis=0, tiled=True),
    )
    stacked, pull_first = jax.vjp(partial(project_spatial, weight=full_sqkv), tokens)
    banded = lax.all_to_all(stacked, "grid", split_axis=2, concat_axis=1, tiled=True)
    pairs = G * H // grid_size
    pair_ids = position * pairs + jnp.arange(pairs, dtype=jnp.int32)
    select = (pair_ids[:, None] // H == jnp.arange(G, dtype=jnp.int32)[None, :]).astype(jnp.float32)
    keep_rows = jnp.dot(select, keep.astype(jnp.float32), precision=lax.Precision.HIGHEST)
    attend = jax.checkpoint(pair_attention)
    attended_bands, pull_spatial = jax.vjp(
        partial(spatial_attention, keep_rows=keep_rows, attend=attend), banded
    )
    attended = lax.all_to_all(attended_bands, "grid", split_axis=0, concat_axis=1, tiled=True)
    mixed, pull_group = jax.vjp(
        partial(block_group, w_so=full_so, w_gqkv=full_gqkv, w_go=full_go), tokens, attended
    )
    grad_direct, grad_attended = pull_group(cotangent)
    grad_bands = lax.all_to_all(grad_attended, "grid", split_axis=1, concat_axis=0, tiled=True)
    (grad_banded,) = pull_spatial(grad_bands)
    grad_stacked = lax.all_to_all(grad_banded, "grid", split_axis=1, concat_axis=2, tiled=True)
    (grad_first,) = pull_first(grad_stacked)
    return (mixed, grad_direct + grad_first)


def nt(a, b):
    return lax.dot_general(a, b, (((1,), (1,)), ((), ())), preferred_element_type=jnp.float32)


def tn(a, b):
    return lax.dot_general(a, b, (((0,), (0,)), ((), ())), preferred_element_type=jnp.float32)


def nn(a, b):
    return jnp.dot(a, b, preferred_element_type=jnp.float32)


def inverse_rms(wide):
    return lax.rsqrt(jnp.mean(wide * wide, axis=-1, keepdims=True) + 1e-06)


def norm_grad(wide, inverse, grad):
    inner = jnp.mean(grad * wide, axis=-1, keepdims=True)
    return grad * inverse - wide * (inverse * inverse * inverse * inner)


def head_pair(values, low):
    zero = jnp.zeros_like(values)
    return jnp.concatenate([jnp.where(low, values, zero), jnp.where(low, zero, values)], axis=0)


def join_pair(stacked, low):
    rows = stacked.shape[0] // 2
    return jnp.where(low, stacked[:rows], stacked[rows:])


def low_lanes(rows):
    return lax.broadcasted_iota(jnp.int32, (rows, 128), 1) < 64


def columns(which, pair, width):
    return slice(which * width + pair * 128, which * width + pair * 128 + 128)


def attention_forward(qkv, allowed, probs):
    rows, width = qkv.shape[0], qkv.shape[1] // 3
    span, pairs, low = 2 * rows, width // 128, low_lanes(rows)
    for pair in range(pairs):
        keyed = head_pair(qkv[:, columns(1, pair, width)], low)
        probs[:, pair * span : pair * span + span] = nt(qkv[:, columns(0, pair, width)], keyed)
    for head in range(2 * pairs):
        at = slice(head * rows, head * rows + rows)
        weights = jnp.where(allowed, jnp.exp(probs[:, at] * 0.125), 0.0)
        probs[:, at] = weights * (1.0 / jnp.sum(weights, axis=-1, keepdims=True))
    results = []
    for pair in range(pairs):
        valued = head_pair(qkv[:, columns(2, pair, width)], low)
        results.append(nn(probs[:, pair * span : pair * span + span].astype(jnp.bfloat16), valued).astype(jnp.bfloat16))
    return jnp.concatenate(results, axis=1)


def attention_backward(qkv, probs, grad, grad_probs, grad_scores, grads):
    rows, width = qkv.shape[0], qkv.shape[1] // 3
    span, pairs, low = 2 * rows, width // 128, low_lanes(rows)
    for pair in range(pairs):
        valued = head_pair(qkv[:, columns(2, pair, width)], low)
        part = nt(grad[:, columns(0, pair, width)], valued)
        grad_probs[:, pair * span : pair * span + span] = part.astype(jnp.bfloat16)
    for head in range(2 * pairs):
        at = slice(head * rows, head * rows + rows)
        share, part = probs[:, at], grad_probs[:, at].astype(jnp.float32)
        inner = jnp.sum(part * share, axis=-1, keepdims=True)
        grad_scores[:, at] = (share * (part - inner) * 0.125).astype(jnp.bfloat16)
    for pair in range(pairs):
        at = slice(pair * span, pair * span + span)
        keyed = head_pair(qkv[:, columns(1, pair, width)], low)
        query, part = qkv[:, columns(0, pair, width)], grad[:, columns(0, pair, width)]
        scored = grad_scores[:, at]
        grads[:, columns(0, pair, width)] = nn(scored, keyed).astype(jnp.bfloat16)
        grads[:, columns(1, pair, width)] = join_pair(tn(scored, query), low).astype(jnp.bfloat16)
        shares = probs[:, at].astype(jnp.bfloat16)
        grads[:, columns(2, pair, width)] = join_pair(tn(shares, part), low).astype(jnp.bfloat16)


def place_rows(refs, plan, first, buffer):
    position = lax.axis_index("grid")
    size = lax.axis_size("grid")
    each = buffer.shape[0] // size
    core = lax.rem(position, 2)
    for ref, (from_sibling, blocks) in zip(refs, plan):
        side = 1 - core if from_sibling else core
        holder = position + 1 - 2 * core if from_sibling else position
        flips = (0, 2 * (side + 1), 4 - 2 * side, 6)
        for at, (step, flip) in enumerate(blocks):
            shard = lax.rem((holder ^ flips[flip]) + (size - 8 * step), size)
            rows = pl.ds(pl.multiple_of(shard * each, each), each)
            buffer[rows, :] = ref[at * each : at * each + each, first : first + buffer.shape[1]]


def packed_row(row, half, patches, groups, by_band):
    band, patch = (row // patches, row % patches) if by_band else (row % groups, row // groups)
    return (band * 2 + half) * patches + patch


def unpack(packed, patches, groups, by_band):
    rows = packed.shape[0] // 2
    row = lax.broadcasted_iota(jnp.int32, (rows, 2 * rows), 0)
    there = lax.broadcasted_iota(jnp.int32, (rows, 2 * rows), 1)
    parts = []
    for half in range(2):
        chosen = (there == packed_row(row, half, patches, groups, by_band)).astype(jnp.bfloat16)
        parts.append(nn(chosen, packed))
    return jnp.concatenate(parts, axis=1).astype(jnp.bfloat16)


def pack(values, patches, groups, by_band):
    rows, width = values.shape
    row = lax.broadcasted_iota(jnp.int32, (2 * rows, rows), 1)
    there = lax.broadcasted_iota(jnp.int32, (2 * rows, rows), 0)
    total = 0.0
    for half in range(2):
        chosen = (there == packed_row(row, half, patches, groups, by_band)).astype(jnp.bfloat16)
        total += nn(chosen, values[:, half * (width // 2) : (half + 1) * (width // 2)])
    return total.astype(jnp.bfloat16)


def prepare(patches, groups, tokens, w_so, w_gqkv, w_go, packed, joined):
    packed[...] = pack(tokens[...], patches, groups, False)
    width = w_so.shape[1]
    joined[:, :width] = w_so[...]
    joined[:, width : 4 * width] = w_gqkv[...]
    joined[:, 4 * width :] = w_go[...]


def add_packed(patches, groups, values, packed, total):
    total[...] = values[...] + unpack(packed[...], patches, groups, False)


def spatial_forward(plan, patches, groups, packed, keep, *refs):
    pieces, (result_out, qkv_out, probs_out, banded_out, turned_out, weight) = refs[:-6], refs[-6:]
    place_rows(pieces, plan, 0, weight)
    banded = unpack(packed[...], patches, groups, True)
    banded_out[...] = banded
    wide = banded.astype(jnp.float32)
    normed = (wide * inverse_rms(wide)).astype(jnp.bfloat16)
    allowed = keep[pl.ds(lax.axis_index("grid"), 1), :] > 0
    qkv_out[...] = nn(normed, weight[...]).astype(jnp.bfloat16)
    result_out[...] = pack(attention_forward(qkv_out, allowed, probs_out), patches, groups, True)
    turned_out[...] = weight[...].T


def spatial_backward(
    patches, groups, grad_packed, banded, qkv, probs, turned, grad_out, grads, grad_probs, grad_scores
):
    grad = unpack(grad_packed[...], patches, groups, True)
    attention_backward(qkv, probs, grad, grad_probs, grad_scores, grads)
    wide = banded[...].astype(jnp.float32)
    inverse = inverse_rms(wide)
    grad_normed = nn(grads[...], turned[...]).astype(jnp.bfloat16).astype(jnp.float32)
    grad_out[...] = pack(norm_grad(wide, inverse, grad_normed).astype(jnp.bfloat16), patches, groups, True)


def group_layer(patches, plan, tokens, attended, cotangent, *refs):
    pieces, rest = refs[:-12], refs[-12:]
    mixed, grad_y, grad_bands, so_buf, qkv_buf, go_buf, qkv, probs, y_buf, grads, grad_probs, grad_scores = rest
    rows, width = tokens.shape
    groups = rows // patches
    place_rows(pieces, plan, 0, so_buf)
    ordered = unpack(attended[...], patches, groups, False)
    y_first = (tokens[...].astype(jnp.float32) + nn(ordered, so_buf[...])).astype(jnp.bfloat16)
    wide = y_first.astype(jnp.float32)
    y_buf[...] = wide
    inverse = inverse_rms(wide)
    normed = (wide * inverse).astype(jnp.bfloat16)
    place_rows(pieces, plan, width, qkv_buf)
    qkv[...] = nn(normed, qkv_buf[...]).astype(jnp.bfloat16)
    place_rows(pieces, plan, 4 * width, go_buf)
    grad_attended = nt(cotangent[...], go_buf[...]).astype(jnp.bfloat16)
    row_patch = lax.broadcasted_iota(jnp.int32, (rows, rows), 0) // groups
    allowed = row_patch == lax.broadcasted_iota(jnp.int32, (rows, rows), 1) // groups
    results = attention_forward(qkv, allowed, probs)
    mixed[...] = (y_buf[...] + nn(results, go_buf[...])).astype(jnp.bfloat16)
    attention_backward(qkv, probs, grad_attended, grad_probs, grad_scores, grads)
    grad_normed = nt(grads[...], qkv_buf[...]).astype(jnp.bfloat16).astype(jnp.float32)
    through = norm_grad(y_buf[...], inverse, grad_normed).astype(jnp.bfloat16)
    total = cotangent[...] + through
    grad_y[...] = total
    spread = nt(total, so_buf[...]).astype(jnp.bfloat16)
    grad_bands[...] = pack(spread, patches, groups, False)


VMEM_SPEC = pl.BlockSpec(memory_space=pltpu.VMEM)


def room(mebibytes):
    return pltpu.CompilerParams(vmem_limit_bytes=mebibytes * 1024 * 1024)


def shape(rows, columns, dtype=jnp.bfloat16):
    return jax.ShapeDtypeStruct((rows, columns), dtype)


def cost(rows, width, weights, passes):
    return pl.CostEstimate(
        flops=2 * passes * weights * rows * width * width,
        bytes_accessed=2 * passes * weights * width * width + 16 * rows * width,
        transcendentals=16 * rows * rows,
    )


def exchange(packed):
    size = lax.axis_size("grid")
    rows, columns = packed.shape
    blocks = packed.reshape(size, rows // size, columns)
    return lax.all_to_all(blocks, "grid", split_axis=0, concat_axis=0, tiled=True).reshape(rows, columns)


def mesh_moves(size):
    everyone = range(size)
    first = [(i, i ^ (2 if i % 2 == 0 else 4)) for i in everyone]
    second = [(i, i ^ (4 if i % 2 == 0 else 2)) for i in everyone]
    sibling = [(i, i ^ 1) for i in everyone]
    along = [[(i, (i + 8 * step) % size) for i in everyone] for step in range(1, size // 8)]
    return first, second, sibling, along


def move(values, table):
    return lax.ppermute(values, "grid", table)


def together(*values):
    return lax.optimization_barrier(values)


def stack(*values):
    return jnp.concatenate(values, axis=0)


def plans(size):
    steps = range(size // 8)
    line = [[(step, flip) for step in steps] for flip in range(4)]
    own, rest = [(0, flip) for flip in range(4)], [blocks[1:] for blocks in line]

    def both_cores(held):
        return [(False, blocks) for blocks in held] + [(True, blocks) for blocks in held]

    return both_cores(line), both_cores([own] + rest)


def banded_layer(tokens, cotangent, w_sqkv, w_so, w_gqkv, w_go, keep):
    patches, groups, width = tokens.shape
    rows = patches * groups
    all_patches = patches * lax.axis_size("grid")
    first, second, sibling, along = mesh_moves(lax.axis_size("grid"))
    spatial_plan, group_plan = plans(lax.axis_size("grid"))
    pairs = width // 128
    packed_shape = shape(2 * rows, width // 2)

    tokens = tokens.reshape(rows, width)
    packed, group = pl.pallas_call(
        partial(prepare, patches, groups),
        out_shape=(packed_shape, shape(w_so.shape[0], 5 * width)),
        in_specs=[VMEM_SPEC] * 4,
        out_specs=(VMEM_SPEC,) * 2,
        name="prepare",
    )(tokens, w_so, w_gqkv, w_go)
    spatial_line = [w_sqkv] + [move(w_sqkv, table) for table in along]
    group_one, group_other = move(group, first), move(group, second)
    spatial_line, group_one, group_other, packed, group = together(
        stack(*spatial_line), group_one, group_other, packed, group
    )
    group_parts = [move(group, table) for table in along[:-1]]
    spatial_one, spatial_other = move(spatial_line, first), move(spatial_line, second)
    group_both = move(group_one, second)
    spatial_one, spatial_other, group_plane, group, group_other, spatial_line, packed, *group_parts = together(
        spatial_one,
        spatial_other,
        stack(group, group_one, group_other, group_both),
        group,
        group_other,
        spatial_line,
        packed,
        *group_parts,
    )
    spatial_both = move(spatial_one, second)
    spatial_across = [move(part, sibling) for part in (spatial_line, spatial_one, spatial_other)]
    group_line = stack(*group_parts, move(group, along[-1]))
    spatial_both, group_line, group_plane, group_other, middle, banded, *spatial_across = together(
        spatial_both, group_line, group_plane, group_other, group_parts[1], exchange(packed), *spatial_across
    )
    other_parts = [move(group_other, along[0]), move(middle, second), move(group_other, along[-1])]
    group_one = move(group_line, first)
    spatial_rows = [spatial_line, spatial_one, spatial_other, spatial_both]
    spatial_rows += [*spatial_across, move(spatial_both, sibling)]
    probs_shape = shape(all_patches, 2 * pairs * all_patches, jnp.float32)
    attended, qkv, probs, banded, turned = pl.pallas_call(
        partial(spatial_forward, spatial_plan, patches, groups),
        out_shape=(
            packed_shape,
            shape(all_patches, 3 * width),
            probs_shape,
            shape(all_patches, width),
            shape(3 * width, width),
        ),
        in_specs=[VMEM_SPEC] * (2 + len(spatial_rows)),
        out_specs=(VMEM_SPEC,) * 5,
        scratch_shapes=[pltpu.VMEM((width, 3 * width), jnp.bfloat16)],
        compiler_params=room(28),
        cost_estimate=cost(all_patches, width, 3, 1),
        name="spatial_forward",
    )(banded, keep, *spatial_rows)
    group_one, attended, group_plane, group_line, *other_parts = together(
        group_one, attended, group_plane, group_line, *other_parts
    )
    group_both = move(group_one, second)
    group_other = stack(*other_parts)
    group_across = [move(part, sibling) for part in (group_plane, group_line, group_one, group_other)]
    group_both, attended, *group_across = together(group_both, exchange(attended), *group_across)
    group_rows = [group_plane, group_line, group_one, group_other, group_both]
    group_rows += [*group_across, move(group_both, sibling)]
    heads_wide = 2 * pairs * rows
    mixed, grad_y, grad_bands = pl.pallas_call(
        partial(group_layer, patches, group_plan),
        out_shape=(shape(rows, width), shape(rows, width), packed_shape),
        in_specs=[VMEM_SPEC] * (3 + len(group_rows)),
        out_specs=(VMEM_SPEC,) * 3,
        scratch_shapes=[
            pltpu.VMEM((width, width), jnp.bfloat16),
            pltpu.VMEM((width, 3 * width), jnp.bfloat16),
            pltpu.VMEM((width, width), jnp.bfloat16),
            pltpu.VMEM((rows, 3 * width), jnp.bfloat16),
            pltpu.VMEM((rows, heads_wide), jnp.float32),
            pltpu.VMEM((rows, width), jnp.float32),
            pltpu.VMEM((rows, 3 * width), jnp.bfloat16),
            pltpu.VMEM((rows, heads_wide), jnp.bfloat16),
            pltpu.VMEM((rows, heads_wide), jnp.bfloat16),
        ],
        compiler_params=room(32),
        cost_estimate=cost(rows, width, 5, 2),
        name="group_layer",
    )(tokens, attended, cotangent.reshape(rows, width), *group_rows)
    heads_wide = 2 * pairs * all_patches
    grad_first = pl.pallas_call(
        partial(spatial_backward, patches, groups),
        out_shape=packed_shape,
        in_specs=[VMEM_SPEC] * 5,
        out_specs=VMEM_SPEC,
        scratch_shapes=[
            pltpu.VMEM((all_patches, 3 * width), jnp.bfloat16),
            pltpu.VMEM((all_patches, heads_wide), jnp.bfloat16),
            pltpu.VMEM((all_patches, heads_wide), jnp.bfloat16),
        ],
        compiler_params=room(18),
        cost_estimate=cost(all_patches, width, 3, 1),
        name="spatial_backward",
    )(exchange(grad_bands), banded, qkv, probs, turned)
    token_grad = pl.pallas_call(
        partial(add_packed, patches, groups),
        out_shape=shape(rows, width),
        in_specs=[VMEM_SPEC] * 2,
        out_specs=VMEM_SPEC,
        compiler_params=room(8),
        name="add_packed",
    )(grad_y, exchange(grad_first))
    whole = (patches, groups, width)
    return (mixed.reshape(whole), token_grad.reshape(whole))


def local(tokens, cotangent, w_sqkv, w_so, w_gqkv, w_go, keep):
    patches, groups, width = tokens.shape
    size = lax.axis_size("grid")
    fits = size == groups and size % 8 == 0 and width % (16 * size) == 0 and width == 64 * H and patches * groups % 128 == 0 and 2 * patches % 8 == 0
    layer = banded_layer if fits else general_layer
    return layer(tokens, cotangent, w_sqkv, w_so, w_gqkv, w_go, keep)


def solution(mesh):
    placed = (
        P(("parts", "grid"), None, None),
        P(("parts", "grid"), None, None),
        P("grid", None),
        P("grid", None),
        P("grid", None),
        P("grid", None),
        P(None, "parts"),
    )
    return jax.shard_map(
        local,
        mesh=mesh,
        in_specs=placed,
        out_specs=(P(("parts", "grid"), None, None), P(("parts", "grid"), None, None)),
        check_vma=False,
    )
```

```python
from functools import partial

import jax
import jax.numpy as jnp
from jax import lax
from jax.experimental import pallas as pl
from jax.experimental.pallas import tpu as pltpu
from jax.sharding import PartitionSpec as P

H = 16
G = 32


def rms_normalize(values):
    wide = values.astype(jnp.float32)
    meansq = jnp.mean(wide * wide, axis=-1, keepdims=True)
    return (wide * lax.rsqrt(meansq + 1e-06)).astype(jnp.bfloat16)


def project_spatial(tokens, weight):
    patches, groups, width = tokens.shape
    normed = rms_normalize(tokens).reshape(patches * groups, width)
    stacked = jnp.dot(normed, weight, preferred_element_type=jnp.float32).astype(jnp.bfloat16)
    stacked = stacked.reshape(patches, groups, 3, width).transpose(2, 0, 1, 3)
    return stacked.reshape(3, patches, groups * width)


def pair_attention(operands):
    stacked, keep_row = operands
    query, keyed, valued = (stacked[0], stacked[1], stacked[2])
    scale = query.shape[-1] ** (-0.5)
    scores = jnp.dot(query, keyed.T, preferred_element_type=jnp.float32) * scale
    weights = jnp.exp(scores) * keep_row[None, :]
    probs = (weights / jnp.sum(weights, axis=-1, keepdims=True)).astype(jnp.bfloat16)
    return jnp.dot(probs, valued, preferred_element_type=jnp.float32).astype(jnp.bfloat16)


def spatial_attention(stacked, keep_rows, attend):
    three, patches, columns = stacked.shape
    pairs = keep_rows.shape[0]
    split = stacked.reshape(3, patches, pairs, columns // pairs).transpose(2, 0, 1, 3)
    result = lax.map(attend, (split, keep_rows))
    return result.transpose(1, 0, 2).reshape(patches, columns)


def block_group(tokens, attended, w_so, w_gqkv, w_go):
    patches, groups, width = tokens.shape
    rows = patches * groups
    heads = H
    y_first = (
        tokens.reshape(rows, width).astype(jnp.float32)
        + jnp.dot(attended.reshape(rows, width), w_so, preferred_element_type=jnp.float32)
    ).astype(jnp.bfloat16)
    normed = rms_normalize(y_first)
    stacked = jnp.dot(normed, w_gqkv, preferred_element_type=jnp.float32).astype(jnp.bfloat16)
    stacked = stacked.reshape(patches, groups, 3, heads, width // heads)
    query = stacked[:, :, 0].astype(jnp.float32)
    keyed = stacked[:, :, 1].astype(jnp.float32)
    valued = stacked[:, :, 2].astype(jnp.float32)
    scale = (width // heads) ** (-0.5)
    scores = jnp.einsum("pgne,pkne->pngk", query, keyed) * scale
    weights = jnp.exp(scores)
    probs = (weights / jnp.sum(weights, axis=-1, keepdims=True)).astype(jnp.bfloat16)
    result = jnp.einsum("pngk,pkne->pgne", probs.astype(jnp.float32), valued).astype(jnp.bfloat16)
    result = result.reshape(rows, width)
    mixed = (
        y_first.astype(jnp.float32) + jnp.dot(result, w_go, preferred_element_type=jnp.float32)
    ).astype(jnp.bfloat16)
    return mixed.reshape(patches, groups, width)


def general_layer(tokens, cotangent, w_sqkv, w_so, w_gqkv, w_go, keep):
    grid_size = lax.axis_size("grid")
    position = lax.axis_index("grid")
    full_sqkv, full_so, full_gqkv, full_go = (
        lax.all_gather(w_sqkv, "grid", axis=0, tiled=True),
        lax.all_gather(w_so, "grid", axis=0, tiled=True),
        lax.all_gather(w_gqkv, "grid", axis=0, tiled=True),
        lax.all_gather(w_go, "grid", axis=0, tiled=True),
    )
    stacked, pull_first = jax.vjp(partial(project_spatial, weight=full_sqkv), tokens)
    banded = lax.all_to_all(stacked, "grid", split_axis=2, concat_axis=1, tiled=True)
    pairs = G * H // grid_size
    pair_ids = position * pairs + jnp.arange(pairs, dtype=jnp.int32)
    select = (pair_ids[:, None] // H == jnp.arange(G, dtype=jnp.int32)[None, :]).astype(jnp.float32)
    keep_rows = jnp.dot(select, keep.astype(jnp.float32), precision=lax.Precision.HIGHEST)
    attend = jax.checkpoint(pair_attention)
    attended_bands, pull_spatial = jax.vjp(
        partial(spatial_attention, keep_rows=keep_rows, attend=attend), banded
    )
    attended = lax.all_to_all(attended_bands, "grid", split_axis=0, concat_axis=1, tiled=True)
    mixed, pull_group = jax.vjp(
        partial(block_group, w_so=full_so, w_gqkv=full_gqkv, w_go=full_go), tokens, attended
    )
    grad_direct, grad_attended = pull_group(cotangent)
    grad_bands = lax.all_to_all(grad_attended, "grid", split_axis=1, concat_axis=0, tiled=True)
    (grad_banded,) = pull_spatial(grad_bands)
    grad_stacked = lax.all_to_all(grad_banded, "grid", split_axis=1, concat_axis=2, tiled=True)
    (grad_first,) = pull_first(grad_stacked)
    return (mixed, grad_direct + grad_first)


def nt(a, b):
    return lax.dot_general(a, b, (((1,), (1,)), ((), ())), preferred_element_type=jnp.float32)


def tn(a, b):
    return lax.dot_general(a, b, (((0,), (0,)), ((), ())), preferred_element_type=jnp.float32)


def nn(a, b):
    return jnp.dot(a, b, preferred_element_type=jnp.float32)


def inverse_rms(wide):
    return lax.rsqrt(jnp.mean(wide * wide, axis=-1, keepdims=True) + 1e-06)


def norm_grad(wide, inverse, grad):
    inner = jnp.mean(grad * wide, axis=-1, keepdims=True)
    return grad * inverse - wide * (inverse * inverse * inverse * inner)


def head_pair(values, low):
    zero = jnp.zeros_like(values)
    return jnp.concatenate([jnp.where(low, values, zero), jnp.where(low, zero, values)], axis=0)


def join_pair(stacked, low):
    rows = stacked.shape[0] // 2
    return jnp.where(low, stacked[:rows], stacked[rows:])


def low_lanes(rows):
    return lax.broadcasted_iota(jnp.int32, (rows, 128), 1) < 64


def columns(which, pair, width):
    return slice(which * width + pair * 128, which * width + pair * 128 + 128)


def attention_forward(qkv, allowed, probs):
    rows, width = qkv.shape[0], qkv.shape[1] // 3
    span, pairs, low = 2 * rows, width // 128, low_lanes(rows)
    for pair in range(pairs):
        keyed = head_pair(qkv[:, columns(1, pair, width)], low)
        probs[:, pair * span : pair * span + span] = nt(qkv[:, columns(0, pair, width)], keyed)
    for head in range(2 * pairs):
        at = slice(head * rows, head * rows + rows)
        weights = jnp.where(allowed, jnp.exp(probs[:, at] * 0.125), 0.0)
        probs[:, at] = weights / jnp.sum(weights, axis=-1, keepdims=True)
    results = []
    for pair in range(pairs):
        valued = head_pair(qkv[:, columns(2, pair, width)], low)
        results.append(nn(probs[:, pair * span : pair * span + span].astype(jnp.bfloat16), valued).astype(jnp.bfloat16))
    return jnp.concatenate(results, axis=1)


def attention_backward(qkv, probs, grad, grad_probs, grad_scores, grads):
    rows, width = qkv.shape[0], qkv.shape[1] // 3
    span, pairs, low = 2 * rows, width // 128, low_lanes(rows)
    for pair in range(pairs):
        valued = head_pair(qkv[:, columns(2, pair, width)], low)
        part = nt(grad[:, columns(0, pair, width)], valued)
        grad_probs[:, pair * span : pair * span + span] = part.astype(jnp.bfloat16)
    for head in range(2 * pairs):
        at = slice(head * rows, head * rows + rows)
        share, part = probs[:, at], grad_probs[:, at].astype(jnp.float32)
        inner = jnp.sum(part * share, axis=-1, keepdims=True)
        grad_scores[:, at] = (share * (part - inner) * 0.125).astype(jnp.bfloat16)
    for pair in range(pairs):
        at = slice(pair * span, pair * span + span)
        keyed = head_pair(qkv[:, columns(1, pair, width)], low)
        query, part = qkv[:, columns(0, pair, width)], grad[:, columns(0, pair, width)]
        scored = grad_scores[:, at]
        grads[:, columns(0, pair, width)] = nn(scored, keyed).astype(jnp.bfloat16)
        grads[:, columns(1, pair, width)] = join_pair(tn(scored, query), low).astype(jnp.bfloat16)
        shares = probs[:, at].astype(jnp.bfloat16)
        grads[:, columns(2, pair, width)] = join_pair(tn(shares, part), low).astype(jnp.bfloat16)


def place_rows(refs, plan, first, buffer):
    position = lax.axis_index("grid")
    size = lax.axis_size("grid")
    each = buffer.shape[0] // size
    core = lax.rem(position, 2)
    for ref, (from_sibling, blocks) in zip(refs, plan):
        side = 1 - core if from_sibling else core
        holder = position + 1 - 2 * core if from_sibling else position
        flips = (0, 2 * (side + 1), 4 - 2 * side, 6)
        for at, (step, flip) in enumerate(blocks):
            shard = lax.rem((holder ^ flips[flip]) + (size - 8 * step), size)
            rows = pl.ds(pl.multiple_of(shard * each, each), each)
            buffer[rows, :] = ref[at * each : at * each + each, first : first + buffer.shape[1]]


def packed_row(row, half, patches, groups, by_band):
    band, patch = (row // patches, row % patches) if by_band else (row % groups, row // groups)
    return (band * 2 + half) * patches + patch


def unpack(packed, patches, groups, by_band):
    rows = packed.shape[0] // 2
    row = lax.broadcasted_iota(jnp.int32, (rows, 2 * rows), 0)
    there = lax.broadcasted_iota(jnp.int32, (rows, 2 * rows), 1)
    parts = []
    for half in range(2):
        chosen = (there == packed_row(row, half, patches, groups, by_band)).astype(jnp.bfloat16)
        parts.append(nn(chosen, packed))
    return jnp.concatenate(parts, axis=1).astype(jnp.bfloat16)


def pack(values, patches, groups, by_band):
    rows, width = values.shape
    row = lax.broadcasted_iota(jnp.int32, (2 * rows, rows), 1)
    there = lax.broadcasted_iota(jnp.int32, (2 * rows, rows), 0)
    total = 0.0
    for half in range(2):
        chosen = (there == packed_row(row, half, patches, groups, by_band)).astype(jnp.bfloat16)
        total += nn(chosen, values[:, half * (width // 2) : (half + 1) * (width // 2)])
    return total.astype(jnp.bfloat16)


def prepare(patches, groups, tokens, w_so, w_gqkv, w_go, packed, joined):
    packed[...] = pack(tokens[...], patches, groups, False)
    width = w_so.shape[1]
    joined[:, :width] = w_so[...]
    joined[:, width : 4 * width] = w_gqkv[...]
    joined[:, 4 * width :] = w_go[...]


def add_packed(patches, groups, values, packed, total):
    total[...] = values[...] + unpack(packed[...], patches, groups, False)


def spatial_forward(plan, patches, groups, packed, keep, *refs):
    pieces, (result_out, qkv_out, probs_out, banded_out, turned_out, weight) = refs[:-6], refs[-6:]
    place_rows(pieces, plan, 0, weight)
    banded = unpack(packed[...], patches, groups, True)
    banded_out[...] = banded
    wide = banded.astype(jnp.float32)
    normed = (wide * inverse_rms(wide)).astype(jnp.bfloat16)
    allowed = keep[pl.ds(lax.axis_index("grid"), 1), :] > 0
    qkv_out[...] = nn(normed, weight[...]).astype(jnp.bfloat16)
    result_out[...] = pack(attention_forward(qkv_out, allowed, probs_out), patches, groups, True)
    turned_out[...] = weight[...].T


def spatial_backward(
    patches, groups, grad_packed, banded, qkv, probs, turned, grad_out, grads, grad_probs, grad_scores
):
    grad = unpack(grad_packed[...], patches, groups, True)
    attention_backward(qkv, probs, grad, grad_probs, grad_scores, grads)
    wide = banded[...].astype(jnp.float32)
    inverse = inverse_rms(wide)
    grad_normed = nn(grads[...], turned[...]).astype(jnp.bfloat16).astype(jnp.float32)
    grad_out[...] = pack(norm_grad(wide, inverse, grad_normed).astype(jnp.bfloat16), patches, groups, True)


def group_layer(patches, plan, tokens, attended, cotangent, *refs):
    pieces, rest = refs[:-12], refs[-12:]
    mixed, grad_y, grad_bands, so_buf, qkv_buf, go_buf, qkv, probs, y_buf, grads, grad_probs, grad_scores = rest
    rows, width = tokens.shape
    groups = rows // patches
    place_rows(pieces, plan, 0, so_buf)
    ordered = unpack(attended[...], patches, groups, False)
    y_first = (tokens[...].astype(jnp.float32) + nn(ordered, so_buf[...])).astype(jnp.bfloat16)
    wide = y_first.astype(jnp.float32)
    y_buf[...] = wide
    inverse = inverse_rms(wide)
    normed = (wide * inverse).astype(jnp.bfloat16)
    place_rows(pieces, plan, width, qkv_buf)
    qkv[...] = nn(normed, qkv_buf[...]).astype(jnp.bfloat16)
    place_rows(pieces, plan, 4 * width, go_buf)
    grad_attended = nt(cotangent[...], go_buf[...]).astype(jnp.bfloat16)
    row_patch = lax.broadcasted_iota(jnp.int32, (rows, rows), 0) // groups
    allowed = row_patch == lax.broadcasted_iota(jnp.int32, (rows, rows), 1) // groups
    results = attention_forward(qkv, allowed, probs)
    mixed[...] = (y_buf[...] + nn(results, go_buf[...])).astype(jnp.bfloat16)
    attention_backward(qkv, probs, grad_attended, grad_probs, grad_scores, grads)
    grad_normed = nt(grads[...], qkv_buf[...]).astype(jnp.bfloat16).astype(jnp.float32)
    through = norm_grad(y_buf[...], inverse, grad_normed).astype(jnp.bfloat16)
    total = cotangent[...] + through
    grad_y[...] = total
    spread = nt(total, so_buf[...]).astype(jnp.bfloat16)
    grad_bands[...] = pack(spread, patches, groups, False)


VMEM_SPEC = pl.BlockSpec(memory_space=pltpu.VMEM)


def room(mebibytes):
    return pltpu.CompilerParams(vmem_limit_bytes=mebibytes * 1024 * 1024)


def shape(rows, columns, dtype=jnp.bfloat16):
    return jax.ShapeDtypeStruct((rows, columns), dtype)


def cost(rows, width, weights, passes):
    return pl.CostEstimate(
        flops=2 * passes * weights * rows * width * width,
        bytes_accessed=2 * passes * weights * width * width + 16 * rows * width,
        transcendentals=16 * rows * rows,
    )


def exchange(packed):
    size = lax.axis_size("grid")
    rows, columns = packed.shape
    blocks = packed.reshape(size, rows // size, columns)
    return lax.all_to_all(blocks, "grid", split_axis=0, concat_axis=0, tiled=True).reshape(rows, columns)


def mesh_moves(size):
    everyone = range(size)
    first = [(i, i ^ (2 if i % 2 == 0 else 4)) for i in everyone]
    second = [(i, i ^ (4 if i % 2 == 0 else 2)) for i in everyone]
    sibling = [(i, i ^ 1) for i in everyone]
    along = [[(i, (i + 8 * step) % size) for i in everyone] for step in range(1, size // 8)]
    return first, second, sibling, along


def move(values, table):
    return lax.ppermute(values, "grid", table)


def together(*values):
    return lax.optimization_barrier(values)


def stack(*values):
    return jnp.concatenate(values, axis=0)


def plans(size):
    steps = range(size // 8)
    line = [[(step, flip) for step in steps] for flip in range(4)]
    own, rest = [(0, flip) for flip in range(4)], [blocks[1:] for blocks in line]

    def both_cores(held):
        return [(False, blocks) for blocks in held] + [(True, blocks) for blocks in held]

    return both_cores(line), both_cores([own] + rest)


def banded_layer(tokens, cotangent, w_sqkv, w_so, w_gqkv, w_go, keep):
    patches, groups, width = tokens.shape
    rows = patches * groups
    all_patches = patches * lax.axis_size("grid")
    first, second, sibling, along = mesh_moves(lax.axis_size("grid"))
    spatial_plan, group_plan = plans(lax.axis_size("grid"))
    pairs = width // 128
    packed_shape = shape(2 * rows, width // 2)

    tokens = tokens.reshape(rows, width)
    packed, group = pl.pallas_call(
        partial(prepare, patches, groups),
        out_shape=(packed_shape, shape(w_so.shape[0], 5 * width)),
        in_specs=[VMEM_SPEC] * 4,
        out_specs=(VMEM_SPEC,) * 2,
        name="prepare",
    )(tokens, w_so, w_gqkv, w_go)
    spatial_line = [w_sqkv] + [move(w_sqkv, table) for table in along]
    group_one, group_other = move(group, first), move(group, second)
    spatial_line, group_one, group_other, packed, group = together(
        stack(*spatial_line), group_one, group_other, packed, group
    )
    group_parts = [move(group, table) for table in along[:-1]]
    spatial_one, spatial_other = move(spatial_line, first), move(spatial_line, second)
    group_both = move(group_one, second)
    spatial_one, spatial_other, group_plane, group, group_other, spatial_line, packed, *group_parts = together(
        spatial_one,
        spatial_other,
        stack(group, group_one, group_other, group_both),
        group,
        group_other,
        spatial_line,
        packed,
        *group_parts,
    )
    spatial_both = move(spatial_one, second)
    spatial_across = [move(part, sibling) for part in (spatial_line, spatial_one, spatial_other)]
    group_line = stack(*group_parts, move(group, along[-1]))
    spatial_both, group_line, group_plane, group_other, middle, banded, *spatial_across = together(
        spatial_both, group_line, group_plane, group_other, group_parts[1], exchange(packed), *spatial_across
    )
    other_parts = [move(group_other, along[0]), move(middle, second), move(group_other, along[-1])]
    group_one = move(group_line, first)
    spatial_rows = [spatial_line, spatial_one, spatial_other, spatial_both]
    spatial_rows += [*spatial_across, move(spatial_both, sibling)]
    probs_shape = shape(all_patches, 2 * pairs * all_patches, jnp.float32)
    attended, qkv, probs, banded, turned = pl.pallas_call(
        partial(spatial_forward, spatial_plan, patches, groups),
        out_shape=(
            packed_shape,
            shape(all_patches, 3 * width),
            probs_shape,
            shape(all_patches, width),
            shape(3 * width, width),
        ),
        in_specs=[VMEM_SPEC] * (2 + len(spatial_rows)),
        out_specs=(VMEM_SPEC,) * 5,
        scratch_shapes=[pltpu.VMEM((width, 3 * width), jnp.bfloat16)],
        compiler_params=room(28),
        cost_estimate=cost(all_patches, width, 3, 1),
        name="spatial_forward",
    )(banded, keep, *spatial_rows)
    group_one, attended, group_plane, group_line, *other_parts = together(
        group_one, attended, group_plane, group_line, *other_parts
    )
    group_both = move(group_one, second)
    group_other = stack(*other_parts)
    group_across = [move(part, sibling) for part in (group_plane, group_line, group_one, group_other)]
    group_both, attended, *group_across = together(group_both, exchange(attended), *group_across)
    group_rows = [group_plane, group_line, group_one, group_other, group_both]
    group_rows += [*group_across, move(group_both, sibling)]
    heads_wide = 2 * pairs * rows
    mixed, grad_y, grad_bands = pl.pallas_call(
        partial(group_layer, patches, group_plan),
        out_shape=(shape(rows, width), shape(rows, width), packed_shape),
        in_specs=[VMEM_SPEC] * (3 + len(group_rows)),
        out_specs=(VMEM_SPEC,) * 3,
        scratch_shapes=[
            pltpu.VMEM((width, width), jnp.bfloat16),
            pltpu.VMEM((width, 3 * width), jnp.bfloat16),
            pltpu.VMEM((width, width), jnp.bfloat16),
            pltpu.VMEM((rows, 3 * width), jnp.bfloat16),
            pltpu.VMEM((rows, heads_wide), jnp.float32),
            pltpu.VMEM((rows, width), jnp.float32),
            pltpu.VMEM((rows, 3 * width), jnp.bfloat16),
            pltpu.VMEM((rows, heads_wide), jnp.bfloat16),
            pltpu.VMEM((rows, heads_wide), jnp.bfloat16),
        ],
        compiler_params=room(32),
        cost_estimate=cost(rows, width, 5, 2),
        name="group_layer",
    )(tokens, attended, cotangent.reshape(rows, width), *group_rows)
    heads_wide = 2 * pairs * all_patches
    grad_first = pl.pallas_call(
        partial(spatial_backward, patches, groups),
        out_shape=packed_shape,
        in_specs=[VMEM_SPEC] * 5,
        out_specs=VMEM_SPEC,
        scratch_shapes=[
            pltpu.VMEM((all_patches, 3 * width), jnp.bfloat16),
            pltpu.VMEM((all_patches, heads_wide), jnp.bfloat16),
            pltpu.VMEM((all_patches, heads_wide), jnp.bfloat16),
        ],
        compiler_params=room(18),
        cost_estimate=cost(all_patches, width, 3, 1),
        name="spatial_backward",
    )(exchange(grad_bands), banded, qkv, probs, turned)
    token_grad = pl.pallas_call(
        partial(add_packed, patches, groups),
        out_shape=shape(rows, width),
        in_specs=[VMEM_SPEC] * 2,
        out_specs=VMEM_SPEC,
        compiler_params=room(8),
        name="add_packed",
    )(grad_y, exchange(grad_first))
    whole = (patches, groups, width)
    return (mixed.reshape(whole), token_grad.reshape(whole))


def local(tokens, cotangent, w_sqkv, w_so, w_gqkv, w_go, keep):
    patches, groups, width = tokens.shape
    size = lax.axis_size("grid")
    fits = size == groups and size % 8 == 0 and width % (16 * size) == 0 and width == 64 * H and patches * groups % 128 == 0 and 2 * patches % 8 == 0
    layer = banded_layer if fits else general_layer
    return layer(tokens, cotangent, w_sqkv, w_so, w_gqkv, w_go, keep)


def solution(mesh):
    placed = (
        P(("parts", "grid"), None, None),
        P(("parts", "grid"), None, None),
        P("grid", None),
        P("grid", None),
        P("grid", None),
        P("grid", None),
        P(None, "parts"),
    )
    return jax.shard_map(
        local,
        mesh=mesh,
        in_specs=placed,
        out_specs=(P(("parts", "grid"), None, None), P(("parts", "grid"), None, None)),
        check_vma=False,
    )
```

```python
from functools import partial

import jax
import jax.numpy as jnp
from jax import lax
from jax.experimental import pallas as pl
from jax.experimental.pallas import tpu as pltpu
from jax.sharding import PartitionSpec as P

H = 16
G = 32


def rms_normalize(values):
    wide = values.astype(jnp.float32)
    meansq = jnp.mean(wide * wide, axis=-1, keepdims=True)
    return (wide * lax.rsqrt(meansq + 1e-06)).astype(jnp.bfloat16)


def project_spatial(tokens, weight):
    patches, groups, width = tokens.shape
    normed = rms_normalize(tokens).reshape(patches * groups, width)
    stacked = jnp.dot(normed, weight, preferred_element_type=jnp.float32).astype(jnp.bfloat16)
    stacked = stacked.reshape(patches, groups, 3, width).transpose(2, 0, 1, 3)
    return stacked.reshape(3, patches, groups * width)


def pair_attention(operands):
    stacked, keep_row = operands
    query, keyed, valued = (stacked[0], stacked[1], stacked[2])
    scale = query.shape[-1] ** (-0.5)
    scores = jnp.dot(query, keyed.T, preferred_element_type=jnp.float32) * scale
    weights = jnp.exp(scores) * keep_row[None, :]
    probs = (weights / jnp.sum(weights, axis=-1, keepdims=True)).astype(jnp.bfloat16)
    return jnp.dot(probs, valued, preferred_element_type=jnp.float32).astype(jnp.bfloat16)


def spatial_attention(stacked, keep_rows, attend):
    three, patches, columns = stacked.shape
    pairs = keep_rows.shape[0]
    split = stacked.reshape(3, patches, pairs, columns // pairs).transpose(2, 0, 1, 3)
    result = lax.map(attend, (split, keep_rows))
    return result.transpose(1, 0, 2).reshape(patches, columns)


def block_group(tokens, attended, w_so, w_gqkv, w_go):
    patches, groups, width = tokens.shape
    rows = patches * groups
    heads = H
    y_first = (
        tokens.reshape(rows, width).astype(jnp.float32)
        + jnp.dot(attended.reshape(rows, width), w_so, preferred_element_type=jnp.float32)
    ).astype(jnp.bfloat16)
    normed = rms_normalize(y_first)
    stacked = jnp.dot(normed, w_gqkv, preferred_element_type=jnp.float32).astype(jnp.bfloat16)
    stacked = stacked.reshape(patches, groups, 3, heads, width // heads)
    query = stacked[:, :, 0].astype(jnp.float32)
    keyed = stacked[:, :, 1].astype(jnp.float32)
    valued = stacked[:, :, 2].astype(jnp.float32)
    scale = (width // heads) ** (-0.5)
    scores = jnp.einsum("pgne,pkne->pngk", query, keyed) * scale
    weights = jnp.exp(scores)
    probs = (weights / jnp.sum(weights, axis=-1, keepdims=True)).astype(jnp.bfloat16)
    result = jnp.einsum("pngk,pkne->pgne", probs.astype(jnp.float32), valued).astype(jnp.bfloat16)
    result = result.reshape(rows, width)
    mixed = (
        y_first.astype(jnp.float32) + jnp.dot(result, w_go, preferred_element_type=jnp.float32)
    ).astype(jnp.bfloat16)
    return mixed.reshape(patches, groups, width)


def general_layer(tokens, cotangent, w_sqkv, w_so, w_gqkv, w_go, keep):
    grid_size = lax.axis_size("grid")
    position = lax.axis_index("grid")
    full_sqkv, full_so, full_gqkv, full_go = (
        lax.all_gather(w_sqkv, "grid", axis=0, tiled=True),
        lax.all_gather(w_so, "grid", axis=0, tiled=True),
        lax.all_gather(w_gqkv, "grid", axis=0, tiled=True),
        lax.all_gather(w_go, "grid", axis=0, tiled=True),
    )
    stacked, pull_first = jax.vjp(partial(project_spatial, weight=full_sqkv), tokens)
    banded = lax.all_to_all(stacked, "grid", split_axis=2, concat_axis=1, tiled=True)
    pairs = G * H // grid_size
    pair_ids = position * pairs + jnp.arange(pairs, dtype=jnp.int32)
    select = (pair_ids[:, None] // H == jnp.arange(G, dtype=jnp.int32)[None, :]).astype(jnp.float32)
    keep_rows = jnp.dot(select, keep.astype(jnp.float32), precision=lax.Precision.HIGHEST)
    attend = jax.checkpoint(pair_attention)
    attended_bands, pull_spatial = jax.vjp(
        partial(spatial_attention, keep_rows=keep_rows, attend=attend), banded
    )
    attended = lax.all_to_all(attended_bands, "grid", split_axis=0, concat_axis=1, tiled=True)
    mixed, pull_group = jax.vjp(
        partial(block_group, w_so=full_so, w_gqkv=full_gqkv, w_go=full_go), tokens, attended
    )
    grad_direct, grad_attended = pull_group(cotangent)
    grad_bands = lax.all_to_all(grad_attended, "grid", split_axis=1, concat_axis=0, tiled=True)
    (grad_banded,) = pull_spatial(grad_bands)
    grad_stacked = lax.all_to_all(grad_banded, "grid", split_axis=1, concat_axis=2, tiled=True)
    (grad_first,) = pull_first(grad_stacked)
    return (mixed, grad_direct + grad_first)


def nt(a, b):
    return lax.dot_general(a, b, (((1,), (1,)), ((), ())), preferred_element_type=jnp.float32)


def tn(a, b):
    return lax.dot_general(a, b, (((0,), (0,)), ((), ())), preferred_element_type=jnp.float32)


def nn(a, b):
    return jnp.dot(a, b, preferred_element_type=jnp.float32)


def inverse_rms(wide):
    return lax.rsqrt(jnp.mean(wide * wide, axis=-1, keepdims=True) + 1e-06)


def norm_grad(wide, inverse, grad):
    inner = jnp.mean(grad * wide, axis=-1, keepdims=True)
    return grad * inverse - wide * (inverse * inverse * inverse * inner)


def head_pair(values, low):
    zero = jnp.zeros_like(values)
    return jnp.concatenate([jnp.where(low, values, zero), jnp.where(low, zero, values)], axis=0)


def join_pair(stacked, low):
    rows = stacked.shape[0] // 2
    return jnp.where(low, stacked[:rows], stacked[rows:])


def low_lanes(rows):
    return lax.broadcasted_iota(jnp.int32, (rows, 128), 1) < 64


def columns(which, pair, width):
    return slice(which * width + pair * 128, which * width + pair * 128 + 128)


def attention_forward(qkv, allowed, probs):
    rows, width = qkv.shape[0], qkv.shape[1] // 3
    span, pairs, low = 2 * rows, width // 128, low_lanes(rows)
    for pair in range(pairs):
        keyed = head_pair(qkv[:, columns(1, pair, width)], low)
        probs[:, pair * span : pair * span + span] = nt(qkv[:, columns(0, pair, width)], keyed)
    for head in range(2 * pairs):
        at = slice(head * rows, head * rows + rows)
        weights = jnp.where(allowed, jnp.exp(probs[:, at] * 0.125), 0.0)
        probs[:, at] = weights / jnp.sum(weights, axis=-1, keepdims=True)
    results = []
    for pair in range(pairs):
        valued = head_pair(qkv[:, columns(2, pair, width)], low)
        results.append(nn(probs[:, pair * span : pair * span + span].astype(jnp.bfloat16), valued).astype(jnp.bfloat16))
    return jnp.concatenate(results, axis=1)


def attention_backward(qkv, probs, grad, grad_probs, grad_scores, grads):
    rows, width = qkv.shape[0], qkv.shape[1] // 3
    span, pairs, low = 2 * rows, width // 128, low_lanes(rows)
    for pair in range(pairs):
        valued = head_pair(qkv[:, columns(2, pair, width)], low)
        part = nt(grad[:, columns(0, pair, width)], valued)
        grad_probs[:, pair * span : pair * span + span] = part.astype(jnp.bfloat16)
    for head in range(2 * pairs):
        at = slice(head * rows, head * rows + rows)
        share, part = probs[:, at], grad_probs[:, at].astype(jnp.float32)
        inner = jnp.sum(part * share, axis=-1, keepdims=True)
        grad_scores[:, at] = (share * (part - inner) * 0.125).astype(jnp.bfloat16)
    for pair in range(pairs):
        at = slice(pair * span, pair * span + span)
        keyed = head_pair(qkv[:, columns(1, pair, width)], low)
        query, part = qkv[:, columns(0, pair, width)], grad[:, columns(0, pair, width)]
        scored = grad_scores[:, at]
        grads[:, columns(0, pair, width)] = nn(scored, keyed).astype(jnp.bfloat16)
        grads[:, columns(1, pair, width)] = join_pair(tn(scored, query), low).astype(jnp.bfloat16)
        shares = probs[:, at].astype(jnp.bfloat16)
        grads[:, columns(2, pair, width)] = join_pair(tn(shares, part), low).astype(jnp.bfloat16)


def place_rows(refs, plan, first, buffer):
    position = lax.axis_index("grid")
    size = lax.axis_size("grid")
    each = buffer.shape[0] // size
    core = lax.rem(position, 2)
    for ref, (from_sibling, blocks) in zip(refs, plan):
        side = 1 - core if from_sibling else core
        holder = position + 1 - 2 * core if from_sibling else position
        flips = (0, 2 * (side + 1), 4 - 2 * side, 6)
        for at, (step, flip) in enumerate(blocks):
            shard = lax.rem((holder ^ flips[flip]) + (size - 8 * step), size)
            rows = pl.ds(pl.multiple_of(shard * each, each), each)
            buffer[rows, :] = ref[at * each : at * each + each, first : first + buffer.shape[1]]


def packed_row(row, half, patches, groups, by_band):
    band, patch = (row // patches, row % patches) if by_band else (row % groups, row // groups)
    return (band * 2 + half) * patches + patch


def unpack(packed, patches, groups, by_band):
    rows = packed.shape[0] // 2
    row = lax.broadcasted_iota(jnp.int32, (rows, 2 * rows), 0)
    there = lax.broadcasted_iota(jnp.int32, (rows, 2 * rows), 1)
    parts = []
    for half in range(2):
        chosen = (there == packed_row(row, half, patches, groups, by_band)).astype(jnp.bfloat16)
        parts.append(nn(chosen, packed))
    return jnp.concatenate(parts, axis=1).astype(jnp.bfloat16)


def pack(values, patches, groups, by_band):
    rows, width = values.shape
    row = lax.broadcasted_iota(jnp.int32, (2 * rows, rows), 1)
    there = lax.broadcasted_iota(jnp.int32, (2 * rows, rows), 0)
    total = 0.0
    for half in range(2):
        chosen = (there == packed_row(row, half, patches, groups, by_band)).astype(jnp.bfloat16)
        total += nn(chosen, values[:, half * (width // 2) : (half + 1) * (width // 2)])
    return total.astype(jnp.bfloat16)


def prepare(patches, groups, tokens, w_so, w_gqkv, w_go, packed, joined):
    packed[...] = pack(tokens[...], patches, groups, False)
    width = w_so.shape[1]
    joined[:, :width] = w_so[...]
    joined[:, width : 4 * width] = w_gqkv[...]
    joined[:, 4 * width :] = w_go[...]


def add_packed(patches, groups, values, packed, total):
    total[...] = values[...] + unpack(packed[...], patches, groups, False)


def spatial_forward(plan, patches, groups, packed, keep, *refs):
    pieces, (result_out, qkv_out, probs_out, banded_out, turned_out, weight) = refs[:-6], refs[-6:]
    place_rows(pieces, plan, 0, weight)
    banded = unpack(packed[...], patches, groups, True)
    banded_out[...] = banded
    wide = banded.astype(jnp.float32)
    normed = (wide * inverse_rms(wide)).astype(jnp.bfloat16)
    allowed = keep[pl.ds(lax.axis_index("grid"), 1), :] > 0
    qkv_out[...] = nn(normed, weight[...]).astype(jnp.bfloat16)
    result_out[...] = pack(attention_forward(qkv_out, allowed, probs_out), patches, groups, True)
    turned_out[...] = weight[...].T


def spatial_backward(
    patches, groups, grad_packed, banded, qkv, probs, turned, grad_out, grads, grad_probs, grad_scores
):
    grad = unpack(grad_packed[...], patches, groups, True)
    attention_backward(qkv, probs, grad, grad_probs, grad_scores, grads)
    wide = banded[...].astype(jnp.float32)
    inverse = inverse_rms(wide)
    grad_normed = nn(grads[...], turned[...]).astype(jnp.bfloat16).astype(jnp.float32)
    grad_out[...] = pack(norm_grad(wide, inverse, grad_normed).astype(jnp.bfloat16), patches, groups, True)


def group_layer(patches, plan, tokens, attended, cotangent, *refs):
    pieces, rest = refs[:-12], refs[-12:]
    mixed, grad_y, grad_bands, so_buf, qkv_buf, go_buf, qkv, probs, y_buf, grads, grad_probs, grad_scores = rest
    rows, width = tokens.shape
    groups = rows // patches
    place_rows(pieces, plan, 0, so_buf)
    ordered = unpack(attended[...], patches, groups, False)
    y_first = (tokens[...].astype(jnp.float32) + nn(ordered, so_buf[...])).astype(jnp.bfloat16)
    wide = y_first.astype(jnp.float32)
    y_buf[...] = wide
    inverse = inverse_rms(wide)
    normed = (wide * inverse).astype(jnp.bfloat16)
    place_rows(pieces, plan, width, qkv_buf)
    qkv[...] = nn(normed, qkv_buf[...]).astype(jnp.bfloat16)
    place_rows(pieces, plan, 4 * width, go_buf)
    grad_attended = nt(cotangent[...], go_buf[...]).astype(jnp.bfloat16)
    row_patch = lax.broadcasted_iota(jnp.int32, (rows, rows), 0) // groups
    allowed = row_patch == lax.broadcasted_iota(jnp.int32, (rows, rows), 1) // groups
    results = attention_forward(qkv, allowed, probs)
    mixed[...] = (y_buf[...] + nn(results, go_buf[...])).astype(jnp.bfloat16)
    attention_backward(qkv, probs, grad_attended, grad_probs, grad_scores, grads)
    grad_normed = nt(grads[...], qkv_buf[...]).astype(jnp.bfloat16).astype(jnp.float32)
    through = norm_grad(y_buf[...], inverse, grad_normed).astype(jnp.bfloat16)
    total = cotangent[...] + through
    grad_y[...] = total
    spread = nt(total, so_buf[...]).astype(jnp.bfloat16)
    grad_bands[...] = pack(spread, patches, groups, False)


VMEM_SPEC = pl.BlockSpec(memory_space=pltpu.VMEM)


def room(mebibytes):
    return pltpu.CompilerParams(vmem_limit_bytes=mebibytes * 1024 * 1024)


def shape(rows, columns, dtype=jnp.bfloat16):
    return jax.ShapeDtypeStruct((rows, columns), dtype)


def cost(rows, width, weights, passes):
    return pl.CostEstimate(
        flops=2 * passes * weights * rows * width * width,
        bytes_accessed=2 * passes * weights * width * width + 16 * rows * width,
        transcendentals=16 * rows * rows,
    )


def exchange(packed):
    size = lax.axis_size("grid")
    rows, columns = packed.shape
    blocks = packed.reshape(size, rows // size, columns)
    return lax.all_to_all(blocks, "grid", split_axis=0, concat_axis=0, tiled=True).reshape(rows, columns)


def mesh_moves(size):
    everyone = range(size)
    first = [(i, i ^ (2 if i % 2 == 0 else 4)) for i in everyone]
    second = [(i, i ^ (4 if i % 2 == 0 else 2)) for i in everyone]
    sibling = [(i, i ^ 1) for i in everyone]
    along = [[(i, (i + 8 * step) % size) for i in everyone] for step in range(1, size // 8)]
    return first, second, sibling, along


def move(values, table):
    return lax.ppermute(values, "grid", table)


def together(*values):
    return lax.optimization_barrier(values)


def stack(*values):
    return jnp.concatenate(values, axis=0)


def plans(size):
    steps = range(size // 8)
    line = [[(step, flip) for step in steps] for flip in range(4)]
    own, rest = [(0, flip) for flip in range(4)], [blocks[1:] for blocks in line]

    def both_cores(held):
        return [(False, blocks) for blocks in held] + [(True, blocks) for blocks in held]

    return both_cores(line), both_cores([own] + rest)


def banded_layer(tokens, cotangent, w_sqkv, w_so, w_gqkv, w_go, keep):
    patches, groups, width = tokens.shape
    rows = patches * groups
    all_patches = patches * lax.axis_size("grid")
    first, second, sibling, along = mesh_moves(lax.axis_size("grid"))
    spatial_plan, group_plan = plans(lax.axis_size("grid"))
    pairs = width // 128
    packed_shape = shape(2 * rows, width // 2)

    tokens = tokens.reshape(rows, width)
    packed, group = pl.pallas_call(
        partial(prepare, patches, groups),
        out_shape=(packed_shape, shape(w_so.shape[0], 5 * width)),
        in_specs=[VMEM_SPEC] * 4,
        out_specs=(VMEM_SPEC,) * 2,
        name="prepare",
    )(tokens, w_so, w_gqkv, w_go)
    spatial_line = [w_sqkv] + [move(w_sqkv, table) for table in along]
    group_one, group_other = move(group, first), move(group, second)
    spatial_line, group_one, group_other, packed, group = together(
        stack(*spatial_line), group_one, group_other, packed, group
    )
    group_parts = [move(group, table) for table in along[:-1]]
    spatial_one, spatial_other = move(spatial_line, first), move(spatial_line, second)
    group_both = move(group_one, second)
    spatial_one, spatial_other, group_plane, group, group_other, spatial_line, packed, *group_parts = together(
        spatial_one,
        spatial_other,
        stack(group, group_one, group_other, group_both),
        group,
        group_other,
        spatial_line,
        packed,
        *group_parts,
    )
    spatial_both = move(spatial_one, second)
    spatial_across = [move(part, sibling) for part in (spatial_line, spatial_one, spatial_other)]
    group_line = stack(*group_parts, move(group, along[-1]))
    spatial_both, group_line, group_plane, group_other, middle, banded, *spatial_across = together(
        spatial_both, group_line, group_plane, group_other, group_parts[1], exchange(packed), *spatial_across
    )
    other_parts = [move(group_other, along[0]), move(middle, second), move(group_other, along[-1])]
    group_one = move(group_line, first)
    spatial_rows = [spatial_line, spatial_one, spatial_other, spatial_both]
    spatial_rows += [*spatial_across, move(spatial_both, sibling)]
    probs_shape = shape(all_patches, 2 * pairs * all_patches, jnp.float32)
    attended, qkv, probs, banded, turned = pl.pallas_call(
        partial(spatial_forward, spatial_plan, patches, groups),
        out_shape=(
            packed_shape,
            shape(all_patches, 3 * width),
            probs_shape,
            shape(all_patches, width),
            shape(3 * width, width),
        ),
        in_specs=[VMEM_SPEC] * (2 + len(spatial_rows)),
        out_specs=(VMEM_SPEC,) * 5,
        scratch_shapes=[pltpu.VMEM((width, 3 * width), jnp.bfloat16)],
        compiler_params=room(28),
        cost_estimate=cost(all_patches, width, 3, 1),
        name="spatial_forward",
    )(banded, keep, *spatial_rows)
    group_one, attended, group_plane, group_line, group_other = together(
        group_one, attended, group_plane, group_line, stack(*other_parts)
    )
    group_both = move(group_one, second)
    group_across = [move(part, sibling) for part in (group_plane, group_line, group_one, group_other)]
    group_both, attended, *group_across = together(group_both, exchange(attended), *group_across)
    group_rows = [group_plane, group_line, group_one, group_other, group_both]
    group_rows += [*group_across, move(group_both, sibling)]
    heads_wide = 2 * pairs * rows
    mixed, grad_y, grad_bands = pl.pallas_call(
        partial(group_layer, patches, group_plan),
        out_shape=(shape(rows, width), shape(rows, width), packed_shape),
        in_specs=[VMEM_SPEC] * (3 + len(group_rows)),
        out_specs=(VMEM_SPEC,) * 3,
        scratch_shapes=[
            pltpu.VMEM((width, width), jnp.bfloat16),
            pltpu.VMEM((width, 3 * width), jnp.bfloat16),
            pltpu.VMEM((width, width), jnp.bfloat16),
            pltpu.VMEM((rows, 3 * width), jnp.bfloat16),
            pltpu.VMEM((rows, heads_wide), jnp.float32),
            pltpu.VMEM((rows, width), jnp.float32),
            pltpu.VMEM((rows, 3 * width), jnp.bfloat16),
            pltpu.VMEM((rows, heads_wide), jnp.bfloat16),
            pltpu.VMEM((rows, heads_wide), jnp.bfloat16),
        ],
        compiler_params=room(32),
        cost_estimate=cost(rows, width, 5, 2),
        name="group_layer",
    )(tokens, attended, cotangent.reshape(rows, width), *group_rows)
    heads_wide = 2 * pairs * all_patches
    grad_first = pl.pallas_call(
        partial(spatial_backward, patches, groups),
        out_shape=packed_shape,
        in_specs=[VMEM_SPEC] * 5,
        out_specs=VMEM_SPEC,
        scratch_shapes=[
            pltpu.VMEM((all_patches, 3 * width), jnp.bfloat16),
            pltpu.VMEM((all_patches, heads_wide), jnp.bfloat16),
            pltpu.VMEM((all_patches, heads_wide), jnp.bfloat16),
        ],
        compiler_params=room(18),
        cost_estimate=cost(all_patches, width, 3, 1),
        name="spatial_backward",
    )(exchange(grad_bands), banded, qkv, probs, turned)
    token_grad = pl.pallas_call(
        partial(add_packed, patches, groups),
        out_shape=shape(rows, width),
        in_specs=[VMEM_SPEC] * 2,
        out_specs=VMEM_SPEC,
        compiler_params=room(8),
        name="add_packed",
    )(grad_y, exchange(grad_first))
    whole = (patches, groups, width)
    return (mixed.reshape(whole), token_grad.reshape(whole))


def local(tokens, cotangent, w_sqkv, w_so, w_gqkv, w_go, keep):
    patches, groups, width = tokens.shape
    size = lax.axis_size("grid")
    fits = size == groups and size % 8 == 0 and width % (16 * size) == 0 and width == 64 * H and patches * groups % 128 == 0 and 2 * patches % 8 == 0
    layer = banded_layer if fits else general_layer
    return layer(tokens, cotangent, w_sqkv, w_so, w_gqkv, w_go, keep)


def solution(mesh):
    placed = (
        P(("parts", "grid"), None, None),
        P(("parts", "grid"), None, None),
        P("grid", None),
        P("grid", None),
        P("grid", None),
        P("grid", None),
        P(None, "parts"),
    )
    return jax.shard_map(
        local,
        mesh=mesh,
        in_specs=placed,
        out_specs=(P(("parts", "grid"), None, None), P(("parts", "grid"), None, None)),
        check_vma=False,
    )
```
